32 devices in a mesh: ctx: 16 (over z, x, core), wa: 2 (over y).
Axes of the slice: x: 2, y: 2, z: 4, core: 2. Of those that a mesh axis runs over, the one named last changes fastest.
Arguments:
- tokens: bfloat16 [2, 2048, 1536], P('wa', 'ctx'), may hold values from -6 to 6
- doc_starts: int32 [2, 16], P('wa'), may hold values from 0 to 2047, as said below
- routes: int32 [2, 2048, 6], P('wa', 'ctx'), may hold values from 0 to 15, all different within a row; in each aligned block of 128 rows (0 to 127, 128 to 255, ..., all dimensions but the last counted through in order) at most 96 rows name the same one
- valid: int32 [2, 2048], P('wa', 'ctx'), may hold values from 0 to 1, as said below
- teacher: bfloat16 [2, 2048, 1536], P('wa', 'ctx'), may hold values from -6 to 6
- out_grad: bfloat16 [2, 2048, 1536], P('wa', 'ctx'), may hold values from -6 to 6
- norm1_gain: bfloat16 [1536], P('wa'), may hold values from 0.5 to 1.5
- w_query: bfloat16 [1536, 1536], P('wa'), may hold values from -0.21875 to 0.21875
- w_key: bfloat16 [1536, 512], P('wa'), may hold values from -0.21875 to 0.21875
- w_value: bfloat16 [1536, 512], P('wa'), may hold values from -0.15625 to 0.15625
- w_out: bfloat16 [1536, 1536], P('wa'), may hold values from -3.5 to 3.5
- norm2_gain: bfloat16 [1536], P('wa'), may hold values from 0.5 to 1.5
- w_router: bfloat16 [1536, 16], P('wa'), may hold values from -0.078125 to 0.078125
- shared_gate: bfloat16 [1536, 1024], P('wa'), may hold values from -0.15625 to 0.15625
- shared_up: bfloat16 [1536, 1024], P('wa'), may hold values from -0.15625 to 0.15625
- shared_down: bfloat16 [1024, 1536], P('wa'), may hold values from -0.1875 to 0.1875
- expert_gate: bfloat16 [16, 1536, 512], P('ctx', 'wa'), may hold values from -0.15625 to 0.15625
- expert_up: bfloat16 [16, 1536, 512], P('ctx', 'wa'), may hold values from -0.15625 to 0.15625
- expert_down: bfloat16 [16, 512, 1536], P('ctx', 'wa'), may hold values from -1 to 1
Outputs:
- loss: float32 [], replicated
- output: bfloat16 [2, 2048, 1536], P('wa', 'ctx')
- input_grad: float32 [2, 2048, 1536], P('wa', 'ctx')
- norm1_gain_grad: float32 [1536], P('wa')
- w_query_grad: float32 [1536, 1536], P('wa')
- w_key_grad: float32 [1536, 512], P('wa')
- w_value_grad: float32 [1536, 512], P('wa')
- w_out_grad: float32 [1536, 1536], P('wa')
- norm2_gain_grad: float32 [1536], P('wa')
- w_router_grad: float32 [1536, 16], P('wa')
- shared_gate_grad: float32 [1536, 1024], P('wa')
- shared_up_grad: float32 [1536, 1024], P('wa')
- shared_down_grad: float32 [1024, 1536], P('wa')
- expert_gate_grad: float32 [16, 1536, 512], P('ctx', 'wa')
- expert_up_grad: float32 [16, 1536, 512], P('ctx', 'wa')
- expert_down_grad: float32 [16, 512, 1536], P('ctx', 'wa')
The draws below stay inside these ranges and needn't reach their ends.
Inputs may be any that keep to these rules, and one draw needn't show every extreme that they name: `doc_starts`: each row lists the first positions of 16 documents that together cover the 2048 positions of a packed sequence, increasing from 0. The longest document has exactly 1088 positions and is the first or the last of its row. `routes`: each row names 6 different experts. Among the 128 rows that one device holds, no expert is named more than 96 times, and in every draw some expert is named exactly 96 times by one device's rows. `valid`: rows whose index in the stored order is a multiple of 128 are 1.
All inputs are finite; a program needn't handle non-finite values.
Results may differ from the reference program's by a relative error of at most 0.023.
Values may be sent and summed in bfloat16 or wider, within the bound.
A program may use at most 384 MiB of HBM per device.

```python
import math
import jax
import jax.numpy as jnp
import numpy as np
from jax import lax

D = 1536
H = 12
KVH = 4
HD = 128
TOPK = 6
FE = 512
FS = 1024
BLK = 64
NDOC = 16
EXPERTS = 16
TOK_DEV = 128
SEQ = 2048
PACKS = 2
MAXDOC = 1088
CAP = 96
N_CTX = 16


def draw_doc_starts(key, part):

    def one_sample(sample_key):
        side_key, cut_key = jax.random.split(sample_key)
        remainder = SEQ - MAXDOC
        cut_points = jnp.sort(jax.random.permutation(cut_key, remainder - 1)[:NDOC - 2] + 1).astype(jnp.int32)
        zero_head = jnp.zeros((1,), jnp.int32)
        long_first = jnp.concatenate([zero_head, MAXDOC + jnp.concatenate([zero_head, cut_points])])
        long_last = jnp.concatenate([zero_head, cut_points, jnp.full((1,), remainder, jnp.int32)])
        at_front = jax.random.randint(side_key, (), 0, 2)
        return jnp.where(at_front == 1, long_first, long_last).astype(jnp.int32)
    return jax.vmap(one_sample)(jax.random.split(key, PACKS))


def draw_valid(key, part):
    stored_rows = jnp.arange(SEQ, dtype=jnp.int32)
    threshold = SEQ // 4 + stored_rows // 2
    rolls = jax.random.randint(key, (PACKS, SEQ), 0, SEQ)
    marks = (rolls < threshold[None, :]) | (stored_rows[None, :] % TOK_DEV == 0)
    return marks.astype(jnp.int32)


def level_of(rng, dims, shards, low, top_value):
    level = 1.0
    for position, parts in shards:
        heights = jax.random.uniform(jax.random.fold_in(jax.random.fold_in(rng, 6), position), (parts,), jnp.float32, low / len(shards), top_value / len(shards))
        level = level * jnp.repeat(jnp.exp(heights), dims[position] // parts).reshape((-1,) + (1,) * (len(dims) - 1 - position))
    return level


def assign_block(own_key, own, number, rows, amount, top, reach, slope):
    sequence = jax.random.permutation(own_key, amount)
    heavy_load, common = portions_of(amount, rows * top, reach, slope, True), portions_of(amount, rows * top, reach, slope, False)
    places = jnp.arange(amount)

    def named(lengths, turn):
        used = int((lengths > 0).sum())
        fixed = max(1, used // 4)
        moved = fixed + (places - fixed + turn * (used - fixed)) % max(1, amount - fixed)
        return jnp.zeros((amount,), jnp.int32).at[sequence[jnp.where(places < fixed, places, moved)]].set(jnp.asarray(lengths, jnp.int32))

    lengths = jnp.where(number % 4 == 0, named(heavy_load, number // 4), named(common, number - number // 4 - 1))
    mixed = jax.random.permutation(jax.random.fold_in(own, 3), amount)
    source_of, receiver = mixed[0:amount // 2 * 2:2], mixed[1:amount // 2 * 2:2]
    slack = jnp.minimum(lengths[source_of] - 1, reach - lengths[receiver]) // 2
    slack = jnp.where((source_of == sequence[0]) | (receiver == sequence[0]) | (lengths[receiver] == 0), 0, jnp.maximum(slack, 0))
    moved = jax.random.randint(jax.random.fold_in(own, 4), (amount // 2,), 0, 1 << 20) % (slack + 1)
    lengths = lengths.at[source_of].add(-moved).at[receiver].add(moved)
    items = jnp.searchsorted(jnp.cumsum(lengths), jnp.arange(rows * top), side="right").astype(jnp.int32)
    grid = items.reshape(top, rows).T
    grid = grid[jax.random.permutation(jax.random.fold_in(own, 1), rows)]
    turn = jax.random.randint(jax.random.fold_in(own, 2), (rows, 1), 0, top)
    return jnp.take_along_axis(grid, (jnp.arange(top)[None, :] + turn) % top, axis=1)


def portions_of(count, total, most, lean, full):
    loads = [(1 << 20) // math.isqrt(standing ** lean) + 1 for standing in range(1, count + 1)]
    largest = most if full else min(most, max(-(-total // count), total * loads[0] // sum(loads)))
    least = 1 if total - largest >= count - 1 else 0
    holding, spare = [largest] + [least] * (count - 1), total - largest - least * (count - 1)
    while spare > 0:
        movable = [i for i in range(1, count) if holding[i] < largest] or [i for i in range(1, count) if holding[i] < most]
        pool, remaining = sum([loads[i] for i in movable]), spare
        for i in movable:
            addition = min(most - holding[i], max(1, remaining * loads[i] // pool), spare)
            holding[i] = holding[i] + addition
            spare = spare - addition
    return np.array(holding)


def noise(stream_key, extent, scale, limit, cuts=(), kind=jnp.bfloat16):
    drawn = scale * jax.random.normal(stream_key, extent, jnp.float32)
    if cuts:
        drawn = drawn * level_of(stream_key, extent, cuts, -0.22, 0.18)
    return jnp.clip(drawn, -limit, limit).astype(kind)


def setup_inputs(seed: int = 0) -> dict:
    seeds = jax.random.split(jax.random.key(seed), 20)
    tokens = noise(seeds[0], (PACKS, SEQ, D), 1.0, 6.0, ((0, 2), (1, 16)))
    doc_starts = draw_doc_starts(jax.random.fold_in(seeds[19], 71), 0)
    routes_keys = jax.random.split(jax.random.fold_in(seeds[2], 1), PACKS * SEQ // TOK_DEV)
    routes_turns = jax.random.permutation(jax.random.fold_in(seeds[2], 3), PACKS * SEQ // TOK_DEV)
    routes = jax.vmap(lambda own, number: assign_block(jax.random.fold_in(seeds[2], 2), own, number, TOK_DEV, EXPERTS, TOPK, CAP, 1))(routes_keys, routes_turns).reshape((PACKS, SEQ, TOPK))
    valid = draw_valid(jax.random.fold_in(seeds[19], 71), 0)
    teacher = noise(seeds[4], (PACKS, SEQ, D), 1.0, 6.0, ((0, 2), (1, 16)))
    out_grad = noise(seeds[5], (PACKS, SEQ, D), 1.0, 6.0, ((0, 2), (1, 16)))
    norm1_gain = jnp.clip(1.0 + 0.1 * jax.random.normal(seeds[6], (D,), jnp.float32), 0.5, 1.5).astype(jnp.bfloat16)
    w_query = noise(seeds[7], (D, H * HD), (D // 2) ** -0.5, 0.21875, ((0, 2),))
    w_key = noise(seeds[8], (D, KVH * HD), (D // 2) ** -0.5, 0.21875, ((0, 2),))
    w_value = noise(seeds[9], (D, KVH * HD), D ** -0.5, 0.15625, ((0, 2),))
    w_out = noise(seeds[10], (H * HD, D), (max(1, H * HD // 512)) ** -0.5, 3.5, ((0, 2),))
    norm2_gain = jnp.clip(1.0 + 0.1 * jax.random.normal(seeds[11], (D,), jnp.float32), 0.5, 1.5).astype(jnp.bfloat16)
    w_router = noise(seeds[12], (D, EXPERTS), (4 * D) ** -0.5, 0.078125, ((0, 2),))
    shared_gate = noise(seeds[13], (D, FS), D ** -0.5, 0.15625, ((0, 2),))
    shared_up = noise(seeds[14], (D, FS), D ** -0.5, 0.15625, ((0, 2),))
    shared_down = noise(seeds[15], (FS, D), FS ** -0.5, 0.1875, ((0, 2),))
    expert_gate = noise(seeds[16], (EXPERTS, D, FE), D ** -0.5, 0.15625, ((0, 16), (1, 2)))
    expert_up = noise(seeds[17], (EXPERTS, D, FE), D ** -0.5, 0.15625, ((0, 16), (1, 2)))
    expert_down = noise(seeds[18], (EXPERTS, FE, D), (FE // 16) ** -0.5, 1.0, ((0, 16), (1, 2)))
    return dict(tokens=tokens, doc_starts=doc_starts, routes=routes, valid=valid, teacher=teacher, out_grad=out_grad, norm1_gain=norm1_gain, w_query=w_query, w_key=w_key, w_value=w_value, w_out=w_out, norm2_gain=norm2_gain, w_router=w_router, shared_gate=shared_gate, shared_up=shared_up, shared_down=shared_down, expert_gate=expert_gate, expert_up=expert_up, expert_down=expert_down)


EPSILON = 1e-05
HIGHEST = lax.Precision.HIGHEST
MASKED_SCORE = -1e+30

@jax.custom_vjp
def low(v):
    return lax.optimization_barrier(v.astype(jnp.bfloat16)).astype(jnp.float32)

@jax.custom_vjp
def low_back(v):
    return v

def low_keep(v):
    return (low(v), None)

def low_pass(kept, grad):
    return (grad,)

def back_keep(v):
    return (v, None)

def back_low(kept, grad):
    return (low(grad),)
low.defvjp(low_keep, low_pass)
low_back.defvjp(back_keep, back_low)

def stored_positions(stored_rows):
    owner_rank = stored_rows // TOK_DEV
    within_rows = stored_rows % TOK_DEV
    first_half = owner_rank * BLK + within_rows
    second_half = (2 * N_CTX - 1 - owner_rank) * BLK + within_rows - BLK
    return jnp.where(within_rows < BLK, first_half, second_half).astype(jnp.int32)

def project(values, weight):
    return jnp.einsum('...d,df->...f', values, weight, precision=HIGHEST)

def rms_norm(values, gain):
    inverse = lax.rsqrt(lax.optimization_barrier(jnp.mean(values * values, axis=-1, keepdims=True)) + EPSILON)
    return values * inverse * gain

def attend(queries, key_rows, value_rows, documents):
    query_block = min(SEQ, 512)
    key_width = min(SEQ, MAXDOC + query_block)
    groups = H // KVH
    score_scale = HD ** (-0.5)
    positions = jnp.arange(SEQ, dtype=jnp.int32)

    def one_block(block_index):
        query_first = (block_index * query_block).astype(jnp.int32)
        key_first = jnp.maximum(query_first + query_block - key_width, 0).astype(jnp.int32)
        query_part = lax.dynamic_slice_in_dim(queries, query_first, query_block, 0).reshape(query_block, KVH, groups, HD)
        key_part = lax.dynamic_slice_in_dim(key_rows, key_first, key_width, 0).reshape(key_width, KVH, HD)
        value_part = lax.dynamic_slice_in_dim(value_rows, key_first, key_width, 0).reshape(key_width, KVH, HD)
        query_pos = lax.dynamic_slice_in_dim(positions, query_first, query_block, 0)
        key_pos = lax.dynamic_slice_in_dim(positions, key_first, key_width, 0)
        query_doc = lax.dynamic_slice_in_dim(documents, query_first, query_block, 0)
        key_doc = lax.dynamic_slice_in_dim(documents, key_first, key_width, 0)
        visible = (key_pos[None, :] <= query_pos[:, None]) & (key_doc[None, :] == query_doc[:, None])
        scores = low_back(jnp.einsum('tagd,sad->agts', query_part, key_part, precision=HIGHEST) * score_scale)
        masked = jnp.where(visible, scores, MASKED_SCORE)
        row_peak = lax.optimization_barrier(jnp.max(masked, axis=-1, keepdims=True))
        totals = lax.optimization_barrier(jnp.sum(jnp.where(visible, jnp.exp(masked - row_peak), 0.0), axis=-1, keepdims=True))
        log_total = row_peak + jnp.log(totals)
        weights_low = low(jnp.where(visible, jnp.exp(masked - log_total), 0.0))
        mixed_rows = jnp.einsum('agts,sad->tagd', weights_low, value_part, precision=HIGHEST)
        return mixed_rows.reshape(query_block, H * HD)
    outputs = lax.map(jax.checkpoint(one_block), jnp.arange(SEQ // query_block, dtype=jnp.int32))
    return outputs.reshape(SEQ, H * HD)

def slot_table(route_rows):
    flat_routes = route_rows.reshape(TOK_DEV * TOPK)
    one_hot = (flat_routes[:, None] == jnp.arange(EXPERTS, dtype=jnp.int32)[None, :]).astype(jnp.int32)
    slot_rank = lax.optimization_barrier(jnp.sum((jnp.cumsum(one_hot, axis=0) - 1) * one_hot, axis=1))
    slot_index = (flat_routes * CAP + slot_rank).astype(jnp.int32)
    pair_table = jnp.full((EXPERTS * CAP,), TOK_DEV * TOPK, jnp.int32).at[slot_index].set(jnp.arange(TOK_DEV * TOPK, dtype=jnp.int32))
    return (slot_index, pair_table)

def routed_experts(normed_two, routes, gates, expert_gate, expert_up, expert_down):
    blocks = PACKS * N_CTX
    row_blocks = normed_two.reshape(blocks, TOK_DEV, D)
    route_blocks = routes.reshape(blocks, TOK_DEV, TOPK)
    gate_blocks = gates.reshape(blocks, TOK_DEV, TOPK)

    def one_block(operands):
        block_rows, route_rows, gate_rows = operands
        slot_index, pair_table = slot_table(route_rows)
        padded = jnp.concatenate([block_rows, jnp.zeros((1, D), block_rows.dtype)], axis=0)
        sent_rows = low_back(padded[pair_table // TOPK]).reshape(EXPERTS, CAP, D)
        gate_act = low_back(jnp.einsum('ecd,edf->ecf', sent_rows, expert_gate, precision=HIGHEST))
        up_activation = low_back(jnp.einsum('ecd,edf->ecf', sent_rows, expert_up, precision=HIGHEST))
        hidden = low(jax.nn.silu(gate_act) * up_activation)
        returned = low_back(low(jnp.einsum('ecf,efd->ecd', hidden, expert_down, precision=HIGHEST))).reshape(EXPERTS * CAP, D)
        picked = returned[slot_index].reshape(TOK_DEV, TOPK, D)
        return lax.optimization_barrier(jnp.sum(gate_rows[:, :, None] * picked, axis=1))
    outputs = lax.map(jax.checkpoint(one_block), (row_blocks, route_blocks, gate_blocks))
    return outputs.reshape(PACKS, SEQ, D)

def forward(tokens_in, norm_first, w_query, w_key, w_value, w_out, norm_second, w_router, shared_gate, shared_up, shared_down, expert_gate, expert_up, expert_down, routes, documents, order, positions):
    normed_one = low(rms_norm(tokens_in, norm_first))
    queries = low_back(low(project(normed_one, w_query)))
    key_rows = low_back(low(project(normed_one, w_key)))
    value_rows = low_back(low(project(normed_one, w_value)))
    attended = []
    for sample in range(PACKS):
        mixed_rows = attend(queries[sample][order], key_rows[sample][order], value_rows[sample][order], documents[sample])
        attended.append(mixed_rows[positions])
    attn_rows = low_back(low(jnp.stack(attended)))
    hidden_one = tokens_in + low_back(project(attn_rows, w_out))
    normed_two = low(rms_norm(hidden_one, norm_second))
    logits = low_back(project(normed_two, w_router))
    choose = (routes[..., None] == jnp.arange(EXPERTS, dtype=jnp.int32)).astype(jnp.float32)
    picked_logits = lax.optimization_barrier(jnp.sum(choose * logits[:, :, None, :], axis=-1))
    gates = jax.nn.softmax(picked_logits, axis=-1)
    shared_g = low_back(project(normed_two, shared_gate))
    shared_u = low_back(project(normed_two, shared_up))
    shared_h = low(jax.nn.silu(shared_g) * shared_u)
    shared_out = low_back(project(shared_h, shared_down))
    routed = routed_experts(normed_two, routes, gates, expert_gate, expert_up, expert_down)
    return hidden_one + shared_out + routed

def reference(tokens, doc_starts, routes, valid, teacher, out_grad, norm1_gain, w_query, w_key, w_value, w_out, norm2_gain, w_router, shared_gate, shared_up, shared_down, expert_gate, expert_up, expert_down):
    stored_rows = jnp.arange(SEQ, dtype=jnp.int32)
    positions = stored_positions(stored_rows)
    order = jnp.argsort(positions).astype(jnp.int32)
    documents = lax.optimization_barrier(jnp.sum((doc_starts[:, None, :] <= stored_rows[None, :, None]).astype(jnp.int32), axis=2)) - 1
    valid_rows = valid.astype(jnp.float32)
    valid_total = jnp.sum(valid_rows)
    target = teacher.astype(jnp.float32)
    params = [array.astype(jnp.float32) for array in (tokens, norm1_gain, w_query, w_key, w_value, w_out, norm2_gain, w_router, shared_gate, shared_up, shared_down, expert_gate, expert_up, expert_down)]

    def objective(*inputs):
        produced = forward(*inputs, routes, documents, order, positions)
        errors = produced - target
        loss_value = jnp.sum(valid_rows[:, :, None] * errors * errors) / (valid_total * D)
        return (produced, loss_value)
    (produced, loss_value), pullback = jax.vjp(objective, *params)
    weight = jnp.asarray(PACKS * SEQ * D, jnp.float32)
    gradients = pullback((out_grad.astype(jnp.float32), weight))
    return (loss_value, produced.astype(jnp.bfloat16), gradients[0], gradients[1], gradients[2], gradients[3], gradients[4], gradients[5], gradients[6], gradients[7], gradients[8], gradients[9], gradients[10], gradients[11], gradients[12], gradients[13])
```

```python
import math

import jax
import jax.numpy as jnp
from jax import lax
from jax.sharding import PartitionSpec as P

D = 1536
H = 12
KVH = 4
HD = 128


EPSILON = 1e-05
MASKED_SCORE = -1e30


def keep_state(state_in):
    return state_in


def stored_position(stored_rows, local_rows, ctx_count):
    half_rows = local_rows // 2
    owner_rank = stored_rows // local_rows
    within_rows = stored_rows % local_rows
    first_half = owner_rank * half_rows + within_rows
    second_half = (2 * ctx_count - 1 - owner_rank) * half_rows + within_rows - half_rows
    return jnp.where(within_rows < half_rows, first_half, second_half)


def document_of(positions, doc_first):
    return jnp.sum((doc_first[None, :] <= positions[:, None]).astype(jnp.int32), axis=1) - 1


def matmul(left, right):
    return jnp.dot(left, right, preferred_element_type=jnp.float32)


def contract_rows(left, right):
    return lax.dot_general(
        left, right, (((0,), (0,)), ((), ())), preferred_element_type=jnp.float32
    )


def contract_cols(left, right):
    return lax.dot_general(
        left, right, (((1,), (1,)), ((), ())), preferred_element_type=jnp.float32
    )


def norm_forward(values, gain):
    inverse = lax.rsqrt(jnp.mean(values * values, axis=1, keepdims=True) + EPSILON)
    return (inverse, values * inverse * gain)


def norm_backward(values, inverse, gain, grad_normed):
    scaled = grad_normed * gain
    inner_sum = jnp.sum(scaled * values, axis=1, keepdims=True)
    grad_values = (
        inverse * scaled - values * (inverse * inverse * inverse) * inner_sum / values.shape[1]
    )
    grad_gain = jnp.sum(grad_normed * values * inverse, axis=0)
    return (grad_values, grad_gain)


def silu_grads(grad_hidden, gate_act, up_activation):
    sigmoid_gate = jax.nn.sigmoid(gate_act)
    grad_gate = grad_hidden * up_activation * sigmoid_gate * (1.0 + gate_act * (1.0 - sigmoid_gate))
    grad_up = grad_hidden * gate_act * sigmoid_gate
    return (grad_gate.astype(jnp.bfloat16), grad_up.astype(jnp.bfloat16))


def visible_pairs(query_pos, query_doc, key_pos, key_doc):
    return (key_pos[None, :] <= query_pos[:, None]) & (key_doc[None, :] == query_doc[:, None])


def block_scores(query_heads, key_part, score_scale):
    return (
        jnp.einsum("tagd,sad->agts", query_heads, key_part, preferred_element_type=jnp.float32)
        * score_scale
    )


def block_probs(query_heads, key_part, visible, log_total, score_scale):
    scores = block_scores(query_heads, key_part, score_scale)
    return jnp.where(visible, jnp.exp(jnp.where(visible, scores, MASKED_SCORE) - log_total), 0.0)


def attend_forward(
    query_heads,
    key_all,
    value_all,
    query_pos,
    query_doc,
    key_pos_all,
    key_doc_all,
    key_width,
    score_scale,
):
    local_rows, kv_heads, groups, head_dim = query_heads.shape
    key_turns = key_all.shape[0] // key_width

    def key_step(block_index, carry_state):
        first_row = block_index * key_width
        key_pos = lax.dynamic_slice_in_dim(key_pos_all, first_row, key_width, 0)
        key_doc = lax.dynamic_slice_in_dim(key_doc_all, first_row, key_width, 0)
        visible = visible_pairs(query_pos, query_doc, key_pos, key_doc)

        def compute(state_in):
            peak_in, total_in, accum_in = state_in
            key_part = lax.dynamic_slice_in_dim(key_all, first_row, key_width, 0).reshape(
                key_width, kv_heads, head_dim
            )
            value_part = lax.dynamic_slice_in_dim(value_all, first_row, key_width, 0).reshape(
                key_width, kv_heads, head_dim
            )
            scores = block_scores(query_heads, key_part, score_scale)
            masked = jnp.where(visible, scores, MASKED_SCORE)
            new_peak = jnp.maximum(peak_in, jnp.max(masked, axis=3, keepdims=True))
            shrink = jnp.exp(peak_in - new_peak)
            weights = jnp.where(visible, jnp.exp(masked - new_peak), 0.0)
            new_total = total_in * shrink + jnp.sum(weights, axis=3, keepdims=True)
            new_accum = accum_in * shrink + jnp.einsum(
                "agts,sad->agtd",
                weights.astype(jnp.bfloat16),
                value_part,
                preferred_element_type=jnp.float32,
            )
            return (new_peak, new_total, new_accum)

        return lax.cond(jnp.any(visible), compute, keep_state, carry_state)

    initial = (
        jnp.full((kv_heads, groups, local_rows, 1), MASKED_SCORE, jnp.float32),
        jnp.zeros((kv_heads, groups, local_rows, 1), jnp.float32),
        jnp.zeros((kv_heads, groups, local_rows, head_dim), jnp.float32),
    )
    row_peak, totals, accumulated = lax.fori_loop(0, key_turns, key_step, initial)
    log_total = row_peak + jnp.log(totals)
    attn_heads = jnp.transpose(accumulated / totals, (2, 0, 1, 3))
    return (log_total, attn_heads.reshape(local_rows, kv_heads * groups * head_dim))


def attend_query_grads(
    query_heads,
    grad_heads,
    key_all,
    value_all,
    log_total,
    delta,
    query_pos,
    query_doc,
    key_pos_all,
    key_doc_all,
    key_width,
    score_scale,
):
    local_rows, kv_heads, groups, head_dim = query_heads.shape

    def key_step(block_index, accumulated):
        first_row = block_index * key_width
        key_pos = lax.dynamic_slice_in_dim(key_pos_all, first_row, key_width, 0)
        key_doc = lax.dynamic_slice_in_dim(key_doc_all, first_row, key_width, 0)
        visible = visible_pairs(query_pos, query_doc, key_pos, key_doc)

        def compute(state_in):
            key_part = lax.dynamic_slice_in_dim(key_all, first_row, key_width, 0).reshape(
                key_width, kv_heads, head_dim
            )
            value_part = lax.dynamic_slice_in_dim(value_all, first_row, key_width, 0).reshape(
                key_width, kv_heads, head_dim
            )
            probs = block_probs(query_heads, key_part, visible, log_total, score_scale)
            grad_probs = jnp.einsum(
                "tagd,sad->agts", grad_heads, value_part, preferred_element_type=jnp.float32
            )
            grad_scores = (probs * (grad_probs - delta)).astype(jnp.bfloat16)
            return state_in + jnp.einsum(
                "agts,sad->tagd", grad_scores, key_part, preferred_element_type=jnp.float32
            )

        return lax.cond(jnp.any(visible), compute, keep_state, accumulated)

    result = lax.fori_loop(
        0, key_all.shape[0] // key_width, key_step, jnp.zeros(query_heads.shape, jnp.float32)
    )
    return result * score_scale


def key_value_grads(
    query_heads,
    grad_heads,
    log_total,
    delta,
    query_pos,
    query_doc,
    key_part,
    value_part,
    key_pos,
    key_doc,
    score_scale,
):
    key_count = key_part.shape[0]
    kv_width = key_part.shape[1] * key_part.shape[2]
    visible = visible_pairs(query_pos, query_doc, key_pos, key_doc)

    def compute(unused):
        probs = block_probs(query_heads, key_part, visible, log_total, score_scale)
        grad_probs = jnp.einsum(
            "tagd,sad->agts", grad_heads, value_part, preferred_element_type=jnp.float32
        )
        grad_scores = (probs * (grad_probs - delta)).astype(jnp.bfloat16)
        grad_keys = (
            jnp.einsum(
                "agts,tagd->sad", grad_scores, query_heads, preferred_element_type=jnp.float32
            )
            * score_scale
        )
        grad_values = jnp.einsum(
            "agts,tagd->sad",
            probs.astype(jnp.bfloat16),
            grad_heads,
            preferred_element_type=jnp.float32,
        )
        return jnp.concatenate(
            [grad_keys.reshape(key_count, kv_width), grad_values.reshape(key_count, kv_width)],
            axis=1,
        )

    def nothing(unused):
        return jnp.zeros((key_count, 2 * kv_width), jnp.float32)

    return lax.cond(jnp.any(visible), compute, nothing, 0)


def pair_swap(value):
    return lax.ppermute(value, "wa", [(0, 1), (1, 0)])


def my_half(value, side, axis):
    size = value.shape[axis] // 2
    return lax.dynamic_slice_in_dim(value, side * size, size, axis)


def ctx_gather(value):
    return lax.all_gather(value, "ctx", axis=0, tiled=True)


def ctx_scatter_sum(value):
    return lax.psum_scatter(value, "ctx", scatter_dimension=0, tiled=True)


def per_device(
    tokens,
    doc_starts,
    routes,
    valid,
    teacher,
    out_grad,
    norm1_gain,
    w_query,
    w_key,
    w_value,
    w_out,
    norm2_gain,
    w_router,
    shared_gate,
    shared_up,
    shared_down,
    expert_gate,
    expert_up,
    expert_down,
):
    ctx_count = lax.axis_size("ctx")
    ctx_rank = lax.axis_index("ctx")
    wa_count = lax.axis_size("wa")
    side = lax.axis_index("wa")
    local_rows = tokens.shape[1]
    seq_len = local_rows * ctx_count
    key_width = min(seq_len, 1024)
    groups = H // KVH
    kv_width = KVH * HD
    score_scale = HD ** (-0.5)
    experts = w_router.shape[1]
    resident = expert_gate.shape[0]

    def over_wa(value, axis=0):
        return lax.all_gather(value, "wa", axis=axis, tiled=True)

    gain_one = over_wa(norm1_gain)
    gain_two = over_wa(norm2_gain)
    weight_query = over_wa(w_query)
    weight_key = over_wa(w_key)
    weight_value = over_wa(w_value)
    weight_out = over_wa(w_out)
    weight_router = over_wa(w_router)
    weight_sgate = over_wa(shared_gate)
    weight_sup = over_wa(shared_up)
    weight_sdown = over_wa(shared_down)
    weight_egate = over_wa(expert_gate, 1)
    weight_eup = over_wa(expert_up, 1)
    weight_edown = over_wa(expert_down, 1)
    gain_one_f = gain_one.astype(jnp.float32)
    gain_two_f = gain_two.astype(jnp.float32)
    valid_rows = valid[0].astype(jnp.float32)
    valid_total = lax.psum(jnp.sum(valid_rows), ("ctx", "wa"))
    doc_first = doc_starts[0]
    own_rows = ctx_rank * local_rows + jnp.arange(local_rows, dtype=jnp.int32)
    query_pos = stored_position(own_rows, local_rows, ctx_count)
    query_doc = document_of(query_pos, doc_first)
    key_pos_all = stored_position(jnp.arange(seq_len, dtype=jnp.int32), local_rows, ctx_count)
    key_doc_all = document_of(key_pos_all, doc_first)
    residual_stream = tokens[0].astype(jnp.float32)
    inverse_one, normed = norm_forward(residual_stream, gain_one_f)
    normed_one = normed.astype(jnp.bfloat16)
    queries = matmul(normed_one, weight_query).astype(jnp.bfloat16)
    key_rows = matmul(normed_one, weight_key).astype(jnp.bfloat16)
    value_rows = matmul(normed_one, weight_value).astype(jnp.bfloat16)
    key_value_all = ctx_gather(jnp.concatenate([key_rows, value_rows], axis=1))
    key_all, value_all = key_value_all[:, :kv_width], key_value_all[:, kv_width:]
    query_heads = queries.reshape(local_rows, KVH, groups, HD)
    log_total, attn_f32 = attend_forward(
        query_heads,
        key_all,
        value_all,
        query_pos,
        query_doc,
        key_pos_all,
        key_doc_all,
        key_width,
        score_scale,
    )
    attn_low = attn_f32.astype(jnp.bfloat16)
    hidden_one = residual_stream + matmul(attn_low, weight_out)
    inverse_two, normed = norm_forward(hidden_one, gain_two_f)
    normed_two = normed.astype(jnp.bfloat16)
    logits = matmul(normed_two, weight_router)
    route_rows = routes[0]
    choose = (route_rows[:, :, None] == jnp.arange(experts, dtype=jnp.int32)[None, None, :]).astype(
        jnp.float32
    )
    chosen = jnp.sum(choose, axis=1)
    peak = jnp.max(jnp.where(chosen > 0, logits, MASKED_SCORE), axis=1, keepdims=True)
    weights = jnp.where(chosen > 0, jnp.exp(jnp.where(chosen > 0, logits, peak) - peak), 0.0)
    gates = weights / jnp.sum(weights, axis=1, keepdims=True)
    normed_all = ctx_gather(normed_two)
    gates_all = lax.all_to_all(
        gates.reshape(local_rows, ctx_count, resident), "ctx", split_axis=1, concat_axis=0, tiled=True
    ).reshape(seq_len, resident)
    shared_g_act = matmul(normed_two, weight_sgate)
    shared_u_act = matmul(normed_two, weight_sup)
    shared_hidden = (jax.nn.silu(shared_g_act) * shared_u_act).astype(jnp.bfloat16)
    shared_out = matmul(shared_hidden, weight_sdown)
    gate_act, up_act, hidden_exp, expert_out = [], [], [], []
    mixed = 0.0
    for q in range(resident):
        gate_act.append(matmul(normed_all, weight_egate[q]))
        up_act.append(matmul(normed_all, weight_eup[q]))
        hidden_exp.append((jax.nn.silu(gate_act[q]) * up_act[q]).astype(jnp.bfloat16))
        expert_out.append(matmul(hidden_exp[q], weight_edown[q]).astype(jnp.bfloat16))
        mixed = mixed + gates_all[:, q : q + 1] * expert_out[q].astype(jnp.float32)
    routed = ctx_scatter_sum(mixed.astype(jnp.bfloat16)).astype(jnp.float32)
    produced = hidden_one + shared_out + routed
    output = produced.astype(jnp.bfloat16)[None]
    errors = produced - teacher[0].astype(jnp.float32)
    local_error = jnp.sum(valid_rows[:, None] * errors * errors)
    tokens_all = wa_count * seq_len
    grad_out = (
        out_grad[0].astype(jnp.float32)
        + 2.0 * tokens_all / valid_total * valid_rows[:, None] * errors
    )
    grad_low = grad_out.astype(jnp.bfloat16)
    grad_all = ctx_gather(grad_low)
    grad_shared_hidden = contract_cols(grad_low, weight_sdown)
    grad_sgate, grad_sup = silu_grads(grad_shared_hidden, shared_g_act, shared_u_act)
    grad_normed = contract_cols(grad_sgate, weight_sgate) + contract_cols(grad_sup, weight_sup)
    gate_dots, egate_grad, eup_grad, edown_grad = [], [], [], []
    grad_rows = 0.0
    for q in range(resident):
        grad_picked = (gates_all[:, q : q + 1] * grad_all.astype(jnp.float32)).astype(jnp.bfloat16)
        gate_dots.append(
            jnp.sum(
                grad_all.astype(jnp.float32) * expert_out[q].astype(jnp.float32),
                axis=1,
                keepdims=True,
            )
        )
        grad_hidden = contract_cols(grad_picked, weight_edown[q])
        grad_gact, grad_uact = silu_grads(grad_hidden, gate_act[q], up_act[q])
        grad_rows = (
            grad_rows
            + contract_cols(grad_gact, weight_egate[q])
            + contract_cols(grad_uact, weight_eup[q])
        )
        egate_grad.append(contract_rows(normed_all, grad_gact))
        eup_grad.append(contract_rows(normed_all, grad_uact))
        edown_grad.append(contract_rows(hidden_exp[q], grad_picked))
    grad_back = ctx_scatter_sum(grad_rows.astype(jnp.bfloat16)).astype(jnp.float32)
    gate_dot = lax.all_to_all(
        jnp.concatenate(gate_dots, axis=1).reshape(ctx_count, local_rows, resident),
        "ctx",
        split_axis=0,
        concat_axis=0,
        tiled=True,
    )
    grad_gates = jnp.transpose(gate_dot, (1, 0, 2)).reshape(local_rows, experts)
    grad_logits = (
        gates * (grad_gates - jnp.sum(gates * grad_gates, axis=1, keepdims=True))
    ).astype(jnp.bfloat16)
    grad_normed = grad_normed + contract_cols(grad_logits, weight_router) + grad_back

    def expert_sum(grads):
        full = jnp.stack(grads)
        other = pair_swap(my_half(full, 1 - side, 1).astype(jnp.bfloat16))
        return my_half(full, side, 1) + other.astype(jnp.float32)

    expert_gate_sum, expert_up_sum, expert_down_sum = (
        expert_sum(egate_grad),
        expert_sum(eup_grad),
        expert_sum(edown_grad),
    )
    grad_hidden_norm, grad_gain_two = norm_backward(
        hidden_one, inverse_two, gain_two_f, grad_normed
    )
    grad_hidden_one = grad_out + grad_hidden_norm
    grad_attn_in = grad_hidden_one.astype(jnp.bfloat16)
    grad_attn_low = contract_cols(grad_attn_in, weight_out).astype(jnp.bfloat16)
    grad_heads = grad_attn_low.reshape(local_rows, KVH, groups, HD)
    delta = jnp.einsum(
        "tagd,tagd->agt",
        grad_heads.astype(jnp.float32),
        attn_f32.reshape(local_rows, KVH, groups, HD),
    )[:, :, :, None]
    grad_query_low = (
        attend_query_grads(
            query_heads,
            grad_heads,
            key_all,
            value_all,
            log_total,
            delta,
            query_pos,
            query_doc,
            key_pos_all,
            key_doc_all,
            key_width,
            score_scale,
        )
        .reshape(local_rows, H * HD)
        .astype(jnp.bfloat16)
    )
    sub_rows = math.gcd(seq_len, key_width)

    def one_piece(piece_index):
        piece_first = piece_index * sub_rows
        key_part = lax.dynamic_slice_in_dim(key_all, piece_first, sub_rows, 0).reshape(
            sub_rows, KVH, HD
        )
        value_part = lax.dynamic_slice_in_dim(value_all, piece_first, sub_rows, 0).reshape(
            sub_rows, KVH, HD
        )
        key_pos = lax.dynamic_slice_in_dim(key_pos_all, piece_first, sub_rows, 0)
        key_doc = lax.dynamic_slice_in_dim(key_doc_all, piece_first, sub_rows, 0)
        return key_value_grads(
            query_heads,
            grad_heads,
            log_total,
            delta,
            query_pos,
            query_doc,
            key_part,
            value_part,
            key_pos,
            key_doc,
            score_scale,
        )

    pieces = lax.map(one_piece, jnp.arange(seq_len // sub_rows, dtype=jnp.int32))
    key_value_grad = ctx_scatter_sum(
        pieces.reshape(seq_len, 2 * kv_width).astype(jnp.bfloat16)
    )
    grad_key_low = key_value_grad[:, :kv_width]
    grad_value_low = key_value_grad[:, kv_width:]
    grad_normed_one = (
        contract_cols(grad_query_low, weight_query)
        + contract_cols(grad_key_low, weight_key)
        + contract_cols(grad_value_low, weight_value)
    )
    grad_residual_norm, grad_gain_one = norm_backward(
        residual_stream, inverse_one, gain_one_f, grad_normed_one
    )
    grad_input = grad_hidden_one + grad_residual_norm

    def weight_grad(left, *rights):
        right = rights[0] if len(rights) == 1 else jnp.concatenate(rights, axis=1)
        other_left = pair_swap(my_half(left, 1 - side, 1))
        other_right = pair_swap(right)
        return (
            contract_rows(my_half(left, side, 1), right) + contract_rows(other_left, other_right)
        ).astype(jnp.bfloat16)

    summed = lax.psum(
        (
            weight_grad(shared_hidden, grad_low),
            weight_grad(normed_two, grad_sgate, grad_sup, grad_logits),
            weight_grad(attn_low, grad_attn_in),
            weight_grad(normed_one, grad_query_low, grad_key_low, grad_value_low),
        ),
        "ctx",
    )
    total_sdown, total_second, total_out, total_first = [s.astype(jnp.float32) for s in summed]
    shared_width = grad_sgate.shape[1]
    vectors = lax.psum(
        jnp.concatenate([grad_gain_one, grad_gain_two, jnp.full((128,), local_error)]),
        ("ctx", "wa"),
    )
    width = grad_gain_one.shape[0]
    loss_value = vectors[2 * width] / (valid_total * D)
    return (
        loss_value,
        output,
        grad_input[None],
        my_half(vectors[:width], side, 0),
        total_first[:, : H * HD],
        total_first[:, H * HD : H * HD + kv_width],
        total_first[:, H * HD + kv_width :],
        total_out,
        my_half(vectors[width : 2 * width], side, 0),
        total_second[:, 2 * shared_width :],
        total_second[:, :shared_width],
        total_second[:, shared_width : 2 * shared_width],
        total_sdown,
        expert_gate_sum,
        expert_up_sum,
        expert_down_sum,
    )


def solution(mesh):
    return jax.shard_map(
        per_device,
        mesh=mesh,
        in_specs=(
            P("wa", "ctx", None),
            P("wa", None),
            P("wa", "ctx", None),
            P("wa", "ctx"),
            P("wa", "ctx", None),
            P("wa", "ctx", None),
            P("wa"),
            P("wa", None),
            P("wa", None),
            P("wa", None),
            P("wa", None),
            P("wa"),
            P("wa", None),
            P("wa", None),
            P("wa", None),
            P("wa", None),
            P("ctx", "wa", None),
            P("ctx", "wa", None),
            P("ctx", "wa", None),
        ),
        out_specs=(
            P(),
            P("wa", "ctx", None),
            P("wa", "ctx", None),
            P("wa"),
            P("wa", None),
            P("wa", None),
            P("wa", None),
            P("wa", None),
            P("wa"),
            P("wa", None),
            P("wa", None),
            P("wa", None),
            P("wa", None),
            P("ctx", "wa", None),
            P("ctx", "wa", None),
            P("ctx", "wa", None),
        ),
        check_vma=False,
    )
```

```python
import functools

import jax
import jax.numpy as jnp
from jax import lax
from jax.experimental import pallas as pl
from jax.experimental.pallas import tpu as pltpu
from jax.sharding import PartitionSpec as P

H = 12
KVH = 4
HD = 128
EPSILON = 1e-05
MASKED_SCORE = -1e30


def stored_position(stored_rows, local_rows, ctx_count):
    half_rows = local_rows // 2
    owner_rank = stored_rows // local_rows
    within_rows = stored_rows % local_rows
    first_half = owner_rank * half_rows + within_rows
    second_half = (2 * ctx_count - 1 - owner_rank) * half_rows + within_rows - half_rows
    return jnp.where(within_rows < half_rows, first_half, second_half)


def document_of(positions, doc_first):
    return jnp.sum((doc_first[None, :] <= positions[:, None]).astype(jnp.int32), axis=1) - 1


def matmul(left, right):
    return jnp.dot(left, right, preferred_element_type=jnp.float32)


def contract_rows(left, right):
    return lax.dot_general(
        left, right, (((0,), (0,)), ((), ())), preferred_element_type=jnp.float32
    )


def contract_cols(left, right):
    return lax.dot_general(
        left, right, (((1,), (1,)), ((), ())), preferred_element_type=jnp.float32
    )


def norm_forward(values, gain):
    inverse = lax.rsqrt(jnp.mean(values * values, axis=1, keepdims=True) + EPSILON)
    return (inverse, values * inverse * gain)


def norm_backward(values, inverse, gain, grad_normed):
    scaled = grad_normed * gain
    inner_sum = jnp.sum(scaled * values, axis=1, keepdims=True)
    grad_values = (
        inverse * scaled - values * (inverse * inverse * inverse) * inner_sum / values.shape[1]
    )
    grad_gain = jnp.sum(grad_normed * values * inverse, axis=0)
    return (grad_values, grad_gain)


def silu_grads(grad_hidden, gate_act, up_activation):
    sigmoid_gate = jax.nn.sigmoid(gate_act)
    grad_gate = grad_hidden * up_activation * sigmoid_gate * (1.0 + gate_act * (1.0 - sigmoid_gate))
    grad_up = grad_hidden * gate_act * sigmoid_gate
    return (grad_gate.astype(jnp.bfloat16), grad_up.astype(jnp.bfloat16))


def pair_swap(value):
    return lax.ppermute(value, "wa", [(0, 1), (1, 0)])


def my_half(value, side, axis):
    size = value.shape[axis] // 2
    return lax.dynamic_slice_in_dim(value, side * size, size, axis)


def heads_as_rows(value):
    return jnp.concatenate(
        [value[:, h * HD : (h + 1) * HD] for h in range(value.shape[1] // HD)], axis=0
    )


def rows_as_heads(value, rows):
    return jnp.concatenate(
        [value[h * rows : (h + 1) * rows] for h in range(value.shape[0] // rows)], axis=1
    )


def seen(query_ref, key_ref, first, count, groups):
    key_pos, key_doc = key_ref[pl.ds(first, count), 0:1], key_ref[pl.ds(first, count), 1:2]
    query_pos, query_doc = query_ref[0:1, :], query_ref[1:2, :]
    visible = (key_pos <= query_pos) & (key_doc == query_doc)
    return jnp.concatenate([visible.astype(jnp.float32)] * groups, axis=1) > 0.5


def attend_kernel(block, query_ref, key_ref, value_ref, query_place, key_place, out_ref, lse_ref):
    rows = query_ref.shape[0]
    groups = query_ref.shape[1] // HD
    scale = HD ** (-0.5)
    queries = heads_as_rows(query_ref[...])

    def step(index, carry):
        peak, total, mixed = carry
        first = pl.multiple_of(index * block, block)
        scores = contract_cols(key_ref[pl.ds(first, block), :], queries) * scale
        visible = seen(query_place, key_place, first, block, groups)
        scores = jnp.where(visible, scores, MASKED_SCORE)
        new_peak = jnp.maximum(peak, jnp.max(scores, axis=0, keepdims=True))
        shrink = jnp.exp(peak - new_peak)
        weights = jnp.where(visible, jnp.exp(scores - new_peak), 0.0)
        total = total * shrink + jnp.sum(weights, axis=0, keepdims=True)
        part = contract_rows(value_ref[pl.ds(first, block), :], weights.astype(jnp.bfloat16))
        return new_peak, total, mixed * shrink + part

    width = groups * rows
    initial = (
        jnp.full((1, width), MASKED_SCORE, jnp.float32),
        jnp.zeros((1, width), jnp.float32),
        jnp.zeros((HD, width), jnp.float32),
    )
    peak, total, mixed = lax.fori_loop(0, key_ref.shape[0] // block, step, initial)
    out_ref[...] = rows_as_heads((mixed / total).T, rows)
    lse_ref[0] = peak + jnp.log(total)


def attend_grads_kernel(
    block,
    query_ref,
    grad_ref,
    key_ref,
    value_ref,
    lse_ref,
    delta_ref,
    query_place,
    key_place,
    query_grad_ref,
    key_grad_ref,
    value_grad_ref,
):
    rows = query_ref.shape[0]
    groups = query_ref.shape[1] // HD
    scale = HD ** (-0.5)
    queries = heads_as_rows(query_ref[...])
    grads = heads_as_rows(grad_ref[...])
    lse, delta = lse_ref[0], delta_ref[0]

    def step(index, total):
        first = pl.multiple_of(index * block, block)
        here = pl.ds(first, block)
        keys = key_ref[here, :]
        scores = contract_cols(keys, queries) * scale
        visible = seen(query_place, key_place, first, block, groups)
        probs = jnp.where(visible, jnp.exp(jnp.where(visible, scores, MASKED_SCORE) - lse), 0.0)
        grad_probs = contract_cols(value_ref[here, :], grads)
        grad_scores = (probs * (grad_probs - delta)).astype(jnp.bfloat16)
        key_grad_ref[here, :] = (matmul(grad_scores, queries) * scale).astype(jnp.bfloat16)
        value_grad_ref[here, :] = matmul(probs.astype(jnp.bfloat16), grads).astype(jnp.bfloat16)
        return total + contract_rows(keys, grad_scores)

    total = lax.fori_loop(
        0, key_ref.shape[0] // block, step, jnp.zeros((HD, groups * rows), jnp.float32)
    )
    query_grad_ref[...] = rows_as_heads((total * scale).T, rows).astype(jnp.bfloat16)


def attention_specs(rows, seq_len):
    wide = HD * (H // KVH)
    return dict(
        query=pl.BlockSpec((rows, wide), lambda a: (0, a)),
        key=pl.BlockSpec((seq_len, HD), lambda a: (0, a)),
        value=pl.BlockSpec((seq_len, HD), lambda a: (0, KVH + a)),
        row=pl.BlockSpec((1, 1, rows * (H // KVH)), lambda a: (a, 0, 0)),
        query_place=pl.BlockSpec((2, rows), lambda a: (0, 0)),
        key_place=pl.BlockSpec((seq_len, 2), lambda a: (0, 0)),
    )


def attend_forward(queries, key_value_all, query_place, key_place):
    rows, seq_len = queries.shape[0], key_value_all.shape[0]
    s = attention_specs(rows, seq_len)
    return pl.pallas_call(
        functools.partial(attend_kernel, min(seq_len, 1024)),
        grid=(KVH,),
        out_shape=[
            jax.ShapeDtypeStruct((rows, H * HD), jnp.float32),
            jax.ShapeDtypeStruct((KVH, 1, rows * (H // KVH)), jnp.float32),
        ],
        in_specs=[s["query"], s["key"], s["value"], s["query_place"], s["key_place"]],
        out_specs=[s["query"], s["row"]],
        compiler_params=pltpu.CompilerParams(vmem_limit_bytes=48 * 2**20),
        name="attend",
    )(queries, key_value_all, key_value_all, query_place, key_place)


def attend_grads(queries, grads, key_value_all, lse, delta, query_place, key_place):
    rows, seq_len = queries.shape[0], key_value_all.shape[0]
    s = attention_specs(rows, seq_len)
    return pl.pallas_call(
        functools.partial(attend_grads_kernel, min(seq_len, 1024)),
        grid=(KVH,),
        out_shape=[
            jax.ShapeDtypeStruct((rows, H * HD), jnp.bfloat16),
            jax.ShapeDtypeStruct((seq_len, KVH * HD), jnp.bfloat16),
            jax.ShapeDtypeStruct((seq_len, KVH * HD), jnp.bfloat16),
        ],
        in_specs=[
            s["query"],
            s["query"],
            s["key"],
            s["value"],
            s["row"],
            s["row"],
            s["query_place"],
            s["key_place"],
        ],
        out_specs=[s["query"], s["key"], s["key"]],
        compiler_params=pltpu.CompilerParams(vmem_limit_bytes=48 * 2**20),
        name="attend_grads",
    )(queries, grads, key_value_all, key_value_all, lse, delta, query_place, key_place)


MESH = pl.DeviceIdType.MESH
NZ, NX, NK = 4, 2, 2
VM = pl.BlockSpec(memory_space=pltpu.VMEM)
HBM = pl.BlockSpec(memory_space=pl.ANY)


def settings(number):
    return pltpu.CompilerParams(
        collective_id=number, has_side_effects=True, vmem_limit_bytes=40 * 2**20
    )


def slot_of(z, x, k):
    return (z * NX + x) * NK + k


def place():
    c = lax.axis_index("ctx")
    return c, c // (NX * NK), lax.rem(c // NK, NX), lax.rem(c, NK), lax.axis_index("wa")


def greet(z, x, k, w, pair, plane=True):
    barrier = pltpu.get_barrier_semaphore()

    def hello(device):
        pl.semaphore_signal(barrier, inc=1, device_id=device, device_id_type=MESH)

    hello((slot_of(z, x, 1 - k), w))
    count = 1
    if pair:
        hello((slot_of(z, x, k), 1 - w))
        count += 1
    if plane:
        hello((slot_of(z, 1 - x, k), w))
        count += 1

        @pl.when(z > 0)
        def _():
            hello((slot_of(z - 1, x, k), w))

        @pl.when(z < NZ - 1)
        def _():
            hello((slot_of(z + 1, x, k), w))

        count += jnp.where(z > 0, 1, 0) + jnp.where(z < NZ - 1, 1, 0)
    pl.semaphore_wait(barrier, count)


def carry_steps(plan, shards, fulls, sems, x, z, k, w):
    own_sem, pair_send, pair_recv, core_send, core_recv = sems
    partner, sibling = (slot_of(z, x, k), 1 - w), (slot_of(z, x, 1 - k), w)

    def rows_of(i, owner):
        h = shards[i].shape[0]
        if plan[i] == "whole":
            return pl.ds(pl.multiple_of(owner * h, h), h)
        half = h // 2
        return pl.ds(pl.multiple_of(owner * h + k * half, half), half)

    def own(i):
        h = shards[i].shape[0]
        return pltpu.make_async_copy(
            shards[i], fulls[i].at[pl.ds(pl.multiple_of(w * h, h), h)], own_sem.at[i]
        )

    def over_pair(i):
        return pltpu.make_async_remote_copy(
            src_ref=shards[i].at[rows_of(i, 0)] if plan[i] == "core" else shards[i],
            dst_ref=fulls[i] if plan[i] == "swap" else fulls[i].at[rows_of(i, w)],
            send_sem=pair_send.at[i],
            recv_sem=pair_recv.at[i],
            device_id=partner,
            device_id_type=MESH,
        )

    def over_core(i):
        here = fulls[i].at[rows_of(i, 1 - w)]
        return pltpu.make_async_remote_copy(
            src_ref=here,
            dst_ref=here,
            send_sem=core_send.at[i],
            recv_sem=core_recv.at[i],
            device_id=sibling,
            device_id_type=MESH,
        )

    every = range(len(shards))

    def start():
        for i in every:
            over_pair(i).start()
        for i in every:
            if plan[i] != "swap":
                own(i).start()

    def hand_on():
        for i in every:
            over_pair(i).wait_recv()
            if plan[i] == "core":
                over_core(i).start()

    def finish():
        for i in every:
            if plan[i] != "swap":
                own(i).wait()
            over_pair(i).wait_send()
            if plan[i] == "core":
                over_core(i).wait()

    return start, hand_on, finish


def carry_semaphores(count):
    return [pltpu.SemaphoreType.DMA((max(count, 1),)) for _ in range(5)]


def weights_kernel(plan, *refs):
    count = len(plan)
    shards, fulls, sems = refs[:count], refs[count : 2 * count], refs[2 * count :]
    me, z, x, k, w = place()
    greet(z, x, k, w, True, False)
    start, hand_on, finish = carry_steps(plan, shards, fulls, sems, x, z, k, w)
    start()
    hand_on()
    finish()


def carried_out(carry):
    return [
        jax.ShapeDtypeStruct(((1 if kind == "swap" else 2) * v.shape[0], *v.shape[1:]), v.dtype)
        for kind, v in carry
    ]


def wa_gather_kernel(carry, number):
    plan, weights = [kind for kind, _ in carry], [v for _, v in carry]
    count = len(weights)
    return pl.pallas_call(
        functools.partial(weights_kernel, plan),
        out_shape=carried_out(carry),
        in_specs=[VM] * count,
        out_specs=[HBM] * count,
        scratch_shapes=carry_semaphores(count),
        compiler_params=settings(number),
        name=f"weights_{number}",
    )(*weights)


def gather_kernel(count, plan, *refs):
    carried = len(plan)
    ins, shards = refs[:count], refs[count : count + carried]
    refs = refs[count + carried :]
    outs, fulls = refs[:count], refs[count : count + carried]
    send_sem, recv_sem, own_sem, *carry_sems = refs[count + carried :]
    me, z, x, k, w = place()
    greet(z, x, k, w, carried > 0)
    up, down = (slot_of(z + 1, x, k), w), (slot_of(z - 1, x, k), w)
    side, sibling = (slot_of(z, 1 - x, k), w), (slot_of(z, x, 1 - k), w)

    def copies(slot, way, device, first=False):
        for i in range(count):
            yield pltpu.make_async_remote_copy(
                src_ref=ins[i] if first else outs[i].at[slot],
                dst_ref=outs[i].at[slot],
                send_sem=send_sem.at[i, slot, way],
                recv_sem=recv_sem.at[i, slot],
                device_id=device,
                device_id_type=MESH,
            )

    def send(*what):
        for c in copies(*what):
            c.start()

    def sent(*what):
        for c in copies(*what):
            c.wait_send()

    def arrived(slot):
        for c in copies(slot, 0, sibling):
            c.wait_recv()

    def across(d, act, wait):
        for sign in (-1, 1) if d else (0,):
            there = z + sign * d

            @pl.when((there >= 0) & (there < NZ))
            def _():
                slot = slot_of(there, 1 - x, k)
                wait(slot)
                act(slot, 3, sibling)

    def walk(act, wait):
        @pl.when(z < NZ - 1)
        def _():
            act(me, 0, up, True)

        @pl.when(z > 0)
        def _():
            act(me, 1, down, True)

        act(me, 2, side, True)
        act(me, 3, sibling, True)
        for d in range(1, NZ):
            for sign in (-1, 1):
                there = z + sign * d

                @pl.when((there >= 0) & (there < NZ))
                def _():
                    slot = slot_of(there, x, k)
                    wait(slot)
                    if sign < 0 and d < NZ - 1:

                        @pl.when(z < NZ - 1)
                        def _():
                            act(slot, 0, up)

                    if sign > 0 and d < NZ - 1:

                        @pl.when(z > 0)
                        def _():
                            act(slot, 1, down)

                    act(slot, 2, side)
                    act(slot, 3, sibling)

            across(d - 1, act, wait)
        across(NZ - 1, act, wait)

    own = [pltpu.make_async_copy(ins[i], outs[i].at[me], own_sem.at[i]) for i in range(count)]
    start, hand_on, finish = carry_steps(plan, shards, fulls, carry_sems, x, z, k, w)
    start()
    walk(send, arrived)
    for o in own:
        o.start()
    hand_on()
    for other in range(NZ * NX):
        arrived(other * NK + 1 - k)
    walk(sent, lambda slot: None)
    for o in own:
        o.wait()
    finish()


def ctx_gather_kernel(values, carry, number):
    plan, weights = [kind for kind, _ in carry], [v for _, v in carry]
    count, carried = len(values), len(weights)
    n = NZ * NX * NK
    done = pl.pallas_call(
        functools.partial(gather_kernel, count, plan),
        out_shape=[jax.ShapeDtypeStruct((n, *v.shape), v.dtype) for v in values]
        + carried_out(carry),
        in_specs=[VM] * (count + carried),
        out_specs=[HBM] * (count + carried),
        scratch_shapes=[
            pltpu.SemaphoreType.DMA((count, n, 4)),
            pltpu.SemaphoreType.DMA((count, n)),
            pltpu.SemaphoreType.DMA((count,)),
        ]
        + carry_semaphores(carried),
        compiler_params=settings(number),
        name=f"gather_{number}",
    )(*values, *weights)
    return done[:count], done[count:]


def scatter_kernel(count, plan, *refs):
    carried = len(plan)
    ins, shards = refs[:count], refs[count : count + carried]
    refs = refs[count + carried :]
    outs, fulls = refs[:count], refs[count : count + carried]
    scratch = refs[count + carried :]
    from_core, from_side, to_side, from_low, from_high, to_z = (
        scratch[g * count : (g + 1) * count] for g in range(6)
    )
    send_core, recv_core, send_side, recv_side, send_z, recv_low, recv_high, *carry_sems = scratch[
        6 * count :
    ]
    me, z, x, k, w = place()
    greet(z, x, k, w, carried > 0)
    up, down = (slot_of(z + 1, x, k), w), (slot_of(z - 1, x, k), w)
    side, sibling = (slot_of(z, 1 - x, k), w), (slot_of(z, x, 1 - k), w)
    f32 = jnp.float32

    def core_copy(i, zz, xx):
        pair = zz * NX + xx
        return pltpu.make_async_remote_copy(
            src_ref=ins[i].at[slot_of(zz, xx, 1 - k)],
            dst_ref=from_core[i].at[pair],
            send_sem=send_core.at[i, pair],
            recv_sem=recv_core.at[i, pair],
            device_id=sibling,
            device_id_type=MESH,
        )

    def side_copy(i, zz):
        return pltpu.make_async_remote_copy(
            src_ref=to_side[i].at[zz],
            dst_ref=from_side[i].at[zz],
            send_sem=send_side.at[i, zz],
            recv_sem=recv_side.at[i, zz],
            device_id=side,
            device_id_type=MESH,
        )

    def z_copy(i, zz, low):
        return pltpu.make_async_remote_copy(
            src_ref=to_z[i].at[zz],
            dst_ref=(from_low if low else from_high)[i].at[zz],
            send_sem=send_z.at[i, zz],
            recv_sem=(recv_low if low else recv_high).at[i, zz],
            device_id=up if low else down,
            device_id_type=MESH,
        )

    def targets(act):
        for d in range(NZ - 1, -1, -1):
            for sign in (1, -1) if d else (0,):
                there = z + sign * d

                @pl.when((there >= 0) & (there < NZ))
                def _():
                    for i in range(count):
                        act(i, there, sign)

    start, hand_on, finish = carry_steps(plan, shards, fulls, carry_sems, x, z, k, w)
    start()
    targets(lambda i, zz, sign: core_copy(i, zz, 1 - x).start())
    targets(lambda i, zz, sign: core_copy(i, zz, x).start())

    def cross(i, zz, sign):
        core_copy(i, zz, 1 - x).wait_recv()
        mine = ins[i][slot_of(zz, 1 - x, k)].astype(f32)
        total = mine + from_core[i][zz * NX + 1 - x].astype(f32)
        to_side[i][zz] = total.astype(to_side[i].dtype)
        side_copy(i, zz).start()

    targets(cross)

    def along(i, zz, sign):
        core_copy(i, zz, x).wait_recv()
        side_copy(i, zz).wait_recv()
        total = ins[i][slot_of(zz, x, k)].astype(f32) + from_core[i][zz * NX + x].astype(f32)
        total = total + from_side[i][zz].astype(f32)
        if sign == 0:
            outs[i][...] = total

            @pl.when(z > 0)
            def _():
                z_copy(i, zz, True).wait_recv()
                outs[i][...] += from_low[i][zz].astype(f32)

            @pl.when(z < NZ - 1)
            def _():
                z_copy(i, zz, False).wait_recv()
                outs[i][...] += from_high[i][zz].astype(f32)

            return
        low = sign > 0
        came = from_low if low else from_high
        first = (z == 0) if low else (z == NZ - 1)

        @pl.when(first)
        def _():
            to_z[i][zz] = total.astype(to_z[i].dtype)

        @pl.when(jnp.logical_not(first))
        def _():
            z_copy(i, zz, low).wait_recv()
            to_z[i][zz] = (total + came[i][zz].astype(f32)).astype(to_z[i].dtype)

        z_copy(i, zz, low).start()

    targets(along)
    hand_on()

    def settle(i, zz, sign):
        core_copy(i, zz, 1 - x).wait_send()
        core_copy(i, zz, x).wait_send()
        side_copy(i, zz).wait_send()
        if sign:
            z_copy(i, zz, sign > 0).wait_send()

    targets(settle)
    finish()


def ctx_scatter_kernel(values, carry, number):
    plan, weights = [kind for kind, _ in carry], [v for _, v in carry]
    count, carried = len(values), len(weights)
    dma = pltpu.SemaphoreType.DMA
    scratch = []
    for lead in (NZ * NX, NZ, NZ, NZ, NZ, NZ):
        scratch += [pltpu.VMEM((lead, *v.shape[1:]), v.dtype) for v in values]
    done = pl.pallas_call(
        functools.partial(scatter_kernel, count, plan),
        out_shape=[jax.ShapeDtypeStruct(v.shape[1:], jnp.float32) for v in values]
        + carried_out(carry),
        in_specs=[VM] * (count + carried),
        out_specs=[VM] * count + [HBM] * carried,
        scratch_shapes=scratch
        + [dma((count, NZ * NX)), dma((count, NZ * NX))]
        + [dma((count, NZ)) for _ in range(5)]
        + carry_semaphores(carried),
        compiler_params=settings(number),
        name=f"scatter_{number}",
    )(*values, *weights)
    return done[:count], done[count:]


def planned():
    return lax.axis_size("ctx") == NZ * NX * NK and lax.axis_size("wa") == 2


def wa_gather(carry, number):
    if planned() and carry:
        return wa_gather_kernel(carry, number)
    return [
        pair_swap(v) if kind == "swap" else lax.all_gather(v, "wa", axis=0, tiled=True)
        for kind, v in carry
    ]


def ctx_gather(values, carry, number):
    if planned():
        return ctx_gather_kernel(values, carry, number)
    return [lax.all_gather(v, "ctx", axis=0) for v in values], wa_gather(carry, number)


def ctx_scatter_sum(values, carry, number):
    if planned():
        return ctx_scatter_kernel(values, carry, number)
    summed = [lax.psum_scatter(v, "ctx", scatter_dimension=0).astype(jnp.float32) for v in values]
    return summed, wa_gather(carry, number)


def per_device(
    tokens,
    doc_starts,
    routes,
    valid,
    teacher,
    out_grad,
    norm1_gain,
    w_query,
    w_key,
    w_value,
    w_out,
    norm2_gain,
    w_router,
    shared_gate,
    shared_up,
    shared_down,
    expert_gate,
    expert_up,
    expert_down,
):
    ctx_count = lax.axis_size("ctx")
    ctx_rank = lax.axis_index("ctx")
    wa_count = lax.axis_size("wa")
    side = lax.axis_index("wa")
    local_rows = tokens.shape[1]
    seq_len = local_rows * ctx_count
    groups = H // KVH
    kv_width = KVH * HD
    experts = w_router.shape[1]
    width = tokens.shape[2]
    lanes = 128
    hidden = expert_gate.shape[2]
    shared_half = shared_down.shape[0]
    run = shared_half // ctx_count
    low = jnp.bfloat16

    gain_rows = width // wa_count // lanes
    valid_rows = valid[0].astype(jnp.float32)
    small = jnp.zeros((16, lanes), jnp.float32)
    small = small.at[:gain_rows].set(norm1_gain.astype(jnp.float32).reshape(gain_rows, lanes))
    small = small.at[8 : 8 + gain_rows].set(
        norm2_gain.astype(jnp.float32).reshape(gain_rows, lanes)
    )
    weight_query, weight_key, weight_value, small_all, valid_there = wa_gather(
        [
            ("core", w_query),
            ("core", w_key),
            ("core", w_value),
            ("core", small),
            ("swap", jnp.broadcast_to(valid_rows, (8, lanes))),
        ],
        1,
    )
    small_all = small_all.reshape(wa_count, 16, lanes)
    gain_one = small_all[:, :gain_rows].reshape(width)
    gain_two = small_all[:, 8 : 8 + gain_rows].reshape(width)
    valid_here = jnp.sum(valid_rows) + jnp.sum(valid_there[0])

    doc_first = doc_starts[0]
    own_rows = ctx_rank * local_rows + jnp.arange(local_rows, dtype=jnp.int32)
    query_pos = stored_position(own_rows, local_rows, ctx_count)
    query_place = jnp.stack([query_pos, document_of(query_pos, doc_first)])
    key_pos = stored_position(jnp.arange(seq_len, dtype=jnp.int32), local_rows, ctx_count)
    key_place = jnp.stack([key_pos, document_of(key_pos, doc_first)], axis=1)

    residual = tokens[0].astype(jnp.float32)
    inverse_one, normed = norm_forward(residual, gain_one)
    normed_one = normed.astype(low)
    queries = matmul(normed_one, weight_query).astype(low)
    key_rows = matmul(normed_one, weight_key).astype(low)
    value_rows = matmul(normed_one, weight_value).astype(low)

    def shared_columns(weight):
        return [
            lax.dynamic_slice_in_dim(weight, half * shared_half + ctx_rank * run, run, 1)
            for half in range(wa_count)
        ]

    wide_in = jnp.concatenate(
        [expert_gate[0], expert_up[0], *shared_columns(shared_gate), *shared_columns(shared_up)],
        axis=1,
    )
    down_rows = lax.dynamic_slice_in_dim(shared_down, ctx_rank * run, run, 0)
    (key_value_all, valid_all), (weight_out, router_t, weight_down, weight_sdown) = ctx_gather(
        [jnp.concatenate([key_rows, value_rows], axis=1), jnp.full((8, lanes), valid_here)],
        [
            ("core", w_out),
            ("core", w_router.astype(jnp.float32).T),
            ("whole", expert_down[0]),
            ("whole", down_rows),
        ],
        2,
    )
    key_value_all = key_value_all.reshape(seq_len, 2 * kv_width)
    valid_total = jnp.sum(valid_all[:, 0, 0])
    router_t = router_t.reshape(wa_count, experts, width // wa_count)
    weight_router = jnp.transpose(router_t, (0, 2, 1)).reshape(width, experts).astype(low)
    attn, lse = attend_forward(queries, key_value_all, query_place, key_place)
    attn_low = attn.astype(low)
    hidden_one = residual + matmul(attn_low, weight_out)
    inverse_two, normed = norm_forward(hidden_one, gain_two)
    normed_two = normed.astype(low)

    logits = matmul(normed_two, weight_router)
    choose = routes[0][:, :, None] == jnp.arange(experts, dtype=jnp.int32)[None, None, :]
    chosen = jnp.any(choose, axis=1)
    peak = jnp.max(jnp.where(chosen, logits, MASKED_SCORE), axis=1, keepdims=True)
    weights = jnp.where(chosen, jnp.exp(jnp.where(chosen, logits, peak) - peak), 0.0)
    gates = weights / jnp.sum(weights, axis=1, keepdims=True)

    (normed_all, gates_all), (weight_in,) = ctx_gather(
        [normed_two, gates.T], [("whole", wide_in)], 3
    )
    normed_all = normed_all.reshape(seq_len, width)
    gate = lax.dynamic_slice_in_dim(gates_all, ctx_rank, 1, 1).reshape(seq_len, 1)
    acts = matmul(normed_all, weight_in)
    gate_act, up_act = acts[:, :hidden], acts[:, hidden : 2 * hidden]
    shared_gact = acts[:, 2 * hidden : 2 * hidden + 2 * run]
    shared_uact = acts[:, 2 * hidden + 2 * run :]
    hidden_exp = (jax.nn.silu(gate_act) * up_act).astype(low)
    shared_hidden = (jax.nn.silu(shared_gact) * shared_uact).astype(low)
    expert_out = matmul(hidden_exp, weight_down).astype(low)
    mixed = gate * expert_out.astype(jnp.float32) + matmul(shared_hidden, weight_sdown)
    (routed,), _ = ctx_scatter_sum(
        [mixed.astype(low).reshape(ctx_count, local_rows, width)], [], 4
    )
    produced = hidden_one + routed
    output = produced.astype(low)[None]

    errors = produced - teacher[0].astype(jnp.float32)
    local_error = jnp.sum(valid_rows[:, None] * errors * errors)
    tokens_all = wa_count * seq_len
    grad_out = (
        out_grad[0].astype(jnp.float32)
        + 2.0 * tokens_all / valid_total * valid_rows[:, None] * errors
    )
    (grad_all,), _ = ctx_gather([grad_out.astype(low)], [], 5)
    grad_all = grad_all.reshape(seq_len, width)

    grad_wide = grad_all.astype(jnp.float32)
    grad_picked = (gate * grad_wide).astype(low)
    gate_dot = jnp.sum(grad_wide * expert_out.astype(jnp.float32), axis=1)
    grad_acts = jnp.concatenate(
        [
            *silu_grads(contract_cols(grad_picked, weight_down), gate_act, up_act),
            *silu_grads(contract_cols(grad_all, weight_sdown), shared_gact, shared_uact),
        ],
        axis=1,
    )
    grad_rows = contract_cols(grad_acts, weight_in)
    small = jnp.full((ctx_count, experts + 8, local_rows), local_error)
    small = small.at[:, :experts].set(0.0)
    small = lax.dynamic_update_slice(
        small, gate_dot.reshape(ctx_count, 1, local_rows), (0, ctx_rank, 0)
    )
    (grad_back, small), (attn_there, normed_one_there, normed_two_there) = ctx_scatter_sum(
        [grad_rows.astype(low).reshape(ctx_count, local_rows, width), small],
        [
            ("swap", my_half(attn_low, 1 - side, 1)),
            ("swap", my_half(normed_one, 1 - side, 1)),
            ("swap", my_half(normed_two, 1 - side, 1)),
        ],
        6,
    )
    grad_gates = small[:experts].T
    error_total = small[experts, 0]
    grad_logits = (
        gates * (grad_gates - jnp.sum(gates * grad_gates, axis=1, keepdims=True))
    ).astype(low)
    grad_normed = grad_back + contract_cols(grad_logits, weight_router)

    in_grad = contract_rows(normed_all, grad_acts)
    down_grad = contract_rows(hidden_exp, grad_picked)
    sdown_grad = contract_rows(shared_hidden, grad_all)

    def for_pair(full):
        return ("swap", my_half(full, 1 - side, 0).astype(low))

    def with_pair(full, other):
        return my_half(full, side, 0) + other.astype(jnp.float32)

    grad_hidden_norm, grad_gain_two = norm_backward(hidden_one, inverse_two, gain_two, grad_normed)
    grad_hidden_one = grad_out + grad_hidden_norm
    grad_attn_in = grad_hidden_one.astype(low)
    grad_heads = contract_cols(grad_attn_in, weight_out).astype(low)
    delta = jnp.einsum(
        "tagd,tagd->agt",
        grad_heads.astype(jnp.float32).reshape(local_rows, KVH, groups, HD),
        attn.reshape(local_rows, KVH, groups, HD),
    ).reshape(KVH, 1, groups * local_rows)
    grad_query, grad_keys, grad_values = attend_grads(
        queries, grad_heads, key_value_all, lse, delta, query_place, key_place
    )
    def for_all(vector):
        flat = jnp.zeros((16 * lanes,), jnp.float32).at[: vector.shape[0]].set(vector)
        return jnp.broadcast_to(flat.reshape(16, lanes), (ctx_count, 16, lanes))

    def from_all(summed, size):
        return summed.reshape(16 * lanes)[:size]

    def by_slot(value):
        return value.reshape(ctx_count, value.shape[0] // ctx_count, value.shape[1])

    half_width = width // wa_count
    (grad_key, grad_value, small), (
        da_there,
        logits_there,
        query_there,
        error_there,
        in_there,
        sdown_there,
    ) = ctx_scatter_sum(
        [
            grad_keys.reshape(ctx_count, local_rows, kv_width),
            grad_values.reshape(ctx_count, local_rows, kv_width),
            for_all(grad_gain_two),
        ],
        [
            ("swap", grad_attn_in),
            ("swap", grad_logits),
            ("swap", grad_query),
            ("swap", jnp.full((8, lanes), error_total)),
            for_pair(in_grad[:, 2 * hidden :]),
            for_pair(sdown_grad),
        ],
        7,
    )
    error_total = error_total + error_there[0, 0]
    key_value_low = jnp.concatenate([grad_key, grad_value], axis=1).astype(low)
    gain_two_sum = from_all(small, width)

    def weight_grad(mine, right, theirs, right_there):
        mine = my_half(mine, side, 1)
        return (contract_rows(mine, right) + contract_rows(theirs, right_there)).astype(low)

    out_part = weight_grad(attn_low, grad_attn_in, attn_there, da_there)
    router_part = contract_rows(grad_logits, my_half(normed_two, side, 1)) + contract_rows(
        logits_there, normed_two_there
    )
    shared_part = with_pair(in_grad[:, 2 * hidden :], in_there).astype(low)
    sdown_part = with_pair(sdown_grad, sdown_there).astype(low)
    rows_two = jnp.zeros((16, lanes), jnp.float32)
    rows_two = rows_two.at[: half_width // lanes].set(
        my_half(gain_two_sum, 1 - side, 0).reshape(-1, lanes)
    )
    router_rows = router_part.reshape(experts, half_width // lanes, lanes)
    router_rows = jnp.pad(router_rows, ((0, 0), (0, 8 - half_width // lanes), (0, 0)))
    (out_sum, router_sum), (kv_there, rows_there, down_there) = ctx_scatter_sum(
        [by_slot(out_part), router_rows],
        [("swap", key_value_low), ("swap", rows_two), for_pair(down_grad)],
        8,
    )
    total_gain_two = my_half(gain_two_sum, side, 0) + rows_there.reshape(-1)[:half_width]

    grad_normed_one = (
        contract_cols(grad_query, weight_query)
        + contract_cols(key_value_low[:, :kv_width], weight_key)
        + contract_cols(key_value_low[:, kv_width:], weight_value)
    )
    grad_residual_norm, grad_gain_one = norm_backward(
        residual, inverse_one, gain_one, grad_normed_one
    )
    grad_input = grad_hidden_one + grad_residual_norm
    (query_sum, kv_sum, small), (in_there,) = ctx_scatter_sum(
        [
            by_slot(weight_grad(normed_one, grad_query, normed_one_there, query_there)),
            by_slot(weight_grad(normed_one, key_value_low, normed_one_there, kv_there)),
            for_all(grad_gain_one),
        ],
        [for_pair(in_grad[:, : 2 * hidden])],
        9,
    )
    gain_one_sum = from_all(small, width)
    rows_one = jnp.zeros((16, lanes), jnp.float32)
    rows_one = rows_one.at[: half_width // lanes].set(
        my_half(gain_one_sum, 1 - side, 0).reshape(-1, lanes)
    )
    (total_query, total_kv, total_out, router_sum, shared_parts, sdown_parts), (rows_there,) = (
        ctx_gather(
            [
                query_sum.astype(low),
                kv_sum.astype(low),
                out_sum.astype(low),
                router_sum,
                shared_part,
                sdown_part,
            ],
            [("swap", rows_one)],
            10,
        )
    )
    total_gain_one = my_half(gain_one_sum, side, 0) + rows_there.reshape(-1)[:half_width]
    total_query = total_query.reshape(half_width, width).astype(jnp.float32)
    total_kv = total_kv.reshape(half_width, 2 * kv_width).astype(jnp.float32)
    total_out = total_out.reshape(half_width, width).astype(jnp.float32)
    router_sum = router_sum[:, : half_width // lanes].reshape(experts, half_width)
    shared_parts = shared_parts.reshape(ctx_count, half_width, 2, wa_count, run)
    shared_parts = jnp.transpose(shared_parts, (2, 1, 3, 0, 4)).astype(jnp.float32)
    shared_parts = shared_parts.reshape(2, half_width, wa_count * shared_half)
    in_grad = with_pair(in_grad[:, : 2 * hidden], in_there)
    down_grad = with_pair(down_grad, down_there)
    return (
        error_total / (valid_total * width),
        output,
        grad_input[None],
        total_gain_one,
        total_query,
        total_kv[:, :kv_width],
        total_kv[:, kv_width:],
        total_out,
        total_gain_two,
        router_sum.T,
        shared_parts[0],
        shared_parts[1],
        sdown_parts.reshape(shared_half, width).astype(jnp.float32),
        in_grad[None, :, :hidden],
        in_grad[None, :, hidden:],
        down_grad[None],
    )


def solution(mesh):
    return jax.shard_map(
        per_device,
        mesh=mesh,
        in_specs=(
            P("wa", "ctx", None),
            P("wa", None),
            P("wa", "ctx", None),
            P("wa", "ctx"),
            P("wa", "ctx", None),
            P("wa", "ctx", None),
            P("wa"),
            P("wa", None),
            P("wa", None),
            P("wa", None),
            P("wa", None),
            P("wa"),
            P("wa", None),
            P("wa", None),
            P("wa", None),
            P("wa", None),
            P("ctx", "wa", None),
            P("ctx", "wa", None),
            P("ctx", "wa", None),
        ),
        out_specs=(
            P(),
            P("wa", "ctx", None),
            P("wa", "ctx", None),
            P("wa"),
            P("wa", None),
            P("wa", None),
            P("wa", None),
            P("wa", None),
            P("wa"),
            P("wa", None),
            P("wa", None),
            P("wa", None),
            P("wa", None),
            P("ctx", "wa", None),
            P("ctx", "wa", None),
            P("ctx", "wa", None),
        ),
        check_vma=False,
    )
```

```python
import functools

import jax
import jax.numpy as jnp
from jax import lax
from jax.experimental import pallas as pl
from jax.experimental.pallas import tpu as pltpu
from jax.sharding import PartitionSpec as P

H = 12
KVH = 4
HD = 128
EPSILON = 1e-05
MASKED_SCORE = -1e30


def stored_position(stored_rows, local_rows, ctx_count):
    half_rows = local_rows // 2
    owner_rank = stored_rows // local_rows
    within_rows = stored_rows % local_rows
    first_half = owner_rank * half_rows + within_rows
    second_half = (2 * ctx_count - 1 - owner_rank) * half_rows + within_rows - half_rows
    return jnp.where(within_rows < half_rows, first_half, second_half)


def document_of(positions, doc_first):
    return jnp.sum((doc_first[None, :] <= positions[:, None]).astype(jnp.int32), axis=1) - 1


def matmul(left, right):
    return jnp.dot(left, right, preferred_element_type=jnp.float32)


def contract_rows(left, right):
    return lax.dot_general(
        left, right, (((0,), (0,)), ((), ())), preferred_element_type=jnp.float32
    )


def contract_cols(left, right):
    return lax.dot_general(
        left, right, (((1,), (1,)), ((), ())), preferred_element_type=jnp.float32
    )


def rms_inverse(values):
    return lax.rsqrt(jnp.mean(values * values, axis=1, keepdims=True) + EPSILON)


def norm_backward(values, inverse, gain, grad_normed):
    scaled = grad_normed * gain
    inner_sum = jnp.sum(scaled * values, axis=1, keepdims=True)
    grad_values = (
        inverse * scaled - values * (inverse * inverse * inverse) * inner_sum / values.shape[1]
    )
    grad_gain = jnp.sum(grad_normed * values * inverse, axis=0)
    return (grad_values, grad_gain)


def pair_swap(value):
    return lax.ppermute(value, "wa", [(0, 1), (1, 0)])


def my_half(value, side, axis):
    size = value.shape[axis] // 2
    return lax.dynamic_slice_in_dim(value, side * size, size, axis)


def heads_as_rows(value):
    return jnp.concatenate(
        [value[:, h * HD : (h + 1) * HD] for h in range(value.shape[1] // HD)], axis=0
    )


def rows_as_heads(value, rows):
    return jnp.concatenate(
        [value[h * rows : (h + 1) * rows] for h in range(value.shape[0] // rows)], axis=1
    )


def seen(query_ref, key_ref, first, count, groups):
    key_pos, key_doc = key_ref[pl.ds(first, count), 0:1], key_ref[pl.ds(first, count), 1:2]
    query_pos, query_doc = query_ref[0:1, :], query_ref[1:2, :]
    visible = (key_pos <= query_pos) & (key_doc == query_doc)
    return jnp.concatenate([visible.astype(jnp.float32)] * groups, axis=1) > 0.5


def attend_kernel(block, query_ref, key_ref, value_ref, query_place, key_place, out_ref, lse_ref):
    rows = query_ref.shape[0]
    groups = query_ref.shape[1] // HD
    scale = HD ** (-0.5)
    queries = heads_as_rows(query_ref[...])

    def step(index, carry):
        peak, total, mixed = carry
        first = pl.multiple_of(index * block, block)
        scores = contract_cols(key_ref[pl.ds(first, block), :], queries) * scale
        visible = seen(query_place, key_place, first, block, groups)
        scores = jnp.where(visible, scores, MASKED_SCORE)
        new_peak = jnp.maximum(peak, jnp.max(scores, axis=0, keepdims=True))
        shrink = jnp.exp(peak - new_peak)
        weights = jnp.where(visible, jnp.exp(scores - new_peak), 0.0)
        total = total * shrink + jnp.sum(weights, axis=0, keepdims=True)
        part = contract_rows(value_ref[pl.ds(first, block), :], weights.astype(jnp.bfloat16))
        return new_peak, total, mixed * shrink + part

    width = groups * rows
    initial = (
        jnp.full((1, width), MASKED_SCORE, jnp.float32),
        jnp.zeros((1, width), jnp.float32),
        jnp.zeros((HD, width), jnp.float32),
    )
    peak, total, mixed = lax.fori_loop(0, key_ref.shape[0] // block, step, initial)
    out_ref[...] = rows_as_heads((mixed / total).T, rows)
    lse_ref[0] = peak + jnp.log(total)


def attend_grads_kernel(
    block,
    query_ref,
    grad_ref,
    key_ref,
    value_ref,
    lse_ref,
    delta_ref,
    query_place,
    key_place,
    query_grad_ref,
    key_grad_ref,
    value_grad_ref,
):
    rows = query_ref.shape[0]
    groups = query_ref.shape[1] // HD
    scale = HD ** (-0.5)
    queries = heads_as_rows(query_ref[...])
    grads = heads_as_rows(grad_ref[...])
    lse, delta = lse_ref[0], delta_ref[0]

    def step(index, total):
        first = pl.multiple_of(index * block, block)
        here = pl.ds(first, block)
        keys = key_ref[here, :]
        scores = contract_cols(keys, queries) * scale
        visible = seen(query_place, key_place, first, block, groups)
        probs = jnp.where(visible, jnp.exp(jnp.where(visible, scores, MASKED_SCORE) - lse), 0.0)
        grad_probs = contract_cols(value_ref[here, :], grads)
        grad_scores = (probs * (grad_probs - delta)).astype(jnp.bfloat16)
        key_grad_ref[here, :] = (matmul(grad_scores, queries) * scale).astype(jnp.bfloat16)
        value_grad_ref[here, :] = matmul(probs.astype(jnp.bfloat16), grads).astype(jnp.bfloat16)
        return total + contract_rows(keys, grad_scores)

    total = lax.fori_loop(
        0, key_ref.shape[0] // block, step, jnp.zeros((HD, groups * rows), jnp.float32)
    )
    query_grad_ref[...] = rows_as_heads((total * scale).T, rows).astype(jnp.bfloat16)


def attention_specs(rows, seq_len):
    wide = HD * (H // KVH)
    return dict(
        query=pl.BlockSpec((rows, wide), lambda a: (0, a)),
        key=pl.BlockSpec((seq_len, HD), lambda a: (0, a)),
        value=pl.BlockSpec((seq_len, HD), lambda a: (0, KVH + a)),
        row=pl.BlockSpec((1, 1, rows * (H // KVH)), lambda a: (a, 0, 0)),
        query_place=pl.BlockSpec((2, rows), lambda a: (0, 0)),
        key_place=pl.BlockSpec((seq_len, 2), lambda a: (0, 0)),
    )


def attend_forward(queries, key_value_all, query_place, key_place):
    rows, seq_len = queries.shape[0], key_value_all.shape[0]
    s = attention_specs(rows, seq_len)
    return pl.pallas_call(
        functools.partial(attend_kernel, min(seq_len, 1024)),
        grid=(KVH,),
        out_shape=[
            jax.ShapeDtypeStruct((rows, H * HD), jnp.float32),
            jax.ShapeDtypeStruct((KVH, 1, rows * (H // KVH)), jnp.float32),
        ],
        in_specs=[s["query"], s["key"], s["value"], s["query_place"], s["key_place"]],
        out_specs=[s["query"], s["row"]],
        compiler_params=pltpu.CompilerParams(vmem_limit_bytes=20 * 2**20),
        name="attend",
    )(queries, key_value_all, key_value_all, query_place, key_place)


def attend_grads(queries, grads, key_value_all, lse, delta, query_place, key_place):
    rows, seq_len = queries.shape[0], key_value_all.shape[0]
    s = attention_specs(rows, seq_len)
    return pl.pallas_call(
        functools.partial(attend_grads_kernel, min(seq_len, 1024)),
        grid=(KVH,),
        out_shape=[
            jax.ShapeDtypeStruct((rows, H * HD), jnp.bfloat16),
            jax.ShapeDtypeStruct((seq_len, KVH * HD), jnp.bfloat16),
            jax.ShapeDtypeStruct((seq_len, KVH * HD), jnp.bfloat16),
        ],
        in_specs=[
            s["query"],
            s["query"],
            s["key"],
            s["value"],
            s["row"],
            s["row"],
            s["query_place"],
            s["key_place"],
        ],
        out_specs=[s["query"], s["key"], s["key"]],
        compiler_params=pltpu.CompilerParams(vmem_limit_bytes=32 * 2**20),
        name="attend_grads",
    )(queries, grads, key_value_all, key_value_all, lse, delta, query_place, key_place)

def expert_forward_kernel(
    side_ref, rows_ref, gate_ref, own_in, other_in, own_down, other_down, sdown, acts_ref, mixed_ref
):
    side = side_ref[0]
    hidden, depth = own_down.shape[0] * 2, own_in.shape[0]
    pad = sdown.shape[0]

    def half(size, which):
        return pl.ds(pl.multiple_of(which * size, size), size)

    acts_ref[...] = matmul(rows_ref[:, half(depth, side)], own_in[...]) + matmul(
        rows_ref[:, half(depth, 1 - side)], other_in[...]
    )
    gate_act, up_act = acts_ref[:, :hidden], acts_ref[:, hidden : 2 * hidden]
    hidden_exp = (gate_act * jax.nn.sigmoid(gate_act) * up_act).astype(jnp.bfloat16)
    shared_gact = acts_ref[:, 2 * hidden : 2 * hidden + pad]
    shared_uact = acts_ref[:, 2 * hidden + pad :]
    shared_hidden = (shared_gact * jax.nn.sigmoid(shared_gact) * shared_uact).astype(jnp.bfloat16)
    first, second = hidden_exp[:, : hidden // 2], hidden_exp[:, hidden // 2 :]
    swap = side == 1
    out = matmul(jnp.where(swap, second, first), own_down[...]) + matmul(
        jnp.where(swap, first, second), other_down[...]
    )
    mixed = gate_ref[...] * out.astype(jnp.bfloat16).astype(jnp.float32)
    mixed_ref[...] = (mixed + matmul(shared_hidden, sdown[...])).astype(jnp.bfloat16)


def expert_backward_kernel(
    side_ref,
    rows_ref,
    grad_ref,
    acts_ref,
    gate_ref,
    own_in,
    other_in,
    own_down,
    other_down,
    sdown,
    grad_rows_ref,
    dots_ref,
    gate_own,
    up_own,
    gate_other,
    up_other,
    down_own,
    down_other,
    shared_out,
    sdown_out,
    acts_grad,
    in_total,
    down_total,
    shared_total,
    sdown_total,
):
    low = jnp.bfloat16
    side = side_ref[0]
    hidden, depth = own_down.shape[0] * 2, own_in.shape[0]
    pad = sdown.shape[0]

    def half(size, which):
        return pl.ds(pl.multiple_of(which * size, size), size)

    @pl.when(pl.program_id(0) == 0)
    def _():
        for total in (in_total, down_total, shared_total, sdown_total):
            total[...] = jnp.zeros_like(total)

    rows, grads, gate = rows_ref[...], grad_ref[...], gate_ref[...]
    ours, theirs = contract_cols(grads, own_down[...]), contract_cols(grads, other_down[...])
    swap = side == 1
    grad_hidden = jnp.concatenate(
        [jnp.where(swap, theirs, ours), jnp.where(swap, ours, theirs)], axis=1
    )

    def through(grad, gate_act, up_act, at):
        sigmoid = jax.nn.sigmoid(gate_act)
        silu = gate_act * sigmoid
        width = gate_act.shape[1]
        grad_gate = grad * up_act * sigmoid * (1.0 + gate_act * (1.0 - sigmoid))
        acts_grad[:, at : at + width] = grad_gate.astype(low)
        acts_grad[:, at + width : at + 2 * width] = (grad * silu).astype(low)
        return (silu * up_act).astype(low)

    hidden_exp = through(
        gate * grad_hidden, acts_ref[:, :hidden], acts_ref[:, hidden : 2 * hidden], 0
    )
    shared_hidden = through(
        contract_cols(grads, sdown[...]),
        acts_ref[:, 2 * hidden : 2 * hidden + pad],
        acts_ref[:, 2 * hidden + pad :],
        2 * hidden,
    )
    dots_ref[...] = jnp.sum(grad_hidden * hidden_exp.astype(jnp.float32), axis=1, keepdims=True)
    grad_rows_ref[:, half(depth, side)] = contract_cols(acts_grad[...], own_in[...]).astype(low)
    grad_rows_ref[:, half(depth, 1 - side)] = contract_cols(acts_grad[...], other_in[...]).astype(
        low
    )
    in_total[...] += contract_rows(rows, acts_grad[:, : 2 * hidden])
    shared_total[...] += contract_rows(acts_grad[:, 2 * hidden :], rows)
    picked = (gate * grads.astype(jnp.float32)).astype(low)
    down_total[...] += contract_rows(hidden_exp, picked)
    sdown_total[...] += contract_rows(shared_hidden, grads)

    @pl.when(pl.program_id(0) == pl.num_programs(0) - 1)
    def _():
        mine, other = half(depth, side), half(depth, 1 - side)
        gate_own[...] = in_total[mine, :hidden]
        up_own[...] = in_total[mine, hidden:]
        gate_other[...] = in_total[other, :hidden].astype(low)
        up_other[...] = in_total[other, hidden:].astype(low)
        down_own[...] = down_total[half(hidden // 2, side), :]
        down_other[...] = down_total[half(hidden // 2, 1 - side), :].astype(low)
        shared_out[...] = shared_total[...]
        sdown_out[...] = sdown_total[...]


def whole(value):
    return pl.BlockSpec(value.shape, lambda i: (0,) * len(value.shape))


def by_rows(block, columns):
    return pl.BlockSpec((block, columns), lambda i: (i, 0))


def expert_forward(side, rows, gate, weights):
    total, width = rows.shape
    block, acts = min(total, 256), weights[0].shape[1]
    return pl.pallas_call(
        expert_forward_kernel,
        grid=(total // block,),
        out_shape=[
            jax.ShapeDtypeStruct((total, acts), jnp.float32),
            jax.ShapeDtypeStruct((total, width), jnp.bfloat16),
        ],
        in_specs=[
            pl.BlockSpec(memory_space=pltpu.SMEM),
            by_rows(block, width),
            by_rows(block, 1),
            *map(whole, weights),
        ],
        out_specs=[by_rows(block, acts), by_rows(block, width)],
        compiler_params=pltpu.CompilerParams(vmem_limit_bytes=32 * 2**20),
        name="expert_forward",
    )(side, rows, gate, *weights)


def expert_backward(side, rows, grads, acts, gate, weights):
    total, width = rows.shape
    block, columns = min(total, 256), weights[0].shape[1]
    depth, hidden = weights[0].shape[0], 2 * weights[2].shape[0]
    pad = weights[4].shape[0]
    shape, f32, low = jax.ShapeDtypeStruct, jnp.float32, jnp.bfloat16
    ends = [
        shape((depth, hidden), f32),
        shape((depth, hidden), f32),
        shape((depth, hidden), low),
        shape((depth, hidden), low),
        shape((hidden // 2, width), f32),
        shape((hidden // 2, width), low),
        shape((2 * pad, width), f32),
        shape((pad, width), f32),
    ]
    return pl.pallas_call(
        expert_backward_kernel,
        grid=(total // block,),
        out_shape=[shape((total, width), low), shape((total, 1), f32), *ends],
        in_specs=[
            pl.BlockSpec(memory_space=pltpu.SMEM),
            by_rows(block, width),
            by_rows(block, width),
            by_rows(block, columns),
            by_rows(block, 1),
            *map(whole, weights),
        ],
        out_specs=[by_rows(block, width), by_rows(block, 1), *map(whole, ends)],
        scratch_shapes=[
            pltpu.VMEM((block, columns), low),
            pltpu.VMEM((width, 2 * hidden), f32),
            pltpu.VMEM((hidden, width), f32),
            pltpu.VMEM((2 * pad, width), f32),
            pltpu.VMEM((pad, width), f32),
        ],
        compiler_params=pltpu.CompilerParams(vmem_limit_bytes=60 * 2**20),
        name="expert_backward",
    )(side, rows, grads, acts, gate, *weights)


MESH = pl.DeviceIdType.MESH
NZ, NX, NK = 4, 2, 2
VM = pl.BlockSpec(memory_space=pltpu.VMEM)
HBM = pl.BlockSpec(memory_space=pl.ANY)


def settings(number, held):
    return pltpu.CompilerParams(
        collective_id=number, has_side_effects=True, vmem_limit_bytes=held + 4 * 2**20
    )


def bytes_of(arrays):
    return sum(v.size * v.dtype.itemsize for v in arrays)


def slot_of(z, x, k):
    return (z * NX + x) * NK + k


def place():
    c = lax.axis_index("ctx")
    return c, c // (NX * NK), lax.rem(c // NK, NX), lax.rem(c, NK), lax.axis_index("wa")


def greet(z, x, k, w, pair, plane=True):
    barrier = pltpu.get_barrier_semaphore()

    def hello(device):
        pl.semaphore_signal(barrier, inc=1, device_id=device, device_id_type=MESH)

    hello((slot_of(z, x, 1 - k), w))
    count = 1
    if pair:
        hello((slot_of(z, x, k), 1 - w))
        count += 1
    if plane:
        hello((slot_of(z, 1 - x, k), w))
        count += 1

        @pl.when(z > 0)
        def _():
            hello((slot_of(z - 1, x, k), w))

        @pl.when(z < NZ - 1)
        def _():
            hello((slot_of(z + 1, x, k), w))

        count += jnp.where(z > 0, 1, 0) + jnp.where(z < NZ - 1, 1, 0)
    pl.semaphore_wait(barrier, count)


def carry_steps(plan, shards, targets, sems, x, z, k, w):
    own_sem, pair_send, pair_recv, core_send, core_recv = sems
    partner, sibling = (slot_of(z, x, k), 1 - w), (slot_of(z, x, 1 - k), w)
    plan, outs, columns = zip(*plan) if plan else ((), (), ())
    fulls = [
        targets[o] if c is None else targets[o].at[:, pl.ds(c, shards[i].shape[1])]
        for i, (o, c) in enumerate(zip(outs, columns))
    ]

    def rows_of(i, owner):
        h = shards[i].shape[0]
        if plan[i] == "whole":
            return pl.ds(pl.multiple_of(owner * h, h), h)
        half = h // 2
        return pl.ds(pl.multiple_of(owner * h + k * half, half), half)

    def own(i):
        h = shards[i].shape[0]
        return pltpu.make_async_copy(
            shards[i], fulls[i].at[pl.ds(pl.multiple_of(w * h, h), h)], own_sem.at[i]
        )

    def over_pair(i):
        return pltpu.make_async_remote_copy(
            src_ref=shards[i].at[rows_of(i, 0)] if plan[i] == "core" else shards[i],
            dst_ref=fulls[i] if plan[i] == "swap" else fulls[i].at[rows_of(i, w)],
            send_sem=pair_send.at[i],
            recv_sem=pair_recv.at[i],
            device_id=partner,
            device_id_type=MESH,
        )

    def over_core(i):
        here = fulls[i].at[rows_of(i, 1 - w)]
        return pltpu.make_async_remote_copy(
            src_ref=here,
            dst_ref=here,
            send_sem=core_send.at[i],
            recv_sem=core_recv.at[i],
            device_id=sibling,
            device_id_type=MESH,
        )

    every = range(len(shards))

    def start():
        for i in every:
            over_pair(i).start()
        for i in every:
            if plan[i] != "swap":
                own(i).start()

    def hand_on():
        for i in every:
            over_pair(i).wait_recv()
            if plan[i] == "core":
                over_core(i).start()

    def finish():
        for i in every:
            if plan[i] != "swap":
                own(i).wait()
            over_pair(i).wait_send()
            if plan[i] == "core":
                over_core(i).wait()

    return start, hand_on, finish


def carry_semaphores(count):
    return [pltpu.SemaphoreType.DMA((max(count, 1),)) for _ in range(5)]


def places(results, carry):
    return [VM if kind == "swap" else HBM for (kind, _), _ in zip(carry, results)]


def carried(carry):
    plan, operands, results = [], [], []
    for kind, value in carry:
        parts = value if kind == "join" else [value]
        column = 0
        for v in parts:
            where = column if kind == "join" else None
            plan.append(("whole" if kind == "join" else kind, len(results), where))
            operands.append(v)
            column += v.shape[1]
        rows = parts[0].shape[0] * (1 if kind == "swap" else 2)
        results.append(jax.ShapeDtypeStruct((rows, column), parts[0].dtype))
    return plan, operands, results


def regions_of(values, x_first):
    found = []
    for i, (v, rows) in enumerate(zip(values, x_first)):
        total = v.shape[-2]
        if rows:
            found.append((i, total - rows, rows, True))
        if rows < total:
            found.append((i, 0, total - rows, False))
    return found


def gather_kernel(count, regions, plan, made, *refs):
    ins, shards = refs[:count], refs[count : count + len(plan)]
    refs = refs[count + len(plan) :]
    outs, fulls = refs[:count], refs[count : count + made]
    send_sem, recv_sem, own_sem, *carry_sems = refs[count + made :]
    me, z, x, k, w = place()
    greet(z, x, k, w, made > 0)
    up, down = (slot_of(z + 1, x, k), w), (slot_of(z - 1, x, k), w)
    side, sibling = (slot_of(z, 1 - x, k), w), (slot_of(z, x, 1 - k), w)
    x_first = any(crosses for *_, crosses in regions)

    def copies(route, slot, way, device, first=False):
        for r, (i, row, rows, crosses) in enumerate(regions):
            if route is None or crosses == route:
                here = pl.ds(row, rows)
                yield pltpu.make_async_remote_copy(
                    src_ref=ins[i].at[here] if first else outs[i].at[slot, here],
                    dst_ref=outs[i].at[slot, here],
                    send_sem=send_sem.at[r, slot, way],
                    recv_sem=recv_sem.at[r, slot],
                    device_id=device,
                    device_id_type=MESH,
                )

    def send(*what):
        for c in copies(*what):
            c.start()

    def sent(*what):
        for c in copies(*what):
            c.wait_send()

    def arrived(route, slot):
        for c in copies(route, slot, 0, sibling):
            c.wait_recv()

    def onward(act, route, slot, sign):
        if sign <= 0:

            @pl.when(z < NZ - 1)
            def _():
                act(route, slot, 0, up)

        if sign >= 0:

            @pl.when(z > 0)
            def _():
                act(route, slot, 1, down)

    def across(d, act, wait):
        for sign in (-1, 1) if d else (0,):
            there = z + sign * d

            @pl.when((there >= 0) & (there < NZ))
            def _():
                slot = slot_of(there, 1 - x, k)
                wait(False, slot)
                act(False, slot, 3, sibling)

    def walk(act, wait):
        act(None, me, 2, side, True)

        @pl.when(z < NZ - 1)
        def _():
            act(None, me, 0, up, True)

        @pl.when(z > 0)
        def _():
            act(None, me, 1, down, True)

        act(None, me, 3, sibling, True)
        if x_first:
            slot = slot_of(z, 1 - x, k)
            wait(True, slot)
            onward(act, True, slot, 0)
            act(True, slot, 3, sibling)
        for d in range(1, NZ):
            for sign in (-1, 1):
                there = z + sign * d

                @pl.when((there >= 0) & (there < NZ))
                def _():
                    slot = slot_of(there, x, k)
                    wait(False, slot)
                    if d < NZ - 1:
                        onward(act, False, slot, sign)
                    act(False, slot, 2, side)
                    act(False, slot, 3, sibling)
                    if x_first:
                        for column in (x, 1 - x):
                            slot = slot_of(there, column, k)
                            wait(True, slot)
                            if d < NZ - 1:
                                onward(act, True, slot, sign)
                            act(True, slot, 3, sibling)

            across(d - 1, act, wait)
        across(NZ - 1, act, wait)

    own = [pltpu.make_async_copy(ins[i], outs[i].at[me], own_sem.at[i]) for i in range(count)]
    start, hand_on, finish = carry_steps(plan, shards, fulls, carry_sems, x, z, k, w)
    start()
    walk(send, arrived)
    for o in own:
        o.start()
    hand_on()
    for other in range(NZ * NX):
        arrived(None, other * NK + 1 - k)
    walk(sent, lambda route, slot: None)
    for o in own:
        o.wait()
    finish()


def ctx_gather_kernel(values, carry, number, x_first):
    plan, weights, results = carried(carry)
    regions = regions_of(values, x_first)
    count, made = len(values), len(results)
    n = NZ * NX * NK
    done = pl.pallas_call(
        functools.partial(gather_kernel, count, regions, plan, made),
        out_shape=[jax.ShapeDtypeStruct((n, *v.shape), v.dtype) for v in values] + results,
        in_specs=[VM] * (count + len(weights)),
        out_specs=[HBM] * count + places(results, carry),
        scratch_shapes=[
            pltpu.SemaphoreType.DMA((len(regions), n, 4)),
            pltpu.SemaphoreType.DMA((len(regions), n)),
            pltpu.SemaphoreType.DMA((count,)),
        ]
        + carry_semaphores(len(plan)),
        compiler_params=settings(number, bytes_of([*values, *weights])),
        name=f"gather_{number}",
    )(*values, *weights)
    return done[:count], done[count:]


def scatter_kernel(count, regions, plan, made, *refs):
    ins, shards = refs[:count], refs[count : count + len(plan)]
    refs = refs[count + len(plan) :]
    outs, fulls = refs[:count], refs[count : count + made]
    scratch = refs[count + made :]
    many = len(regions)
    from_core, from_side, to_side, from_low, from_high, to_z = (
        scratch[g * many : (g + 1) * many] for g in range(6)
    )
    send_core, recv_core, send_side, recv_side, send_z, recv_low, recv_high, *carry_sems = scratch[
        6 * many :
    ]
    me, z, x, k, w = place()
    greet(z, x, k, w, made > 0)
    up, down = (slot_of(z + 1, x, k), w), (slot_of(z - 1, x, k), w)
    side, sibling = (slot_of(z, 1 - x, k), w), (slot_of(z, x, 1 - k), w)
    f32 = jnp.float32

    def part(r, zz, xx, core):
        i, row, rows, _ = regions[r]
        return ins[i].at[slot_of(zz, xx, core), pl.ds(row, rows)]

    def core_copy(r, zz, xx):
        pair = zz * NX + xx
        return pltpu.make_async_remote_copy(
            src_ref=part(r, zz, xx, 1 - k),
            dst_ref=from_core[r].at[pair],
            send_sem=send_core.at[r, pair],
            recv_sem=recv_core.at[r, pair],
            device_id=sibling,
            device_id_type=MESH,
        )

    def side_copy(r, at):
        return pltpu.make_async_remote_copy(
            src_ref=to_side[r].at[at],
            dst_ref=from_side[r].at[at],
            send_sem=send_side.at[r, at],
            recv_sem=recv_side.at[r, at],
            device_id=side,
            device_id_type=MESH,
        )

    def z_copy(r, at, low):
        return pltpu.make_async_remote_copy(
            src_ref=to_z[r].at[at],
            dst_ref=(from_low if low else from_high)[r].at[at],
            send_sem=send_z.at[r, at],
            recv_sem=(recv_low if low else recv_high).at[r, at],
            device_id=up if low else down,
            device_id_type=MESH,
        )

    def targets(act, route=None):
        for d in range(NZ - 1, -1, -1):
            for sign in (1, -1) if d else (0,):
                there = z + sign * d

                @pl.when((there >= 0) & (there < NZ))
                def _():
                    for r in range(many):
                        if route is None or regions[r][3] == route:
                            act(r, there, sign)

    start, hand_on, finish = carry_steps(plan, shards, fulls, carry_sems, x, z, k, w)
    start()
    targets(lambda r, zz, sign: core_copy(r, zz, 1 - x).start())
    targets(lambda r, zz, sign: core_copy(r, zz, x).start())

    def chip_sum(r, zz, xx):
        return part(r, zz, xx, k)[...].astype(f32) + from_core[r][zz * NX + xx].astype(f32)

    def cross(r, zz, sign):
        core_copy(r, zz, 1 - x).wait_recv()
        to_side[r][zz] = chip_sum(r, zz, 1 - x).astype(to_side[r].dtype)
        side_copy(r, zz).start()

    targets(cross, False)

    def pass_on(r, at, total, sign):
        low = sign > 0
        came = from_low if low else from_high
        first = (z == 0) if low else (z == NZ - 1)

        @pl.when(first)
        def _():
            to_z[r][at] = total.astype(to_z[r].dtype)

        @pl.when(jnp.logical_not(first))
        def _():
            z_copy(r, at, low).wait_recv()
            to_z[r][at] = (total + came[r][at].astype(f32)).astype(to_z[r].dtype)

        z_copy(r, at, low).start()

    def add_line(r, at, here):
        @pl.when(z > 0)
        def _():
            z_copy(r, at, True).wait_recv()
            here[...] += from_low[r][at].astype(f32)

        @pl.when(z < NZ - 1)
        def _():
            z_copy(r, at, False).wait_recv()
            here[...] += from_high[r][at].astype(f32)

    def along(r, zz, sign):
        i, row, rows, crosses = regions[r]
        here = outs[i].at[pl.ds(row, rows)]
        if not crosses:
            core_copy(r, zz, x).wait_recv()
            side_copy(r, zz).wait_recv()
            total = chip_sum(r, zz, x) + from_side[r][zz].astype(f32)
            if sign:
                pass_on(r, zz, total, sign)
            else:
                here[...] = total
                add_line(r, zz, here)
            return
        for xx in (1 - x, x):
            at = zz * NX + xx
            core_copy(r, zz, xx).wait_recv()
            total = chip_sum(r, zz, xx)
            if sign:
                pass_on(r, at, total, sign)
                continue
            here[...] = total
            add_line(r, at, here)
            if xx is x:
                side_copy(r, 0).wait_recv()
                here[...] += from_side[r][0].astype(f32)
            else:
                to_side[r][0] = here[...].astype(to_side[r].dtype)
                side_copy(r, 0).start()

    targets(along)
    hand_on()

    def settle(r, zz, sign):
        core_copy(r, zz, 1 - x).wait_send()
        core_copy(r, zz, x).wait_send()
        if not regions[r][3]:
            side_copy(r, zz).wait_send()
            if sign:
                z_copy(r, zz, sign > 0).wait_send()
        elif sign:
            z_copy(r, zz * NX, sign > 0).wait_send()
            z_copy(r, zz * NX + 1, sign > 0).wait_send()
        else:
            side_copy(r, 0).wait_send()

    targets(settle)
    finish()


def ctx_scatter_kernel(values, carry, number, x_first):
    plan, weights, results = carried(carry)
    regions = regions_of(values, x_first)
    count, made, many = len(values), len(results), len(regions)
    dma = pltpu.SemaphoreType.DMA
    scratch = []
    for straight, crossing in ((8, 8), (4, 1), (4, 1), (4, 8), (4, 8), (4, 8)):
        scratch += [
            pltpu.VMEM(
                (crossing if crosses else straight, rows, values[i].shape[2]), values[i].dtype
            )
            for i, _, rows, crosses in regions
        ]
    done = pl.pallas_call(
        functools.partial(scatter_kernel, count, regions, plan, made),
        out_shape=[jax.ShapeDtypeStruct(v.shape[1:], jnp.float32) for v in values] + results,
        in_specs=[VM] * (count + len(weights)),
        out_specs=[VM] * count + places(results, carry),
        scratch_shapes=scratch
        + [dma((many, NZ * NX)) for _ in range(7)]
        + carry_semaphores(len(plan)),
        compiler_params=settings(number, 3 * bytes_of(values) + bytes_of(weights)),
        name=f"scatter_{number}",
    )(*values, *weights)
    return done[:count], done[count:]


def planned():
    return lax.axis_size("ctx") == NZ * NX * NK and lax.axis_size("wa") == 2


def wa_gather(carry):
    joined = [jnp.concatenate(v, axis=1) if kind == "join" else v for kind, v in carry]
    return [
        pair_swap(v) if kind == "swap" else lax.all_gather(v, "wa", axis=0, tiled=True)
        for (kind, _), v in zip(carry, joined)
    ]


def ctx_gather(values, carry, number, x_first):
    if planned():
        return ctx_gather_kernel(values, carry, number, x_first)
    return [lax.all_gather(v, "ctx", axis=0) for v in values], wa_gather(carry)


def ctx_scatter_sum(values, carry, number, x_first):
    if planned():
        return ctx_scatter_kernel(values, carry, number, x_first)
    summed = [lax.psum_scatter(v, "ctx", scatter_dimension=0).astype(jnp.float32) for v in values]
    return summed, wa_gather(carry)


def per_device(
    tokens,
    doc_starts,
    routes,
    valid,
    teacher,
    out_grad,
    norm1_gain,
    w_query,
    w_key,
    w_value,
    w_out,
    norm2_gain,
    w_router,
    shared_gate,
    shared_up,
    shared_down,
    expert_gate,
    expert_up,
    expert_down,
):
    ctx_count = lax.axis_size("ctx")
    ctx_rank = lax.axis_index("ctx")
    wa_count = lax.axis_size("wa")
    side = lax.axis_index("wa")
    local_rows = tokens.shape[1]
    seq_len = local_rows * ctx_count
    groups = H // KVH
    kv_width = KVH * HD
    experts = w_router.shape[1]
    width = tokens.shape[2]
    lanes = 128
    shared_half = shared_down.shape[0]
    run = shared_half // ctx_count
    low = jnp.bfloat16

    gain_rows = width // wa_count // lanes
    valid_rows = valid[0].astype(jnp.float32)
    small = jnp.zeros((16, lanes), jnp.float32)
    small = small.at[:gain_rows].set(norm1_gain.astype(jnp.float32).reshape(gain_rows, lanes))
    small = small.at[8 : 8 + gain_rows].set(
        norm2_gain.astype(jnp.float32).reshape(gain_rows, lanes)
    )
    small = small.at[6].set(valid_rows)
    tokens_there = pair_swap(tokens[0])
    small_there = pair_swap(small)
    small_all = jnp.where(
        side == 0, jnp.stack([small, small_there]), jnp.stack([small_there, small])
    )
    gain_one = small_all[:, :gain_rows].reshape(width)
    gain_two = small_all[:, 8 : 8 + gain_rows].reshape(width)
    valid_here = jnp.sum(small_all[:, 6])

    doc_first = doc_starts[0]
    own_rows = ctx_rank * local_rows + jnp.arange(local_rows, dtype=jnp.int32)
    query_pos = stored_position(own_rows, local_rows, ctx_count)
    query_place = jnp.stack([query_pos, document_of(query_pos, doc_first)])
    key_pos = stored_position(jnp.arange(seq_len, dtype=jnp.int32), local_rows, ctx_count)
    key_place = jnp.stack([key_pos, document_of(key_pos, doc_first)], axis=1)

    residual = tokens[0].astype(jnp.float32)
    residual_there = tokens_there.astype(jnp.float32)
    inverse_one = rms_inverse(residual)
    scaled_half = jnp.concatenate(
        [
            my_half(residual * inverse_one, side, 1),
            my_half(residual_there * rms_inverse(residual_there), side, 1),
        ]
    )
    normed_half = (scaled_half * norm1_gain.astype(jnp.float32)).astype(low)
    key_value_part = jnp.concatenate(
        [matmul(normed_half, w_key), matmul(normed_half, w_value)], axis=1
    )
    key_value_there = pair_swap(key_value_part[local_rows:].astype(low))
    key_value_own = (key_value_part[:local_rows] + key_value_there.astype(jnp.float32)).astype(low)
    query_part = matmul(normed_half, w_query)

    def shared_columns(weight):
        return [
            lax.dynamic_slice_in_dim(weight, half * shared_half + ctx_rank * run, run, 1)
            for half in range(wa_count)
        ]

    units = wa_count * run
    blank = jnp.zeros((shared_gate.shape[0], lanes - units), low)
    down_rows = lax.dynamic_slice_in_dim(shared_down, ctx_rank * run, run, 0)
    (key_value_all, valid_all), (
        query_there,
        weight_out,
        router_t,
    ) = ctx_gather(
        [key_value_own, jnp.full((8, lanes), valid_here)],
        [
            ("swap", query_part[local_rows:].astype(low)),
            ("core", w_out),
            ("core", w_router.astype(jnp.float32).T),
        ],
        2,
        [16, 0],
    )
    wide_in = jnp.concatenate(
        [
            expert_gate[0],
            expert_up[0],
            *shared_columns(shared_gate),
            blank,
            *shared_columns(shared_up),
            blank,
        ],
        axis=1,
    )
    wide_in, down, down_rows, key_value_all = lax.optimization_barrier(
        (wide_in, expert_down[0], down_rows, key_value_all)
    )
    down_rows_there = pair_swap(down_rows)
    weight_sdown = jnp.where(
        side == 0,
        jnp.concatenate([down_rows, down_rows_there]),
        jnp.concatenate([down_rows_there, down_rows]),
    )
    weight_sdown = jnp.pad(weight_sdown, ((0, lanes - units), (0, 0)))
    expert_weights = [wide_in, pair_swap(wide_in), down, pair_swap(down), weight_sdown]
    which = jnp.full((1,), side, jnp.int32)
    queries = (query_part[:local_rows] + query_there.astype(jnp.float32)).astype(low)
    key_value_all = key_value_all.reshape(seq_len, 2 * kv_width)
    valid_total = jnp.sum(valid_all[:, 0, 0])
    router_t = router_t.reshape(wa_count, experts, width // wa_count)
    weight_router = jnp.transpose(router_t, (0, 2, 1)).reshape(width, experts).astype(low)
    attn, lse = attend_forward(queries, key_value_all, query_place, key_place)
    attn_low = attn.astype(low)
    hidden_one = residual + matmul(attn_low, weight_out)
    inverse_two = rms_inverse(hidden_one)
    normed_two = (hidden_one * inverse_two * gain_two).astype(low)

    logits = matmul(normed_two, weight_router)
    choose = routes[0][:, :, None] == jnp.arange(experts, dtype=jnp.int32)[None, None, :]
    chosen = jnp.any(choose, axis=1)
    peak = jnp.max(jnp.where(chosen, logits, MASKED_SCORE), axis=1, keepdims=True)
    weights = jnp.where(chosen, jnp.exp(jnp.where(chosen, logits, peak) - peak), 0.0)
    gates = weights / jnp.sum(weights, axis=1, keepdims=True)

    (normed_all, gates_all), _ = ctx_gather([normed_two, gates.T], [], 3, [16, 0])
    normed_all = normed_all.reshape(seq_len, width)
    gate = lax.dynamic_slice_in_dim(gates_all, ctx_rank, 1, 1).reshape(seq_len, 1)
    acts, mixed = expert_forward(which, normed_all, gate, expert_weights)
    (routed,), _ = ctx_scatter_sum(
        [mixed.reshape(ctx_count, local_rows, width)], [], 4, [16]
    )
    produced = hidden_one + routed
    output = produced.astype(low)[None]

    errors = produced - teacher[0].astype(jnp.float32)
    local_error = jnp.sum(valid_rows[:, None] * errors * errors)
    tokens_all = wa_count * seq_len
    grad_out = (
        out_grad[0].astype(jnp.float32)
        + 2.0 * tokens_all / valid_total * valid_rows[:, None] * errors
    )
    (grad_all,), _ = ctx_gather([grad_out.astype(low)], [], 5, [16])
    grad_all = grad_all.reshape(seq_len, width)

    (
        grad_rows,
        gate_dot,
        gate_grad,
        up_grad,
        gate_grad_other,
        up_grad_other,
        down_grad,
        down_grad_other,
        shared_grad,
        sdown_grad,
    ) = expert_backward(which, normed_all, grad_all, acts, gate, expert_weights)
    shared_grad = jnp.concatenate([shared_grad[:units], shared_grad[lanes : lanes + units]])
    sdown_grad = sdown_grad[:units]
    small = jnp.full((ctx_count, experts + 8, local_rows), local_error)
    small = small.at[:, :experts].set(0.0)
    small = lax.dynamic_update_slice(
        small, gate_dot.reshape(ctx_count, 1, local_rows), (0, ctx_rank, 0)
    )
    (grad_back, small), (attn_there, normed_two_there) = ctx_scatter_sum(
        [grad_rows.reshape(ctx_count, local_rows, width), small],
        [
            ("swap", my_half(attn_low, 1 - side, 1)),
            ("swap", my_half(normed_two, 1 - side, 1)),
        ],
        6,
        [16, 0],
    )
    grad_gates = small[:experts].T
    error_total = small[experts, 0]
    grad_logits = (
        gates * (grad_gates - jnp.sum(gates * grad_gates, axis=1, keepdims=True))
    ).astype(low)
    grad_normed = grad_back + contract_cols(grad_logits, weight_router)

    def for_pair(full):
        return ("swap", my_half(full, 1 - side, 0).astype(low))

    def with_pair(full, other):
        return my_half(full, side, 0) + other.astype(jnp.float32)

    grad_hidden_norm, grad_gain_two = norm_backward(hidden_one, inverse_two, gain_two, grad_normed)
    grad_hidden_one = grad_out + grad_hidden_norm
    grad_attn_in = grad_hidden_one.astype(low)
    grad_heads = contract_cols(grad_attn_in, weight_out).astype(low)
    delta = jnp.einsum(
        "tagd,tagd->agt",
        grad_heads.astype(jnp.float32).reshape(local_rows, KVH, groups, HD),
        attn.reshape(local_rows, KVH, groups, HD),
    ).reshape(KVH, 1, groups * local_rows)
    grad_query, grad_keys, grad_values = attend_grads(
        queries, grad_heads, key_value_all, lse, delta, query_place, key_place
    )
    def for_all(vector):
        flat = jnp.zeros((16 * lanes,), jnp.float32).at[: vector.shape[0]].set(vector)
        return jnp.broadcast_to(flat.reshape(16, lanes), (ctx_count, 16, lanes))

    def from_all(summed, size):
        return summed.reshape(16 * lanes)[:size]

    def by_slot(value):
        return value.reshape(ctx_count, value.shape[0] // ctx_count, value.shape[1])

    half_width = width // wa_count
    (grad_key, grad_value, small), (
        da_there,
        logits_there,
        query_grad_there,
        error_there,
        shared_there,
        sdown_there,
    ) = ctx_scatter_sum(
        [
            grad_keys.reshape(ctx_count, local_rows, kv_width),
            grad_values.reshape(ctx_count, local_rows, kv_width),
            for_all(grad_gain_two),
        ],
        [
            ("swap", grad_attn_in),
            ("swap", grad_logits),
            ("swap", grad_query),
            ("swap", jnp.full((8, lanes), error_total)),
            ("swap", my_half(shared_grad, 1 - side, 1).astype(low)),
            for_pair(sdown_grad),
        ],
        7,
        [16, 16, 0],
    )
    error_total = error_total + error_there[0, 0]
    key_value_low = jnp.concatenate([grad_key, grad_value], axis=1).astype(low)
    gain_two_sum = from_all(small, width)

    def weight_grad(mine, right, theirs, right_there):
        mine = my_half(mine, side, 1)
        return (contract_rows(mine, right) + contract_rows(theirs, right_there)).astype(low)

    out_part = weight_grad(attn_low, grad_attn_in, attn_there, da_there)
    router_part = contract_rows(grad_logits, my_half(normed_two, side, 1)) + contract_rows(
        logits_there, normed_two_there
    )
    shared_part = my_half(shared_grad, side, 1) + shared_there.astype(jnp.float32)
    sdown_part = with_pair(sdown_grad, sdown_there).astype(low)
    rows_two = jnp.zeros((16, lanes), jnp.float32)
    rows_two = rows_two.at[: half_width // lanes].set(
        my_half(gain_two_sum, 1 - side, 0).reshape(-1, lanes)
    )
    router_rows = router_part.reshape(experts, half_width // lanes, lanes)
    router_rows = jnp.pad(router_rows, ((0, 0), (0, 8 - half_width // lanes), (0, 0)))
    (out_sum, router_sum), (kv_grad_there, rows_there, down_there) = ctx_scatter_sum(
        [by_slot(out_part), router_rows],
        [("swap", key_value_low), ("swap", rows_two), ("swap", down_grad_other)],
        8,
        [0, 0],
    )
    total_gain_two = my_half(gain_two_sum, side, 0) + rows_there.reshape(-1)[:half_width]

    query_both = jnp.concatenate([grad_query, query_grad_there])
    kv_both = jnp.concatenate([key_value_low, kv_grad_there])
    normed_grad = (
        contract_cols(query_both, w_query)
        + contract_cols(kv_both[:, :kv_width], w_key)
        + contract_cols(kv_both[:, kv_width:], w_value)
    )
    (query_sum, kv_sum, small), (normed_grad_there, gate_there) = ctx_scatter_sum(
        [
            by_slot(contract_rows(normed_half, query_both).astype(low)),
            by_slot(contract_rows(normed_half, kv_both).astype(low)),
            for_all(jnp.sum(normed_grad * scaled_half, axis=0)),
        ],
        [
            ("swap", normed_grad[local_rows:].astype(low)),
            ("swap", gate_grad_other),
        ],
        9,
        [0, 16, 0],
    )
    total_gain_one = from_all(small, half_width)
    low_half, high_half = normed_grad[:local_rows], normed_grad_there.astype(jnp.float32)
    grad_normed_one = jnp.where(
        side == 0,
        jnp.concatenate([low_half, high_half], axis=1),
        jnp.concatenate([high_half, low_half], axis=1),
    )
    grad_residual_norm, _ = norm_backward(residual, inverse_one, gain_one, grad_normed_one)
    grad_input = grad_hidden_one + grad_residual_norm
    (total_query, total_kv, total_out, router_sum, shared_parts, sdown_parts), (up_there,) = ctx_gather(
        [
            query_sum.astype(low),
            kv_sum.astype(low),
            out_sum.astype(low),
            router_sum,
            shared_part.astype(low),
            sdown_part,
        ],
        [("swap", up_grad_other)],
        10,
        [0, 0, 0, 0, 0, sdown_part.shape[0]],
    )
    total_query = total_query.reshape(half_width, width).astype(jnp.float32)
    total_kv = total_kv.reshape(half_width, 2 * kv_width).astype(jnp.float32)
    total_out = total_out.reshape(half_width, width).astype(jnp.float32)
    router_sum = router_sum[:, : half_width // lanes].reshape(experts, half_width)
    row = jnp.arange(ctx_count * units, dtype=jnp.int32)[:, None]
    half, unit = row % units // run, row % run
    column = half * shared_half + row // units * run + unit
    select = (column == jnp.arange(ctx_count * units, dtype=jnp.int32)[None, :]).astype(low)
    total_sgate, total_sup = [
        contract_rows(
            shared_parts[:, first : first + units].reshape(ctx_count * units, half_width), select
        )
        for first in (0, units)
    ]
    down_grad = down_grad + down_there.astype(jnp.float32)
    return (
        error_total / (valid_total * width),
        output,
        grad_input[None],
        total_gain_one,
        total_query,
        total_kv[:, :kv_width],
        total_kv[:, kv_width:],
        total_out,
        total_gain_two,
        router_sum.T,
        total_sgate,
        total_sup,
        sdown_parts.reshape(shared_half, width).astype(jnp.float32),
        (gate_grad + gate_there.astype(jnp.float32))[None],
        (up_grad + up_there.astype(jnp.float32))[None],
        down_grad[None],
    )


def solution(mesh):
    return jax.shard_map(
        per_device,
        mesh=mesh,
        in_specs=(
            P("wa", "ctx", None),
            P("wa", None),
            P("wa", "ctx", None),
            P("wa", "ctx"),
            P("wa", "ctx", None),
            P("wa", "ctx", None),
            P("wa"),
            P("wa", None),
            P("wa", None),
            P("wa", None),
            P("wa", None),
            P("wa"),
            P("wa", None),
            P("wa", None),
            P("wa", None),
            P("wa", None),
            P("ctx", "wa", None),
            P("ctx", "wa", None),
            P("ctx", "wa", None),
        ),
        out_specs=(
            P(),
            P("wa", "ctx", None),
            P("wa", "ctx", None),
            P("wa"),
            P("wa", None),
            P("wa", None),
            P("wa", None),
            P("wa", None),
            P("wa"),
            P("wa", None),
            P("wa", None),
            P("wa", None),
            P("wa", None),
            P("ctx", "wa", None),
            P("ctx", "wa", None),
            P("ctx", "wa", None),
        ),
        check_vma=False,
    )
```

```python
import functools

import jax
import jax.numpy as jnp
from jax import lax
from jax.experimental import pallas as pl
from jax.experimental.pallas import tpu as pltpu
from jax.sharding import PartitionSpec as P

H = 12
KVH = 4
HD = 128
EPSILON = 1e-05
MASKED_SCORE = -1e30


def stored_position(stored_rows, local_rows, ctx_count):
    half_rows = local_rows // 2
    owner_rank = stored_rows // local_rows
    within_rows = stored_rows % local_rows
    first_half = owner_rank * half_rows + within_rows
    second_half = (2 * ctx_count - 1 - owner_rank) * half_rows + within_rows - half_rows
    return jnp.where(within_rows < half_rows, first_half, second_half)


def document_of(positions, doc_first):
    return jnp.sum((doc_first[None, :] <= positions[:, None]).astype(jnp.int32), axis=1) - 1


def matmul(left, right):
    return jnp.dot(left, right, preferred_element_type=jnp.float32)


def contract_rows(left, right):
    return lax.dot_general(
        left, right, (((0,), (0,)), ((), ())), preferred_element_type=jnp.float32
    )


def contract_cols(left, right):
    return lax.dot_general(
        left, right, (((1,), (1,)), ((), ())), preferred_element_type=jnp.float32
    )


def rms_inverse(values):
    return lax.rsqrt(jnp.mean(values * values, axis=1, keepdims=True) + EPSILON)


def norm_backward(values, inverse, gain, grad_normed):
    scaled = grad_normed * gain
    inner_sum = jnp.sum(scaled * values, axis=1, keepdims=True)
    grad_values = (
        inverse * scaled - values * (inverse * inverse * inverse) * inner_sum / values.shape[1]
    )
    grad_gain = jnp.sum(grad_normed * values * inverse, axis=0)
    return (grad_values, grad_gain)


def pair_swap(value):
    return lax.ppermute(value, "wa", [(0, 1), (1, 0)])


def my_half(value, side, axis):
    size = value.shape[axis] // 2
    return lax.dynamic_slice_in_dim(value, side * size, size, axis)


def heads_as_rows(value):
    return jnp.concatenate(
        [value[:, h * HD : (h + 1) * HD] for h in range(value.shape[1] // HD)], axis=0
    )


def rows_as_heads(value, rows):
    return jnp.concatenate(
        [value[h * rows : (h + 1) * rows] for h in range(value.shape[0] // rows)], axis=1
    )


def seen(query_ref, key_ref, first, count, groups):
    key_pos, key_doc = key_ref[pl.ds(first, count), 0:1], key_ref[pl.ds(first, count), 1:2]
    query_pos, query_doc = query_ref[0:1, :], query_ref[1:2, :]
    visible = (key_pos <= query_pos) & (key_doc == query_doc)
    return jnp.concatenate([visible.astype(jnp.float32)] * groups, axis=1) > 0.5


def attend_kernel(block, query_ref, key_ref, value_ref, query_place, key_place, out_ref, lse_ref):
    rows = query_ref.shape[0]
    groups = query_ref.shape[1] // HD
    scale = HD ** (-0.5)
    queries = heads_as_rows(query_ref[...])

    def step(index, carry):
        peak, total, mixed = carry
        first = pl.multiple_of(index * block, block)
        scores = contract_cols(key_ref[pl.ds(first, block), :], queries) * scale
        visible = seen(query_place, key_place, first, block, groups)
        scores = jnp.where(visible, scores, MASKED_SCORE)
        new_peak = jnp.maximum(peak, jnp.max(scores, axis=0, keepdims=True))
        shrink = jnp.exp(peak - new_peak)
        weights = jnp.where(visible, jnp.exp(scores - new_peak), 0.0)
        total = total * shrink + jnp.sum(weights, axis=0, keepdims=True)
        part = contract_rows(value_ref[pl.ds(first, block), :], weights.astype(jnp.bfloat16))
        return new_peak, total, mixed * shrink + part

    width = groups * rows
    initial = (
        jnp.full((1, width), MASKED_SCORE, jnp.float32),
        jnp.zeros((1, width), jnp.float32),
        jnp.zeros((HD, width), jnp.float32),
    )
    peak, total, mixed = lax.fori_loop(0, key_ref.shape[0] // block, step, initial)
    out_ref[...] = rows_as_heads((mixed / total).T, rows)
    lse_ref[0] = peak + jnp.log(total)


def attend_grads_kernel(
    block,
    query_ref,
    grad_ref,
    key_ref,
    value_ref,
    lse_ref,
    delta_ref,
    query_place,
    key_place,
    query_grad_ref,
    key_grad_ref,
    value_grad_ref,
):
    rows = query_ref.shape[0]
    groups = query_ref.shape[1] // HD
    scale = HD ** (-0.5)
    queries = heads_as_rows(query_ref[...])
    grads = heads_as_rows(grad_ref[...])
    lse, delta = lse_ref[0], delta_ref[0]

    def step(index, total):
        first = pl.multiple_of(index * block, block)
        here = pl.ds(first, block)
        keys = key_ref[here, :]
        scores = contract_cols(keys, queries) * scale
        visible = seen(query_place, key_place, first, block, groups)
        probs = jnp.where(visible, jnp.exp(jnp.where(visible, scores, MASKED_SCORE) - lse), 0.0)
        grad_probs = contract_cols(value_ref[here, :], grads)
        grad_scores = (probs * (grad_probs - delta)).astype(jnp.bfloat16)
        key_grad_ref[here, :] = (matmul(grad_scores, queries) * scale).astype(jnp.bfloat16)
        value_grad_ref[here, :] = matmul(probs.astype(jnp.bfloat16), grads).astype(jnp.bfloat16)
        return total + contract_rows(keys, grad_scores)

    total = lax.fori_loop(
        0, key_ref.shape[0] // block, step, jnp.zeros((HD, groups * rows), jnp.float32)
    )
    query_grad_ref[...] = rows_as_heads((total * scale).T, rows).astype(jnp.bfloat16)


def attention_specs(rows, seq_len):
    wide = HD * (H // KVH)
    return dict(
        query=pl.BlockSpec((rows, wide), lambda a: (0, a)),
        key=pl.BlockSpec((seq_len, HD), lambda a: (0, a)),
        value=pl.BlockSpec((seq_len, HD), lambda a: (0, KVH + a)),
        row=pl.BlockSpec((1, 1, rows * (H // KVH)), lambda a: (a, 0, 0)),
        query_place=pl.BlockSpec((2, rows), lambda a: (0, 0)),
        key_place=pl.BlockSpec((seq_len, 2), lambda a: (0, 0)),
    )


def attend_forward(queries, key_value_all, query_place, key_place):
    rows, seq_len = queries.shape[0], key_value_all.shape[0]
    s = attention_specs(rows, seq_len)
    return pl.pallas_call(
        functools.partial(attend_kernel, min(seq_len, 1024)),
        grid=(KVH,),
        out_shape=[
            jax.ShapeDtypeStruct((rows, H * HD), jnp.float32),
            jax.ShapeDtypeStruct((KVH, 1, rows * (H // KVH)), jnp.float32),
        ],
        in_specs=[s["query"], s["key"], s["value"], s["query_place"], s["key_place"]],
        out_specs=[s["query"], s["row"]],
        compiler_params=pltpu.CompilerParams(vmem_limit_bytes=20 * 2**20),
        name="attend",
    )(queries, key_value_all, key_value_all, query_place, key_place)


def attend_grads(queries, grads, key_value_all, lse, delta, query_place, key_place):
    rows, seq_len = queries.shape[0], key_value_all.shape[0]
    s = attention_specs(rows, seq_len)
    return pl.pallas_call(
        functools.partial(attend_grads_kernel, min(seq_len, 1024)),
        grid=(KVH,),
        out_shape=[
            jax.ShapeDtypeStruct((rows, H * HD), jnp.bfloat16),
            jax.ShapeDtypeStruct((seq_len, KVH * HD), jnp.bfloat16),
            jax.ShapeDtypeStruct((seq_len, KVH * HD), jnp.bfloat16),
        ],
        in_specs=[
            s["query"],
            s["query"],
            s["key"],
            s["value"],
            s["row"],
            s["row"],
            s["query_place"],
            s["key_place"],
        ],
        out_specs=[s["query"], s["key"], s["key"]],
        compiler_params=pltpu.CompilerParams(vmem_limit_bytes=32 * 2**20),
        name="attend_grads",
    )(queries, grads, key_value_all, key_value_all, lse, delta, query_place, key_place)

def expert_forward_kernel(
    side_ref, rows_ref, gate_ref, own_in, other_in, own_down, other_down, sdown, acts_ref, mixed_ref
):
    side = side_ref[0]
    hidden, depth = own_down.shape[0] * 2, own_in.shape[0]
    pad = sdown.shape[0]

    def half(size, which):
        return pl.ds(pl.multiple_of(which * size, size), size)

    acts_ref[...] = matmul(rows_ref[:, half(depth, side)], own_in[...]) + matmul(
        rows_ref[:, half(depth, 1 - side)], other_in[...]
    )
    gate_act, up_act = acts_ref[:, :hidden], acts_ref[:, hidden : 2 * hidden]
    hidden_exp = (gate_act * jax.nn.sigmoid(gate_act) * up_act).astype(jnp.bfloat16)
    shared_gact = acts_ref[:, 2 * hidden : 2 * hidden + pad]
    shared_uact = acts_ref[:, 2 * hidden + pad :]
    shared_hidden = (shared_gact * jax.nn.sigmoid(shared_gact) * shared_uact).astype(jnp.bfloat16)
    first, second = hidden_exp[:, : hidden // 2], hidden_exp[:, hidden // 2 :]
    swap = side == 1
    out = matmul(jnp.where(swap, second, first), own_down[...]) + matmul(
        jnp.where(swap, first, second), other_down[...]
    )
    mixed = gate_ref[...] * out.astype(jnp.bfloat16).astype(jnp.float32)
    mixed_ref[...] = (mixed + matmul(shared_hidden, sdown[...])).astype(jnp.bfloat16)


def expert_backward_kernel(
    side_ref,
    rows_ref,
    grad_ref,
    acts_ref,
    gate_ref,
    own_in,
    other_in,
    own_down,
    other_down,
    sdown,
    grad_rows_ref,
    dots_ref,
    gate_own,
    up_own,
    gate_other,
    up_other,
    down_own,
    down_other,
    shared_out,
    sdown_out,
    acts_grad,
    in_total,
    down_total,
    shared_total,
    sdown_total,
):
    low = jnp.bfloat16
    side = side_ref[0]
    hidden, depth = own_down.shape[0] * 2, own_in.shape[0]
    pad = sdown.shape[0]

    def half(size, which):
        return pl.ds(pl.multiple_of(which * size, size), size)

    @pl.when(pl.program_id(0) == 0)
    def _():
        for total in (in_total, down_total, shared_total, sdown_total):
            total[...] = jnp.zeros_like(total)

    rows, grads, gate = rows_ref[...], grad_ref[...], gate_ref[...]
    ours, theirs = contract_cols(grads, own_down[...]), contract_cols(grads, other_down[...])
    swap = side == 1
    grad_hidden = jnp.concatenate(
        [jnp.where(swap, theirs, ours), jnp.where(swap, ours, theirs)], axis=1
    )

    def through(grad, gate_act, up_act, at):
        sigmoid = jax.nn.sigmoid(gate_act)
        silu = gate_act * sigmoid
        width = gate_act.shape[1]
        grad_gate = grad * up_act * sigmoid * (1.0 + gate_act * (1.0 - sigmoid))
        acts_grad[:, at : at + width] = grad_gate.astype(low)
        acts_grad[:, at + width : at + 2 * width] = (grad * silu).astype(low)
        return (silu * up_act).astype(low)

    hidden_exp = through(
        gate * grad_hidden, acts_ref[:, :hidden], acts_ref[:, hidden : 2 * hidden], 0
    )
    shared_hidden = through(
        contract_cols(grads, sdown[...]),
        acts_ref[:, 2 * hidden : 2 * hidden + pad],
        acts_ref[:, 2 * hidden + pad :],
        2 * hidden,
    )
    dots_ref[...] = jnp.sum(grad_hidden * hidden_exp.astype(jnp.float32), axis=1, keepdims=True)
    grad_rows_ref[:, half(depth, side)] = contract_cols(acts_grad[...], own_in[...]).astype(low)
    grad_rows_ref[:, half(depth, 1 - side)] = contract_cols(acts_grad[...], other_in[...]).astype(
        low
    )
    in_total[...] += contract_rows(rows, acts_grad[:, : 2 * hidden])
    shared_total[...] += contract_rows(acts_grad[:, 2 * hidden :], rows)
    picked = (gate * grads.astype(jnp.float32)).astype(low)
    down_total[...] += contract_rows(hidden_exp, picked)
    sdown_total[...] += contract_rows(shared_hidden, grads)

    @pl.when(pl.program_id(0) == pl.num_programs(0) - 1)
    def _():
        mine, other = half(depth, side), half(depth, 1 - side)
        gate_own[...] = in_total[mine, :hidden]
        up_own[...] = in_total[mine, hidden:]
        gate_other[...] = in_total[other, :hidden].astype(low)
        up_other[...] = in_total[other, hidden:].astype(low)
        down_own[...] = down_total[half(hidden // 2, side), :]
        down_other[...] = down_total[half(hidden // 2, 1 - side), :].astype(low)
        shared_out[...] = shared_total[...]
        sdown_out[...] = sdown_total[...]


def whole(value):
    return pl.BlockSpec(value.shape, lambda i: (0,) * len(value.shape))


def by_rows(block, columns):
    return pl.BlockSpec((block, columns), lambda i: (i, 0))


def expert_forward(side, rows, gate, weights):
    total, width = rows.shape
    block, acts = min(total, 256), weights[0].shape[1]
    return pl.pallas_call(
        expert_forward_kernel,
        grid=(total // block,),
        out_shape=[
            jax.ShapeDtypeStruct((total, acts), jnp.float32),
            jax.ShapeDtypeStruct((total, width), jnp.bfloat16),
        ],
        in_specs=[
            pl.BlockSpec(memory_space=pltpu.SMEM),
            by_rows(block, width),
            by_rows(block, 1),
            *map(whole, weights),
        ],
        out_specs=[by_rows(block, acts), by_rows(block, width)],
        compiler_params=pltpu.CompilerParams(vmem_limit_bytes=32 * 2**20),
        name="expert_forward",
    )(side, rows, gate, *weights)


def expert_backward(side, rows, grads, acts, gate, weights):
    total, width = rows.shape
    block, columns = min(total, 256), weights[0].shape[1]
    depth, hidden = weights[0].shape[0], 2 * weights[2].shape[0]
    pad = weights[4].shape[0]
    shape, f32, low = jax.ShapeDtypeStruct, jnp.float32, jnp.bfloat16
    ends = [
        shape((depth, hidden), f32),
        shape((depth, hidden), f32),
        shape((depth, hidden), low),
        shape((depth, hidden), low),
        shape((hidden // 2, width), f32),
        shape((hidden // 2, width), low),
        shape((2 * pad, width), f32),
        shape((pad, width), f32),
    ]
    return pl.pallas_call(
        expert_backward_kernel,
        grid=(total // block,),
        out_shape=[shape((total, width), low), shape((total, 1), f32), *ends],
        in_specs=[
            pl.BlockSpec(memory_space=pltpu.SMEM),
            by_rows(block, width),
            by_rows(block, width),
            by_rows(block, columns),
            by_rows(block, 1),
            *map(whole, weights),
        ],
        out_specs=[by_rows(block, width), by_rows(block, 1), *map(whole, ends)],
        scratch_shapes=[
            pltpu.VMEM((block, columns), low),
            pltpu.VMEM((width, 2 * hidden), f32),
            pltpu.VMEM((hidden, width), f32),
            pltpu.VMEM((2 * pad, width), f32),
            pltpu.VMEM((pad, width), f32),
        ],
        compiler_params=pltpu.CompilerParams(vmem_limit_bytes=60 * 2**20),
        name="expert_backward",
    )(side, rows, grads, acts, gate, *weights)


MESH = pl.DeviceIdType.MESH
NZ, NX, NK = 4, 2, 2
PIECE = 200_000
VM = pl.BlockSpec(memory_space=pltpu.VMEM)
HBM = pl.BlockSpec(memory_space=pl.ANY)


def settings(number, held):
    return pltpu.CompilerParams(
        collective_id=number, has_side_effects=True, vmem_limit_bytes=held + 4 * 2**20
    )


def bytes_of(arrays):
    return sum(v.size * v.dtype.itemsize for v in arrays)


def slot_of(z, x, k):
    return (z * NX + x) * NK + k


def place():
    c = lax.axis_index("ctx")
    return c, c // (NX * NK), lax.rem(c // NK, NX), lax.rem(c, NK), lax.axis_index("wa")


def greet(z, x, k, w, pair, plane=True):
    barrier = pltpu.get_barrier_semaphore()

    def hello(device):
        pl.semaphore_signal(barrier, inc=1, device_id=device, device_id_type=MESH)

    hello((slot_of(z, x, 1 - k), w))
    count = 1
    if pair:
        hello((slot_of(z, x, k), 1 - w))
        count += 1
    if plane:
        hello((slot_of(z, 1 - x, k), w))
        count += 1

        @pl.when(z > 0)
        def _():
            hello((slot_of(z - 1, x, k), w))

        @pl.when(z < NZ - 1)
        def _():
            hello((slot_of(z + 1, x, k), w))

        count += jnp.where(z > 0, 1, 0) + jnp.where(z < NZ - 1, 1, 0)
    pl.semaphore_wait(barrier, count)


def carry_steps(plan, shards, targets, sems, x, z, k, w):
    own_sem, pair_send, pair_recv, core_send, core_recv = sems
    partner, sibling = (slot_of(z, x, k), 1 - w), (slot_of(z, x, 1 - k), w)
    plan, outs, columns = zip(*plan) if plan else ((), (), ())
    fulls = [
        targets[o] if c is None else targets[o].at[:, pl.ds(c, shards[i].shape[1])]
        for i, (o, c) in enumerate(zip(outs, columns))
    ]

    def rows_of(i, owner):
        h = shards[i].shape[0]
        if plan[i] == "whole":
            return pl.ds(pl.multiple_of(owner * h, h), h)
        half = h // 2
        return pl.ds(pl.multiple_of(owner * h + k * half, half), half)

    def own(i):
        h = shards[i].shape[0]
        return pltpu.make_async_copy(
            shards[i], fulls[i].at[pl.ds(pl.multiple_of(w * h, h), h)], own_sem.at[i]
        )

    def over_pair(i):
        return pltpu.make_async_remote_copy(
            src_ref=shards[i].at[rows_of(i, 0)] if plan[i] == "core" else shards[i],
            dst_ref=fulls[i] if plan[i] == "swap" else fulls[i].at[rows_of(i, w)],
            send_sem=pair_send.at[i],
            recv_sem=pair_recv.at[i],
            device_id=partner,
            device_id_type=MESH,
        )

    def over_core(i):
        here = fulls[i].at[rows_of(i, 1 - w)]
        return pltpu.make_async_remote_copy(
            src_ref=here,
            dst_ref=here,
            send_sem=core_send.at[i],
            recv_sem=core_recv.at[i],
            device_id=sibling,
            device_id_type=MESH,
        )

    every = range(len(shards))

    def start():
        for i in every:
            over_pair(i).start()
        for i in every:
            if plan[i] != "swap":
                own(i).start()

    def hand_on():
        for i in every:
            over_pair(i).wait_recv()
            if plan[i] == "core":
                over_core(i).start()

    def finish():
        for i in every:
            if plan[i] != "swap":
                own(i).wait()
            over_pair(i).wait_send()
            if plan[i] == "core":
                over_core(i).wait()

    return start, hand_on, finish


def carry_semaphores(count):
    return [pltpu.SemaphoreType.DMA((max(count, 1),)) for _ in range(5)]


def places(results, carry):
    return [VM if kind == "swap" else HBM for (kind, _), _ in zip(carry, results)]


def carried(carry):
    plan, operands, results = [], [], []
    for kind, value in carry:
        parts = value if kind == "join" else [value]
        column = 0
        for v in parts:
            where = column if kind == "join" else None
            plan.append(("whole" if kind == "join" else kind, len(results), where))
            operands.append(v)
            column += v.shape[1]
        rows = parts[0].shape[0] * (1 if kind == "swap" else 2)
        results.append(jax.ShapeDtypeStruct((rows, column), parts[0].dtype))
    return plan, operands, results


def regions_of(values, x_first):
    found = []
    for i, (v, rows) in enumerate(zip(values, x_first)):
        total = v.shape[-2]
        if rows:
            found.append((i, total - rows, rows, True))
        straight = total - rows
        parts = max(1, -(-straight * v.shape[-1] * v.dtype.itemsize // PIECE))
        step = -(-straight // parts // 16) * 16 if parts > 1 else max(straight, 1)
        for first in range(0, straight, step):
            found.append((i, first, min(step, straight - first), False))
    return found


def gather_kernel(count, regions, plan, made, *refs):
    ins, shards = refs[:count], refs[count : count + len(plan)]
    refs = refs[count + len(plan) :]
    outs, fulls = refs[:count], refs[count : count + made]
    send_sem, recv_sem, own_sem, *carry_sems = refs[count + made :]
    me, z, x, k, w = place()
    greet(z, x, k, w, made > 0)
    up, down = (slot_of(z + 1, x, k), w), (slot_of(z - 1, x, k), w)
    side, sibling = (slot_of(z, 1 - x, k), w), (slot_of(z, x, 1 - k), w)

    every = range(len(regions))
    straight = [r for r in every if not regions[r][3]]
    crossing = [r for r in every if regions[r][3]]

    def copy(r, slot, way, device, first=False):
        i, row, rows, _ = regions[r]
        here = pl.ds(row, rows)
        return pltpu.make_async_remote_copy(
            src_ref=ins[i].at[here] if first else outs[i].at[slot, here],
            dst_ref=outs[i].at[slot, here],
            send_sem=send_sem.at[r, slot, way],
            recv_sem=recv_sem.at[r, slot],
            device_id=device,
            device_id_type=MESH,
        )

    def send(*what):
        copy(*what).start()

    def sent(*what):
        copy(*what).wait_send()

    def arrived(r, slot):
        copy(r, slot, 0, sibling).wait_recv()

    def onward(act, r, slot, sign):
        if sign <= 0:

            @pl.when(z < NZ - 1)
            def _():
                act(r, slot, 0, up)

        if sign >= 0:

            @pl.when(z > 0)
            def _():
                act(r, slot, 1, down)

    def across(d, act, wait):
        for sign in (-1, 1) if d else (0,):
            there = z + sign * d

            @pl.when((there >= 0) & (there < NZ))
            def _():
                slot = slot_of(there, 1 - x, k)
                for r in straight:
                    wait(r, slot)
                    act(r, slot, 3, sibling)

    def walk(act, wait):
        for r in every:
            act(r, me, 2, side, True)

        @pl.when(z < NZ - 1)
        def _():
            for r in every:
                act(r, me, 0, up, True)

        @pl.when(z > 0)
        def _():
            for r in every:
                act(r, me, 1, down, True)

        for r in every:
            act(r, me, 3, sibling, True)
        slot = slot_of(z, 1 - x, k)
        for r in crossing:
            wait(r, slot)
            onward(act, r, slot, 0)
            act(r, slot, 3, sibling)
        for d in range(1, NZ):
            for sign in (-1, 1):
                there = z + sign * d

                @pl.when((there >= 0) & (there < NZ))
                def _():
                    slot = slot_of(there, x, k)
                    for r in straight:
                        wait(r, slot)
                        if d < NZ - 1:
                            onward(act, r, slot, sign)
                        act(r, slot, 2, side)
                        act(r, slot, 3, sibling)
                    for r in crossing:
                        for column in (x, 1 - x):
                            slot = slot_of(there, column, k)
                            wait(r, slot)
                            if d < NZ - 1:
                                onward(act, r, slot, sign)
                            act(r, slot, 3, sibling)

            across(d - 1, act, wait)
        across(NZ - 1, act, wait)

    own = [pltpu.make_async_copy(ins[i], outs[i].at[me], own_sem.at[i]) for i in range(count)]
    start, hand_on, finish = carry_steps(plan, shards, fulls, carry_sems, x, z, k, w)
    start()
    walk(send, arrived)
    for o in own:
        o.start()
    hand_on()
    for other in range(NZ * NX):
        for r in every:
            arrived(r, other * NK + 1 - k)
    walk(sent, lambda r, slot: None)
    for o in own:
        o.wait()
    finish()


def ctx_gather_kernel(values, carry, number, x_first):
    plan, weights, results = carried(carry)
    regions = regions_of(values, x_first)
    count, made = len(values), len(results)
    n = NZ * NX * NK
    done = pl.pallas_call(
        functools.partial(gather_kernel, count, regions, plan, made),
        out_shape=[jax.ShapeDtypeStruct((n, *v.shape), v.dtype) for v in values] + results,
        in_specs=[VM] * (count + len(weights)),
        out_specs=[HBM] * count + places(results, carry),
        scratch_shapes=[
            pltpu.SemaphoreType.DMA((len(regions), n, 4)),
            pltpu.SemaphoreType.DMA((len(regions), n)),
            pltpu.SemaphoreType.DMA((count,)),
        ]
        + carry_semaphores(len(plan)),
        compiler_params=settings(number, bytes_of([*values, *weights])),
        name=f"gather_{number}",
    )(*values, *weights)
    return done[:count], done[count:]


def scatter_kernel(count, regions, plan, made, *refs):
    ins, shards = refs[:count], refs[count : count + len(plan)]
    refs = refs[count + len(plan) :]
    outs, fulls = refs[:count], refs[count : count + made]
    scratch = refs[count + made :]
    many = len(regions)
    from_core, from_side, to_side, from_low, from_high, to_z = (
        scratch[g * many : (g + 1) * many] for g in range(6)
    )
    send_core, recv_core, send_side, recv_side, send_z, recv_low, recv_high, *carry_sems = scratch[
        6 * many :
    ]
    me, z, x, k, w = place()
    greet(z, x, k, w, made > 0)
    up, down = (slot_of(z + 1, x, k), w), (slot_of(z - 1, x, k), w)
    side, sibling = (slot_of(z, 1 - x, k), w), (slot_of(z, x, 1 - k), w)
    f32 = jnp.float32

    def part(r, zz, xx, core):
        i, row, rows, _ = regions[r]
        return ins[i].at[slot_of(zz, xx, core), pl.ds(row, rows)]

    def core_copy(r, zz, xx):
        pair = zz * NX + xx
        return pltpu.make_async_remote_copy(
            src_ref=part(r, zz, xx, 1 - k),
            dst_ref=from_core[r].at[pair],
            send_sem=send_core.at[r, pair],
            recv_sem=recv_core.at[r, pair],
            device_id=sibling,
            device_id_type=MESH,
        )

    def side_copy(r, at):
        return pltpu.make_async_remote_copy(
            src_ref=to_side[r].at[at],
            dst_ref=from_side[r].at[at],
            send_sem=send_side.at[r, at],
            recv_sem=recv_side.at[r, at],
            device_id=side,
            device_id_type=MESH,
        )

    def z_copy(r, at, low):
        return pltpu.make_async_remote_copy(
            src_ref=to_z[r].at[at],
            dst_ref=(from_low if low else from_high)[r].at[at],
            send_sem=send_z.at[r, at],
            recv_sem=(recv_low if low else recv_high).at[r, at],
            device_id=up if low else down,
            device_id_type=MESH,
        )

    def targets(act, route=None):
        for d in range(NZ - 1, -1, -1):
            for sign in (1, -1) if d else (0,):
                there = z + sign * d

                @pl.when((there >= 0) & (there < NZ))
                def _():
                    for r in range(many):
                        if route is None or regions[r][3] == route:
                            act(r, there, sign)

    start, hand_on, finish = carry_steps(plan, shards, fulls, carry_sems, x, z, k, w)
    start()
    targets(lambda r, zz, sign: core_copy(r, zz, 1 - x).start())
    targets(lambda r, zz, sign: core_copy(r, zz, x).start())

    def chip_sum(r, zz, xx):
        return part(r, zz, xx, k)[...].astype(f32) + from_core[r][zz * NX + xx].astype(f32)

    def cross(r, zz, sign):
        core_copy(r, zz, 1 - x).wait_recv()
        to_side[r][zz] = chip_sum(r, zz, 1 - x).astype(to_side[r].dtype)
        side_copy(r, zz).start()

    targets(cross, False)

    def pass_on(r, at, total, sign):
        low = sign > 0
        came = from_low if low else from_high
        first = (z == 0) if low else (z == NZ - 1)

        @pl.when(first)
        def _():
            to_z[r][at] = total.astype(to_z[r].dtype)

        @pl.when(jnp.logical_not(first))
        def _():
            z_copy(r, at, low).wait_recv()
            to_z[r][at] = (total + came[r][at].astype(f32)).astype(to_z[r].dtype)

        z_copy(r, at, low).start()

    def add_line(r, at, here):
        @pl.when(z > 0)
        def _():
            z_copy(r, at, True).wait_recv()
            here[...] += from_low[r][at].astype(f32)

        @pl.when(z < NZ - 1)
        def _():
            z_copy(r, at, False).wait_recv()
            here[...] += from_high[r][at].astype(f32)

    def along(r, zz, sign):
        i, row, rows, crosses = regions[r]
        here = outs[i].at[pl.ds(row, rows)]
        if not crosses:
            core_copy(r, zz, x).wait_recv()
            side_copy(r, zz).wait_recv()
            total = chip_sum(r, zz, x) + from_side[r][zz].astype(f32)
            if sign:
                pass_on(r, zz, total, sign)
            else:
                here[...] = total
                add_line(r, zz, here)
            return
        for xx in (1 - x, x):
            at = zz * NX + xx
            core_copy(r, zz, xx).wait_recv()
            total = chip_sum(r, zz, xx)
            if sign:
                pass_on(r, at, total, sign)
                continue
            here[...] = total
            add_line(r, at, here)
            if xx is x:
                side_copy(r, 0).wait_recv()
                here[...] += from_side[r][0].astype(f32)
            else:
                to_side[r][0] = here[...].astype(to_side[r].dtype)
                side_copy(r, 0).start()

    targets(along)
    hand_on()

    def settle(r, zz, sign):
        core_copy(r, zz, 1 - x).wait_send()
        core_copy(r, zz, x).wait_send()
        if not regions[r][3]:
            side_copy(r, zz).wait_send()
            if sign:
                z_copy(r, zz, sign > 0).wait_send()
        elif sign:
            z_copy(r, zz * NX, sign > 0).wait_send()
            z_copy(r, zz * NX + 1, sign > 0).wait_send()
        else:
            side_copy(r, 0).wait_send()

    targets(settle)
    finish()


def ctx_scatter_kernel(values, carry, number, x_first):
    plan, weights, results = carried(carry)
    regions = regions_of(values, x_first)
    count, made, many = len(values), len(results), len(regions)
    dma = pltpu.SemaphoreType.DMA
    scratch = []
    for straight, crossing in ((8, 8), (4, 1), (4, 1), (4, 8), (4, 8), (4, 8)):
        scratch += [
            pltpu.VMEM(
                (crossing if crosses else straight, rows, values[i].shape[2]), values[i].dtype
            )
            for i, _, rows, crosses in regions
        ]
    done = pl.pallas_call(
        functools.partial(scatter_kernel, count, regions, plan, made),
        out_shape=[jax.ShapeDtypeStruct(v.shape[1:], jnp.float32) for v in values] + results,
        in_specs=[VM] * (count + len(weights)),
        out_specs=[VM] * count + places(results, carry),
        scratch_shapes=scratch
        + [dma((many, NZ * NX)) for _ in range(7)]
        + carry_semaphores(len(plan)),
        compiler_params=settings(number, 3 * bytes_of(values) + bytes_of(weights)),
        name=f"scatter_{number}",
    )(*values, *weights)
    return done[:count], done[count:]


def planned():
    return lax.axis_size("ctx") == NZ * NX * NK and lax.axis_size("wa") == 2


def wa_gather(carry):
    joined = [jnp.concatenate(v, axis=1) if kind == "join" else v for kind, v in carry]
    return [
        pair_swap(v) if kind == "swap" else lax.all_gather(v, "wa", axis=0, tiled=True)
        for (kind, _), v in zip(carry, joined)
    ]


def ctx_gather(values, carry, number, x_first):
    if planned():
        return ctx_gather_kernel(values, carry, number, x_first)
    return [lax.all_gather(v, "ctx", axis=0) for v in values], wa_gather(carry)


def ctx_scatter_sum(values, carry, number, x_first):
    if planned():
        return ctx_scatter_kernel(values, carry, number, x_first)
    summed = [lax.psum_scatter(v, "ctx", scatter_dimension=0).astype(jnp.float32) for v in values]
    return summed, wa_gather(carry)


def per_device(
    tokens,
    doc_starts,
    routes,
    valid,
    teacher,
    out_grad,
    norm1_gain,
    w_query,
    w_key,
    w_value,
    w_out,
    norm2_gain,
    w_router,
    shared_gate,
    shared_up,
    shared_down,
    expert_gate,
    expert_up,
    expert_down,
):
    ctx_count = lax.axis_size("ctx")
    ctx_rank = lax.axis_index("ctx")
    wa_count = lax.axis_size("wa")
    side = lax.axis_index("wa")
    local_rows = tokens.shape[1]
    seq_len = local_rows * ctx_count
    groups = H // KVH
    kv_width = KVH * HD
    experts = w_router.shape[1]
    width = tokens.shape[2]
    lanes = 128
    shared_half = shared_down.shape[0]
    run = shared_half // ctx_count
    low = jnp.bfloat16

    gain_rows = width // wa_count // lanes
    valid_rows = valid[0].astype(jnp.float32)
    small = jnp.zeros((16, lanes), jnp.float32)
    small = small.at[:gain_rows].set(norm1_gain.astype(jnp.float32).reshape(gain_rows, lanes))
    small = small.at[8 : 8 + gain_rows].set(
        norm2_gain.astype(jnp.float32).reshape(gain_rows, lanes)
    )
    small = small.at[6].set(valid_rows)
    tokens_there = pair_swap(tokens[0])
    small_there = pair_swap(small)
    small_all = jnp.where(
        side == 0, jnp.stack([small, small_there]), jnp.stack([small_there, small])
    )
    gain_one = small_all[:, :gain_rows].reshape(width)
    gain_two = small_all[:, 8 : 8 + gain_rows].reshape(width)
    valid_here = jnp.sum(small_all[:, 6])

    doc_first = doc_starts[0]
    own_rows = ctx_rank * local_rows + jnp.arange(local_rows, dtype=jnp.int32)
    query_pos = stored_position(own_rows, local_rows, ctx_count)
    query_place = jnp.stack([query_pos, document_of(query_pos, doc_first)])
    key_pos = stored_position(jnp.arange(seq_len, dtype=jnp.int32), local_rows, ctx_count)
    key_place = jnp.stack([key_pos, document_of(key_pos, doc_first)], axis=1)

    residual = tokens[0].astype(jnp.float32)
    residual_there = tokens_there.astype(jnp.float32)
    inverse_one = rms_inverse(residual)
    scaled_half = jnp.concatenate(
        [
            my_half(residual * inverse_one, side, 1),
            my_half(residual_there * rms_inverse(residual_there), side, 1),
        ]
    )
    normed_half = (scaled_half * norm1_gain.astype(jnp.float32)).astype(low)
    key_value_part = jnp.concatenate(
        [matmul(normed_half, w_key), matmul(normed_half, w_value)], axis=1
    )
    key_value_there = pair_swap(key_value_part[local_rows:].astype(low))
    key_value_own = (key_value_part[:local_rows] + key_value_there.astype(jnp.float32)).astype(low)
    query_part = matmul(normed_half, w_query)

    def shared_columns(weight):
        return [
            lax.dynamic_slice_in_dim(weight, half * shared_half + ctx_rank * run, run, 1)
            for half in range(wa_count)
        ]

    units = wa_count * run
    blank = jnp.zeros((shared_gate.shape[0], lanes - units), low)
    down_rows = lax.dynamic_slice_in_dim(shared_down, ctx_rank * run, run, 0)
    (key_value_all, valid_all), (
        query_there,
        weight_out,
        router_t,
    ) = ctx_gather(
        [key_value_own, jnp.full((8, lanes), valid_here)],
        [
            ("swap", query_part[local_rows:].astype(low)),
            ("core", w_out),
            ("core", w_router.astype(jnp.float32).T),
        ],
        2,
        [16, 0],
    )
    wide_in = jnp.concatenate(
        [
            expert_gate[0],
            expert_up[0],
            *shared_columns(shared_gate),
            blank,
            *shared_columns(shared_up),
            blank,
        ],
        axis=1,
    )
    wide_in, down, down_rows, key_value_all = lax.optimization_barrier(
        (wide_in, expert_down[0], down_rows, key_value_all)
    )
    down_rows_there = pair_swap(down_rows)
    weight_sdown = jnp.where(
        side == 0,
        jnp.concatenate([down_rows, down_rows_there]),
        jnp.concatenate([down_rows_there, down_rows]),
    )
    weight_sdown = jnp.pad(weight_sdown, ((0, lanes - units), (0, 0)))
    down_there = pair_swap(down)
    expert_weights = [wide_in, pair_swap(wide_in), down, down_there, weight_sdown]
    which = jnp.full((1,), side, jnp.int32)
    queries = (query_part[:local_rows] + query_there.astype(jnp.float32)).astype(low)
    key_value_all = key_value_all.reshape(seq_len, 2 * kv_width)
    valid_total = jnp.sum(valid_all[:, 0, 0])
    router_t = router_t.reshape(wa_count, experts, width // wa_count)
    weight_router = jnp.transpose(router_t, (0, 2, 1)).reshape(width, experts).astype(low)
    attn, lse = attend_forward(queries, key_value_all, query_place, key_place)
    attn_low = attn.astype(low)
    attn_low, expert_weights[3] = lax.optimization_barrier((attn_low, expert_weights[3]))
    hidden_one = residual + matmul(attn_low, weight_out)
    inverse_two = rms_inverse(hidden_one)
    normed_two = (hidden_one * inverse_two * gain_two).astype(low)

    logits = matmul(normed_two, weight_router)
    choose = routes[0][:, :, None] == jnp.arange(experts, dtype=jnp.int32)[None, None, :]
    chosen = jnp.any(choose, axis=1)
    peak = jnp.max(jnp.where(chosen, logits, MASKED_SCORE), axis=1, keepdims=True)
    weights = jnp.where(chosen, jnp.exp(jnp.where(chosen, logits, peak) - peak), 0.0)
    gates = weights / jnp.sum(weights, axis=1, keepdims=True)

    (normed_all, gates_all), _ = ctx_gather([normed_two, gates.T], [], 3, [16, 0])
    normed_all = normed_all.reshape(seq_len, width)
    gate = lax.dynamic_slice_in_dim(gates_all, ctx_rank, 1, 1).reshape(seq_len, 1)
    acts, mixed = expert_forward(which, normed_all, gate, expert_weights)
    (routed,), _ = ctx_scatter_sum(
        [mixed.reshape(ctx_count, local_rows, width)], [], 4, [16]
    )
    produced = hidden_one + routed
    output = produced.astype(low)[None]

    errors = produced - teacher[0].astype(jnp.float32)
    local_error = jnp.sum(valid_rows[:, None] * errors * errors)
    tokens_all = wa_count * seq_len
    grad_out = (
        out_grad[0].astype(jnp.float32)
        + 2.0 * tokens_all / valid_total * valid_rows[:, None] * errors
    )
    (grad_all,), _ = ctx_gather([grad_out.astype(low)], [], 5, [16])
    grad_all = grad_all.reshape(seq_len, width)

    (
        grad_rows,
        gate_dot,
        gate_grad,
        up_grad,
        gate_grad_other,
        up_grad_other,
        down_grad,
        down_grad_other,
        shared_grad,
        sdown_grad,
    ) = expert_backward(which, normed_all, grad_all, acts, gate, expert_weights)
    shared_grad = jnp.concatenate([shared_grad[:units], shared_grad[lanes : lanes + units]])
    sdown_grad = sdown_grad[:units]
    small = jnp.full((ctx_count, experts + 8, local_rows), local_error)
    small = small.at[:, :experts].set(0.0)
    small = lax.dynamic_update_slice(
        small, gate_dot.reshape(ctx_count, 1, local_rows), (0, ctx_rank, 0)
    )
    (grad_back, small), (attn_there, normed_two_there) = ctx_scatter_sum(
        [grad_rows.reshape(ctx_count, local_rows, width), small],
        [
            ("swap", my_half(attn_low, 1 - side, 1)),
            ("swap", my_half(normed_two, 1 - side, 1)),
        ],
        6,
        [16, 0],
    )
    grad_gates = small[:experts].T
    error_total = small[experts, 0]
    grad_logits = (
        gates * (grad_gates - jnp.sum(gates * grad_gates, axis=1, keepdims=True))
    ).astype(low)
    grad_normed = grad_back + contract_cols(grad_logits, weight_router)

    def for_pair(full):
        return ("swap", my_half(full, 1 - side, 0).astype(low))

    def with_pair(full, other):
        return my_half(full, side, 0) + other.astype(jnp.float32)

    grad_hidden_norm, grad_gain_two = norm_backward(hidden_one, inverse_two, gain_two, grad_normed)
    grad_hidden_one = grad_out + grad_hidden_norm
    grad_attn_in = grad_hidden_one.astype(low)
    grad_heads = contract_cols(grad_attn_in, weight_out).astype(low)
    delta = jnp.einsum(
        "tagd,tagd->agt",
        grad_heads.astype(jnp.float32).reshape(local_rows, KVH, groups, HD),
        attn.reshape(local_rows, KVH, groups, HD),
    ).reshape(KVH, 1, groups * local_rows)
    grad_query, grad_keys, grad_values = attend_grads(
        queries, grad_heads, key_value_all, lse, delta, query_place, key_place
    )
    def for_all(vector):
        flat = jnp.zeros((16 * lanes,), jnp.float32).at[: vector.shape[0]].set(vector)
        return jnp.broadcast_to(flat.reshape(16, lanes), (ctx_count, 16, lanes))

    def from_all(summed, size):
        return summed.reshape(16 * lanes)[:size]

    def by_slot(value):
        return value.reshape(ctx_count, value.shape[0] // ctx_count, value.shape[1])

    half_width = width // wa_count
    (grad_key, grad_value, small), (
        da_there,
        logits_there,
        query_grad_there,
        error_there,
        shared_there,
        sdown_there,
    ) = ctx_scatter_sum(
        [
            grad_keys.reshape(ctx_count, local_rows, kv_width),
            grad_values.reshape(ctx_count, local_rows, kv_width),
            for_all(grad_gain_two),
        ],
        [
            ("swap", grad_attn_in),
            ("swap", grad_logits),
            ("swap", grad_query),
            ("swap", jnp.full((8, lanes), error_total)),
            ("swap", my_half(shared_grad, 1 - side, 1).astype(low)),
            for_pair(sdown_grad),
        ],
        7,
        [16, 16, 0],
    )
    error_total = error_total + error_there[0, 0]
    key_value_low = jnp.concatenate([grad_key, grad_value], axis=1).astype(low)
    gain_two_sum = from_all(small, width)

    def weight_grad(mine, right, theirs, right_there):
        mine = my_half(mine, side, 1)
        return (contract_rows(mine, right) + contract_rows(theirs, right_there)).astype(low)

    out_part = weight_grad(attn_low, grad_attn_in, attn_there, da_there)
    router_part = contract_rows(grad_logits, my_half(normed_two, side, 1)) + contract_rows(
        logits_there, normed_two_there
    )
    shared_part = my_half(shared_grad, side, 1) + shared_there.astype(jnp.float32)
    sdown_part = with_pair(sdown_grad, sdown_there).astype(low)
    rows_two = jnp.zeros((16, lanes), jnp.float32)
    rows_two = rows_two.at[: half_width // lanes].set(
        my_half(gain_two_sum, 1 - side, 0).reshape(-1, lanes)
    )
    router_rows = router_part.reshape(experts, half_width // lanes, lanes)
    router_rows = jnp.pad(router_rows, ((0, 0), (0, 8 - half_width // lanes), (0, 0)))
    (out_sum, router_sum), (kv_grad_there, rows_there, down_there) = ctx_scatter_sum(
        [by_slot(out_part), router_rows],
        [("swap", key_value_low), ("swap", rows_two), ("swap", down_grad_other)],
        8,
        [0, 0],
    )
    total_gain_two = my_half(gain_two_sum, side, 0) + rows_there.reshape(-1)[:half_width]

    query_both = jnp.concatenate([grad_query, query_grad_there])
    kv_both = jnp.concatenate([key_value_low, kv_grad_there])
    normed_grad = (
        contract_cols(query_both, w_query)
        + contract_cols(kv_both[:, :kv_width], w_key)
        + contract_cols(kv_both[:, kv_width:], w_value)
    )
    (query_sum, kv_sum, small), (normed_grad_there, gate_there) = ctx_scatter_sum(
        [
            by_slot(contract_rows(normed_half, query_both).astype(low)),
            by_slot(contract_rows(normed_half, kv_both).astype(low)),
            for_all(jnp.sum(normed_grad * scaled_half, axis=0)),
        ],
        [
            ("swap", normed_grad[local_rows:].astype(low)),
            ("swap", gate_grad_other),
        ],
        9,
        [0, 16, 0],
    )
    total_gain_one = from_all(small, half_width)
    low_half, high_half = normed_grad[:local_rows], normed_grad_there.astype(jnp.float32)
    grad_normed_one = jnp.where(
        side == 0,
        jnp.concatenate([low_half, high_half], axis=1),
        jnp.concatenate([high_half, low_half], axis=1),
    )
    grad_residual_norm, _ = norm_backward(residual, inverse_one, gain_one, grad_normed_one)
    grad_input = grad_hidden_one + grad_residual_norm
    (total_query, total_kv, total_out, router_sum, shared_parts, sdown_parts), (up_there,) = ctx_gather(
        [
            query_sum.astype(low),
            kv_sum.astype(low),
            out_sum.astype(low),
            router_sum,
            shared_part.astype(low),
            sdown_part,
        ],
        [("swap", up_grad_other)],
        10,
        [0, 0, 0, 0, 0, sdown_part.shape[0]],
    )
    total_query = total_query.reshape(half_width, width).astype(jnp.float32)
    total_kv = total_kv.reshape(half_width, 2 * kv_width).astype(jnp.float32)
    total_out = total_out.reshape(half_width, width).astype(jnp.float32)
    router_sum = router_sum[:, : half_width // lanes].reshape(experts, half_width)
    row = jnp.arange(ctx_count * units, dtype=jnp.int32)[:, None]
    half, unit = row % units // run, row % run
    column = half * shared_half + row // units * run + unit
    select = (column == jnp.arange(ctx_count * units, dtype=jnp.int32)[None, :]).astype(low)
    total_sgate, total_sup = [
        contract_rows(
            shared_parts[:, first : first + units].reshape(ctx_count * units, half_width), select
        )
        for first in (0, units)
    ]
    down_grad = down_grad + down_there.astype(jnp.float32)
    return (
        error_total / (valid_total * width),
        output,
        grad_input[None],
        total_gain_one,
        total_query,
        total_kv[:, :kv_width],
        total_kv[:, kv_width:],
        total_out,
        total_gain_two,
        router_sum.T,
        total_sgate,
        total_sup,
        sdown_parts.reshape(shared_half, width).astype(jnp.float32),
        (gate_grad + gate_there.astype(jnp.float32))[None],
        (up_grad + up_there.astype(jnp.float32))[None],
        down_grad[None],
    )


def solution(mesh):
    return jax.shard_map(
        per_device,
        mesh=mesh,
        in_specs=(
            P("wa", "ctx", None),
            P("wa", None),
            P("wa", "ctx", None),
            P("wa", "ctx"),
            P("wa", "ctx", None),
            P("wa", "ctx", None),
            P("wa"),
            P("wa", None),
            P("wa", None),
            P("wa", None),
            P("wa", None),
            P("wa"),
            P("wa", None),
            P("wa", None),
            P("wa", None),
            P("wa", None),
            P("ctx", "wa", None),
            P("ctx", "wa", None),
            P("ctx", "wa", None),
        ),
        out_specs=(
            P(),
            P("wa", "ctx", None),
            P("wa", "ctx", None),
            P("wa"),
            P("wa", None),
            P("wa", None),
            P("wa", None),
            P("wa", None),
            P("wa"),
            P("wa", None),
            P("wa", None),
            P("wa", None),
            P("wa", None),
            P("ctx", "wa", None),
            P("ctx", "wa", None),
            P("ctx", "wa", None),
        ),
        check_vma=False,
    )
```

```python
import functools

import jax
import jax.numpy as jnp
from jax import lax
from jax.experimental import pallas as pl
from jax.experimental.pallas import tpu as pltpu
from jax.sharding import PartitionSpec as P

H = 12
KVH = 4
HD = 128
EPSILON = 1e-05
MASKED_SCORE = -1e30


def stored_position(stored_rows, local_rows, ctx_count):
    half_rows = local_rows // 2
    owner_rank = stored_rows // local_rows
    within_rows = stored_rows % local_rows
    first_half = owner_rank * half_rows + within_rows
    second_half = (2 * ctx_count - 1 - owner_rank) * half_rows + within_rows - half_rows
    return jnp.where(within_rows < half_rows, first_half, second_half)


def document_of(positions, doc_first):
    return jnp.sum((doc_first[None, :] <= positions[:, None]).astype(jnp.int32), axis=1) - 1


def matmul(left, right):
    return jnp.dot(left, right, preferred_element_type=jnp.float32)


def contract_rows(left, right):
    return lax.dot_general(
        left, right, (((0,), (0,)), ((), ())), preferred_element_type=jnp.float32
    )


def contract_cols(left, right):
    return lax.dot_general(
        left, right, (((1,), (1,)), ((), ())), preferred_element_type=jnp.float32
    )


def rms_inverse(values):
    return lax.rsqrt(jnp.mean(values * values, axis=1, keepdims=True) + EPSILON)


def norm_backward(values, inverse, gain, grad_normed):
    scaled = grad_normed * gain
    inner_sum = jnp.sum(scaled * values, axis=1, keepdims=True)
    grad_values = (
        inverse * scaled - values * (inverse * inverse * inverse) * inner_sum / values.shape[1]
    )
    grad_gain = jnp.sum(grad_normed * values * inverse, axis=0)
    return (grad_values, grad_gain)


def pair_swap(value):
    return lax.ppermute(value, "wa", [(0, 1), (1, 0)])


def my_half(value, side, axis):
    size = value.shape[axis] // 2
    return lax.dynamic_slice_in_dim(value, side * size, size, axis)


def heads_as_rows(value):
    return jnp.concatenate(
        [value[:, h * HD : (h + 1) * HD] for h in range(value.shape[1] // HD)], axis=0
    )


def rows_as_heads(value, rows):
    return jnp.concatenate(
        [value[h * rows : (h + 1) * rows] for h in range(value.shape[0] // rows)], axis=1
    )


def seen(query_ref, key_ref, first, count, groups):
    key_pos, key_doc = key_ref[pl.ds(first, count), 0:1], key_ref[pl.ds(first, count), 1:2]
    query_pos, query_doc = query_ref[0:1, :], query_ref[1:2, :]
    visible = (key_pos <= query_pos) & (key_doc == query_doc)
    return jnp.concatenate([visible.astype(jnp.float32)] * groups, axis=1) > 0.5


def attend_kernel(block, query_ref, key_ref, value_ref, query_place, key_place, out_ref, lse_ref):
    rows = query_ref.shape[0]
    groups = query_ref.shape[1] // HD
    scale = HD ** (-0.5)
    queries = heads_as_rows(query_ref[...])

    def step(index, carry):
        peak, total, mixed = carry
        first = pl.multiple_of(index * block, block)
        scores = contract_cols(key_ref[pl.ds(first, block), :], queries) * scale
        visible = seen(query_place, key_place, first, block, groups)
        scores = jnp.where(visible, scores, MASKED_SCORE)
        new_peak = jnp.maximum(peak, jnp.max(scores, axis=0, keepdims=True))
        shrink = jnp.exp(peak - new_peak)
        weights = jnp.where(visible, jnp.exp(scores - new_peak), 0.0)
        total = total * shrink + jnp.sum(weights, axis=0, keepdims=True)
        part = contract_rows(value_ref[pl.ds(first, block), :], weights.astype(jnp.bfloat16))
        return new_peak, total, mixed * shrink + part

    width = groups * rows
    initial = (
        jnp.full((1, width), MASKED_SCORE, jnp.float32),
        jnp.zeros((1, width), jnp.float32),
        jnp.zeros((HD, width), jnp.float32),
    )
    peak, total, mixed = lax.fori_loop(0, key_ref.shape[0] // block, step, initial)
    out_ref[...] = rows_as_heads((mixed / total).T, rows)
    lse_ref[0] = peak + jnp.log(total)


def attend_grads_kernel(
    block,
    query_ref,
    grad_ref,
    key_ref,
    value_ref,
    lse_ref,
    delta_ref,
    query_place,
    key_place,
    query_grad_ref,
    key_grad_ref,
    value_grad_ref,
):
    rows = query_ref.shape[0]
    groups = query_ref.shape[1] // HD
    scale = HD ** (-0.5)
    queries = heads_as_rows(query_ref[...])
    grads = heads_as_rows(grad_ref[...])
    lse, delta = lse_ref[0], delta_ref[0]

    def step(index, total):
        first = pl.multiple_of(index * block, block)
        here = pl.ds(first, block)
        keys = key_ref[here, :]
        scores = contract_cols(keys, queries) * scale
        visible = seen(query_place, key_place, first, block, groups)
        probs = jnp.where(visible, jnp.exp(jnp.where(visible, scores, MASKED_SCORE) - lse), 0.0)
        grad_probs = contract_cols(value_ref[here, :], grads)
        grad_scores = (probs * (grad_probs - delta)).astype(jnp.bfloat16)
        key_grad_ref[here, :] = (matmul(grad_scores, queries) * scale).astype(jnp.bfloat16)
        value_grad_ref[here, :] = matmul(probs.astype(jnp.bfloat16), grads).astype(jnp.bfloat16)
        return total + contract_rows(keys, grad_scores)

    total = lax.fori_loop(
        0, key_ref.shape[0] // block, step, jnp.zeros((HD, groups * rows), jnp.float32)
    )
    query_grad_ref[...] = rows_as_heads((total * scale).T, rows).astype(jnp.bfloat16)


def attention_specs(rows, seq_len):
    wide = HD * (H // KVH)
    return dict(
        query=pl.BlockSpec((rows, wide), lambda a: (0, a)),
        key=pl.BlockSpec((seq_len, HD), lambda a: (0, a)),
        value=pl.BlockSpec((seq_len, HD), lambda a: (0, KVH + a)),
        row=pl.BlockSpec((1, 1, rows * (H // KVH)), lambda a: (a, 0, 0)),
        query_place=pl.BlockSpec((2, rows), lambda a: (0, 0)),
        key_place=pl.BlockSpec((seq_len, 2), lambda a: (0, 0)),
    )


def attend_forward(queries, key_value_all, query_place, key_place):
    rows, seq_len = queries.shape[0], key_value_all.shape[0]
    s = attention_specs(rows, seq_len)
    return pl.pallas_call(
        functools.partial(attend_kernel, min(seq_len, 1024)),
        grid=(KVH,),
        out_shape=[
            jax.ShapeDtypeStruct((rows, H * HD), jnp.float32),
            jax.ShapeDtypeStruct((KVH, 1, rows * (H // KVH)), jnp.float32),
        ],
        in_specs=[s["query"], s["key"], s["value"], s["query_place"], s["key_place"]],
        out_specs=[s["query"], s["row"]],
        compiler_params=pltpu.CompilerParams(vmem_limit_bytes=20 * 2**20),
        name="attend",
    )(queries, key_value_all, key_value_all, query_place, key_place)


def attend_grads(queries, grads, key_value_all, lse, delta, query_place, key_place):
    rows, seq_len = queries.shape[0], key_value_all.shape[0]
    s = attention_specs(rows, seq_len)
    return pl.pallas_call(
        functools.partial(attend_grads_kernel, min(seq_len, 1024)),
        grid=(KVH,),
        out_shape=[
            jax.ShapeDtypeStruct((rows, H * HD), jnp.bfloat16),
            jax.ShapeDtypeStruct((seq_len, KVH * HD), jnp.bfloat16),
            jax.ShapeDtypeStruct((seq_len, KVH * HD), jnp.bfloat16),
        ],
        in_specs=[
            s["query"],
            s["query"],
            s["key"],
            s["value"],
            s["row"],
            s["row"],
            s["query_place"],
            s["key_place"],
        ],
        out_specs=[s["query"], s["key"], s["key"]],
        compiler_params=pltpu.CompilerParams(vmem_limit_bytes=32 * 2**20),
        name="attend_grads",
    )(queries, grads, key_value_all, key_value_all, lse, delta, query_place, key_place)

def expert_forward_kernel(
    side_ref, rows_ref, gate_ref, own_in, other_in, own_down, other_down, sdown, acts_ref, mixed_ref
):
    side = side_ref[0]
    hidden, depth = own_down.shape[0] * 2, own_in.shape[0]
    pad = sdown.shape[0]

    def half(size, which):
        return pl.ds(pl.multiple_of(which * size, size), size)

    acts_ref[...] = matmul(rows_ref[:, half(depth, side)], own_in[...]) + matmul(
        rows_ref[:, half(depth, 1 - side)], other_in[...]
    )
    gate_act, up_act = acts_ref[:, :hidden], acts_ref[:, hidden : 2 * hidden]
    hidden_exp = (gate_act * jax.nn.sigmoid(gate_act) * up_act).astype(jnp.bfloat16)
    shared_gact = acts_ref[:, 2 * hidden : 2 * hidden + pad]
    shared_uact = acts_ref[:, 2 * hidden + pad :]
    shared_hidden = (shared_gact * jax.nn.sigmoid(shared_gact) * shared_uact).astype(jnp.bfloat16)
    first, second = hidden_exp[:, : hidden // 2], hidden_exp[:, hidden // 2 :]
    swap = side == 1
    out = matmul(jnp.where(swap, second, first), own_down[...]) + matmul(
        jnp.where(swap, first, second), other_down[...]
    )
    mixed = gate_ref[...] * out.astype(jnp.bfloat16).astype(jnp.float32)
    mixed_ref[...] = (mixed + matmul(shared_hidden, sdown[...])).astype(jnp.bfloat16)


def expert_backward_kernel(
    side_ref,
    rows_ref,
    grad_ref,
    acts_ref,
    gate_ref,
    own_in,
    other_in,
    own_down,
    other_down,
    sdown,
    grad_rows_ref,
    dots_ref,
    gate_own,
    up_own,
    gate_other,
    up_other,
    down_own,
    down_other,
    shared_out,
    sdown_out,
    acts_grad,
    in_total,
    down_total,
    shared_total,
    sdown_total,
):
    low = jnp.bfloat16
    side = side_ref[0]
    hidden, depth = own_down.shape[0] * 2, own_in.shape[0]
    pad = sdown.shape[0]

    def half(size, which):
        return pl.ds(pl.multiple_of(which * size, size), size)

    @pl.when(pl.program_id(0) == 0)
    def _():
        for total in (in_total, down_total, shared_total, sdown_total):
            total[...] = jnp.zeros_like(total)

    rows, grads, gate = rows_ref[...], grad_ref[...], gate_ref[...]
    ours, theirs = contract_cols(grads, own_down[...]), contract_cols(grads, other_down[...])
    swap = side == 1
    grad_hidden = jnp.concatenate(
        [jnp.where(swap, theirs, ours), jnp.where(swap, ours, theirs)], axis=1
    )

    def through(grad, gate_act, up_act, at):
        sigmoid = jax.nn.sigmoid(gate_act)
        silu = gate_act * sigmoid
        width = gate_act.shape[1]
        grad_gate = grad * up_act * sigmoid * (1.0 + gate_act * (1.0 - sigmoid))
        acts_grad[:, at : at + width] = grad_gate.astype(low)
        acts_grad[:, at + width : at + 2 * width] = (grad * silu).astype(low)
        return (silu * up_act).astype(low)

    hidden_exp = through(
        gate * grad_hidden, acts_ref[:, :hidden], acts_ref[:, hidden : 2 * hidden], 0
    )
    shared_hidden = through(
        contract_cols(grads, sdown[...]),
        acts_ref[:, 2 * hidden : 2 * hidden + pad],
        acts_ref[:, 2 * hidden + pad :],
        2 * hidden,
    )
    dots_ref[...] = jnp.sum(grad_hidden * hidden_exp.astype(jnp.float32), axis=1, keepdims=True)
    grad_rows_ref[:, half(depth, side)] = contract_cols(acts_grad[...], own_in[...]).astype(low)
    grad_rows_ref[:, half(depth, 1 - side)] = contract_cols(acts_grad[...], other_in[...]).astype(
        low
    )
    in_total[...] += contract_rows(rows, acts_grad[:, : 2 * hidden])
    shared_total[...] += contract_rows(acts_grad[:, 2 * hidden :], rows)
    picked = (gate * grads.astype(jnp.float32)).astype(low)
    down_total[...] += contract_rows(hidden_exp, picked)
    sdown_total[...] += contract_rows(shared_hidden, grads)

    @pl.when(pl.program_id(0) == pl.num_programs(0) - 1)
    def _():
        mine, other = half(depth, side), half(depth, 1 - side)
        gate_own[...] = in_total[mine, :hidden]
        up_own[...] = in_total[mine, hidden:]
        gate_other[...] = in_total[other, :hidden].astype(low)
        up_other[...] = in_total[other, hidden:].astype(low)
        down_own[...] = down_total[half(hidden // 2, side), :]
        down_other[...] = down_total[half(hidden // 2, 1 - side), :].astype(low)
        shared_out[...] = shared_total[...]
        sdown_out[...] = sdown_total[...]


def whole(value):
    return pl.BlockSpec(
        value.shape, lambda i: (0,) * len(value.shape), pipeline_mode=pl.Buffered(1)
    )


def by_rows(block, columns):
    return pl.BlockSpec((block, columns), lambda i: (i, 0))


def expert_forward(side, rows, gate, weights):
    total, width = rows.shape
    block, acts = min(total, 512), weights[0].shape[1]
    return pl.pallas_call(
        expert_forward_kernel,
        grid=(total // block,),
        out_shape=[
            jax.ShapeDtypeStruct((total, acts), jnp.float32),
            jax.ShapeDtypeStruct((total, width), jnp.bfloat16),
        ],
        in_specs=[
            pl.BlockSpec(memory_space=pltpu.SMEM),
            by_rows(block, width),
            by_rows(block, 1),
            *map(whole, weights),
        ],
        out_specs=[by_rows(block, acts), by_rows(block, width)],
        compiler_params=pltpu.CompilerParams(vmem_limit_bytes=32 * 2**20),
        name="expert_forward",
    )(side, rows, gate, *weights)


def expert_backward(side, rows, grads, acts, gate, weights):
    total, width = rows.shape
    block, columns = min(total, 256), weights[0].shape[1]
    depth, hidden = weights[0].shape[0], 2 * weights[2].shape[0]
    pad = weights[4].shape[0]
    shape, f32, low = jax.ShapeDtypeStruct, jnp.float32, jnp.bfloat16
    ends = [
        shape((depth, hidden), f32),
        shape((depth, hidden), f32),
        shape((depth, hidden), low),
        shape((depth, hidden), low),
        shape((hidden // 2, width), f32),
        shape((hidden // 2, width), low),
        shape((2 * pad, width), f32),
        shape((pad, width), f32),
    ]
    return pl.pallas_call(
        expert_backward_kernel,
        grid=(total // block,),
        out_shape=[shape((total, width), low), shape((total, 1), f32), *ends],
        in_specs=[
            pl.BlockSpec(memory_space=pltpu.SMEM),
            by_rows(block, width),
            by_rows(block, width),
            by_rows(block, columns),
            by_rows(block, 1),
            *map(whole, weights),
        ],
        out_specs=[by_rows(block, width), by_rows(block, 1), *map(whole, ends)],
        scratch_shapes=[
            pltpu.VMEM((block, columns), low),
            pltpu.VMEM((width, 2 * hidden), f32),
            pltpu.VMEM((hidden, width), f32),
            pltpu.VMEM((2 * pad, width), f32),
            pltpu.VMEM((pad, width), f32),
        ],
        compiler_params=pltpu.CompilerParams(vmem_limit_bytes=60 * 2**20),
        name="expert_backward",
    )(side, rows, grads, acts, gate, *weights)


MESH = pl.DeviceIdType.MESH
NZ, NX, NK = 4, 2, 2
PIECE = 200_000
VM = pl.BlockSpec(memory_space=pltpu.VMEM)
HBM = pl.BlockSpec(memory_space=pl.ANY)


def settings(number, held):
    return pltpu.CompilerParams(
        collective_id=number, has_side_effects=True, vmem_limit_bytes=held + 4 * 2**20
    )


def bytes_of(arrays):
    return sum(v.size * v.dtype.itemsize for v in arrays)


def slot_of(z, x, k):
    return (z * NX + x) * NK + k


def place():
    c = lax.axis_index("ctx")
    return c, c // (NX * NK), lax.rem(c // NK, NX), lax.rem(c, NK), lax.axis_index("wa")


def greet(z, x, k, w, pair, plane=True):
    barrier = pltpu.get_barrier_semaphore()

    def hello(device):
        pl.semaphore_signal(barrier, inc=1, device_id=device, device_id_type=MESH)

    hello((slot_of(z, x, 1 - k), w))
    count = 1
    if pair:
        hello((slot_of(z, x, k), 1 - w))
        count += 1
    if plane:
        hello((slot_of(z, 1 - x, k), w))
        count += 1

        @pl.when(z > 0)
        def _():
            hello((slot_of(z - 1, x, k), w))

        @pl.when(z < NZ - 1)
        def _():
            hello((slot_of(z + 1, x, k), w))

        count += jnp.where(z > 0, 1, 0) + jnp.where(z < NZ - 1, 1, 0)
    pl.semaphore_wait(barrier, count)


def carry_steps(plan, shards, targets, sems, x, z, k, w):
    own_sem, pair_send, pair_recv, core_send, core_recv = sems
    partner, sibling = (slot_of(z, x, k), 1 - w), (slot_of(z, x, 1 - k), w)
    plan, outs, columns = zip(*plan) if plan else ((), (), ())
    fulls = [
        targets[o] if c is None else targets[o].at[:, pl.ds(c, shards[i].shape[1])]
        for i, (o, c) in enumerate(zip(outs, columns))
    ]

    def rows_of(i, owner):
        h = shards[i].shape[0]
        if plan[i] == "whole":
            return pl.ds(pl.multiple_of(owner * h, h), h)
        half = h // 2
        return pl.ds(pl.multiple_of(owner * h + k * half, half), half)

    def own(i):
        h = shards[i].shape[0]
        return pltpu.make_async_copy(
            shards[i], fulls[i].at[pl.ds(pl.multiple_of(w * h, h), h)], own_sem.at[i]
        )

    def over_pair(i):
        return pltpu.make_async_remote_copy(
            src_ref=shards[i].at[rows_of(i, 0)] if plan[i] == "core" else shards[i],
            dst_ref=fulls[i] if plan[i] == "swap" else fulls[i].at[rows_of(i, w)],
            send_sem=pair_send.at[i],
            recv_sem=pair_recv.at[i],
            device_id=partner,
            device_id_type=MESH,
        )

    def over_core(i):
        here = fulls[i].at[rows_of(i, 1 - w)]
        return pltpu.make_async_remote_copy(
            src_ref=here,
            dst_ref=here,
            send_sem=core_send.at[i],
            recv_sem=core_recv.at[i],
            device_id=sibling,
            device_id_type=MESH,
        )

    every = range(len(shards))

    def start():
        for i in every:
            over_pair(i).start()
        for i in every:
            if plan[i] != "swap":
                own(i).start()

    def hand_on():
        for i in every:
            over_pair(i).wait_recv()
            if plan[i] == "core":
                over_core(i).start()

    def finish():
        for i in every:
            if plan[i] != "swap":
                own(i).wait()
            over_pair(i).wait_send()
            if plan[i] == "core":
                over_core(i).wait()

    return start, hand_on, finish


def carry_semaphores(count):
    return [pltpu.SemaphoreType.DMA((max(count, 1),)) for _ in range(5)]


def places(results, carry):
    return [VM if kind == "swap" else HBM for (kind, _), _ in zip(carry, results)]


def carried(carry):
    plan, operands, results = [], [], []
    for kind, value in carry:
        parts = value if kind == "join" else [value]
        column = 0
        for v in parts:
            where = column if kind == "join" else None
            plan.append(("whole" if kind == "join" else kind, len(results), where))
            operands.append(v)
            column += v.shape[1]
        rows = parts[0].shape[0] * (1 if kind == "swap" else 2)
        results.append(jax.ShapeDtypeStruct((rows, column), parts[0].dtype))
    return plan, operands, results


def regions_of(values, x_first):
    found = []
    for i, (v, rows) in enumerate(zip(values, x_first)):
        total = v.shape[-2]
        if rows:
            found.append((i, total - rows, rows, True))
        straight = total - rows
        parts = max(1, -(-straight * v.shape[-1] * v.dtype.itemsize // PIECE))
        step = -(-straight // parts // 16) * 16 if parts > 1 else max(straight, 1)
        for first in range(0, straight, step):
            found.append((i, first, min(step, straight - first), False))
    return found


def gather_kernel(count, regions, plan, made, *refs):
    ins, shards = refs[:count], refs[count : count + len(plan)]
    refs = refs[count + len(plan) :]
    outs, fulls = refs[:count], refs[count : count + made]
    send_sem, recv_sem, own_sem, *carry_sems = refs[count + made :]
    me, z, x, k, w = place()
    greet(z, x, k, w, made > 0)
    up, down = (slot_of(z + 1, x, k), w), (slot_of(z - 1, x, k), w)
    side, sibling = (slot_of(z, 1 - x, k), w), (slot_of(z, x, 1 - k), w)

    every = range(len(regions))
    straight = [r for r in every if not regions[r][3]]
    crossing = [r for r in every if regions[r][3]]

    def copy(r, slot, way, device, first=False):
        i, row, rows, _ = regions[r]
        here = pl.ds(row, rows)
        return pltpu.make_async_remote_copy(
            src_ref=ins[i].at[here] if first else outs[i].at[slot, here],
            dst_ref=outs[i].at[slot, here],
            send_sem=send_sem.at[r, slot, way],
            recv_sem=recv_sem.at[r, slot],
            device_id=device,
            device_id_type=MESH,
        )

    def send(*what):
        copy(*what).start()

    def sent(*what):
        copy(*what).wait_send()

    def arrived(r, slot):
        copy(r, slot, 0, sibling).wait_recv()

    def onward(act, r, slot, sign):
        if sign <= 0:

            @pl.when(z < NZ - 1)
            def _():
                act(r, slot, 0, up)

        if sign >= 0:

            @pl.when(z > 0)
            def _():
                act(r, slot, 1, down)

    def across(d, act, wait):
        for sign in (-1, 1) if d else (0,):
            there = z + sign * d

            @pl.when((there >= 0) & (there < NZ))
            def _():
                slot = slot_of(there, 1 - x, k)
                for r in straight:
                    wait(r, slot)
                    act(r, slot, 3, sibling)

    def walk(act, wait):
        for r in every:
            act(r, me, 2, side, True)

        @pl.when(z < NZ - 1)
        def _():
            for r in every:
                act(r, me, 0, up, True)

        @pl.when(z > 0)
        def _():
            for r in every:
                act(r, me, 1, down, True)

        for r in every:
            act(r, me, 3, sibling, True)
        slot = slot_of(z, 1 - x, k)
        for r in crossing:
            wait(r, slot)
            onward(act, r, slot, 0)
            act(r, slot, 3, sibling)
        for d in range(1, NZ):
            for sign in (-1, 1):
                there = z + sign * d

                @pl.when((there >= 0) & (there < NZ))
                def _():
                    slot = slot_of(there, x, k)
                    for r in straight:
                        wait(r, slot)
                        if d < NZ - 1:
                            onward(act, r, slot, sign)
                        act(r, slot, 2, side)
                        act(r, slot, 3, sibling)
                    for r in crossing:
                        for column in (x, 1 - x):
                            slot = slot_of(there, column, k)
                            wait(r, slot)
                            if d < NZ - 1:
                                onward(act, r, slot, sign)
                            act(r, slot, 3, sibling)

            across(d - 1, act, wait)
        across(NZ - 1, act, wait)

    own = [pltpu.make_async_copy(ins[i], outs[i].at[me], own_sem.at[i]) for i in range(count)]
    start, hand_on, finish = carry_steps(plan, shards, fulls, carry_sems, x, z, k, w)
    start()
    walk(send, arrived)
    for o in own:
        o.start()
    hand_on()
    for other in range(NZ * NX):
        for r in every:
            arrived(r, other * NK + 1 - k)
    walk(sent, lambda r, slot: None)
    for o in own:
        o.wait()
    finish()


def ctx_gather_kernel(values, carry, number, x_first):
    plan, weights, results = carried(carry)
    regions = regions_of(values, x_first)
    count, made = len(values), len(results)
    n = NZ * NX * NK
    done = pl.pallas_call(
        functools.partial(gather_kernel, count, regions, plan, made),
        out_shape=[jax.ShapeDtypeStruct((n, *v.shape), v.dtype) for v in values] + results,
        in_specs=[VM] * (count + len(weights)),
        out_specs=[HBM] * count + places(results, carry),
        scratch_shapes=[
            pltpu.SemaphoreType.DMA((len(regions), n, 4)),
            pltpu.SemaphoreType.DMA((len(regions), n)),
            pltpu.SemaphoreType.DMA((count,)),
        ]
        + carry_semaphores(len(plan)),
        compiler_params=settings(number, bytes_of([*values, *weights])),
        name=f"gather_{number}",
    )(*values, *weights)
    return done[:count], done[count:]


def scatter_kernel(count, regions, plan, made, *refs):
    ins, shards = refs[:count], refs[count : count + len(plan)]
    refs = refs[count + len(plan) :]
    outs, fulls = refs[:count], refs[count : count + made]
    scratch = refs[count + made :]
    many = len(regions)
    from_core, from_side, to_side, from_low, from_high, to_z = (
        scratch[g * many : (g + 1) * many] for g in range(6)
    )
    send_core, recv_core, send_side, recv_side, send_z, recv_low, recv_high, *carry_sems = scratch[
        6 * many :
    ]
    me, z, x, k, w = place()
    greet(z, x, k, w, made > 0)
    up, down = (slot_of(z + 1, x, k), w), (slot_of(z - 1, x, k), w)
    side, sibling = (slot_of(z, 1 - x, k), w), (slot_of(z, x, 1 - k), w)
    f32 = jnp.float32

    def part(r, zz, xx, core):
        i, row, rows, _ = regions[r]
        return ins[i].at[slot_of(zz, xx, core), pl.ds(row, rows)]

    def core_copy(r, zz, xx):
        pair = zz * NX + xx
        return pltpu.make_async_remote_copy(
            src_ref=part(r, zz, xx, 1 - k),
            dst_ref=from_core[r].at[pair],
            send_sem=send_core.at[r, pair],
            recv_sem=recv_core.at[r, pair],
            device_id=sibling,
            device_id_type=MESH,
        )

    def side_copy(r, at):
        return pltpu.make_async_remote_copy(
            src_ref=to_side[r].at[at],
            dst_ref=from_side[r].at[at],
            send_sem=send_side.at[r, at],
            recv_sem=recv_side.at[r, at],
            device_id=side,
            device_id_type=MESH,
        )

    def z_copy(r, at, low):
        return pltpu.make_async_remote_copy(
            src_ref=to_z[r].at[at],
            dst_ref=(from_low if low else from_high)[r].at[at],
            send_sem=send_z.at[r, at],
            recv_sem=(recv_low if low else recv_high).at[r, at],
            device_id=up if low else down,
            device_id_type=MESH,
        )

    def targets(act, route=None):
        for d in range(NZ - 1, -1, -1):
            for sign in (1, -1) if d else (0,):
                there = z + sign * d

                @pl.when((there >= 0) & (there < NZ))
                def _():
                    for r in range(many):
                        if route is None or regions[r][3] == route:
                            act(r, there, sign)

    start, hand_on, finish = carry_steps(plan, shards, fulls, carry_sems, x, z, k, w)
    start()
    targets(lambda r, zz, sign: core_copy(r, zz, 1 - x).start())
    targets(lambda r, zz, sign: core_copy(r, zz, x).start())

    def chip_sum(r, zz, xx):
        return part(r, zz, xx, k)[...].astype(f32) + from_core[r][zz * NX + xx].astype(f32)

    def cross(r, zz, sign):
        core_copy(r, zz, 1 - x).wait_recv()
        to_side[r][zz] = chip_sum(r, zz, 1 - x).astype(to_side[r].dtype)
        side_copy(r, zz).start()

    targets(cross, False)

    def pass_on(r, at, total, sign):
        low = sign > 0
        came = from_low if low else from_high
        first = (z == 0) if low else (z == NZ - 1)

        @pl.when(first)
        def _():
            to_z[r][at] = total.astype(to_z[r].dtype)

        @pl.when(jnp.logical_not(first))
        def _():
            z_copy(r, at, low).wait_recv()
            to_z[r][at] = (total + came[r][at].astype(f32)).astype(to_z[r].dtype)

        z_copy(r, at, low).start()

    def add_line(r, at, here):
        @pl.when(z > 0)
        def _():
            z_copy(r, at, True).wait_recv()
            here[...] += from_low[r][at].astype(f32)

        @pl.when(z < NZ - 1)
        def _():
            z_copy(r, at, False).wait_recv()
            here[...] += from_high[r][at].astype(f32)

    def along(r, zz, sign):
        i, row, rows, crosses = regions[r]
        here = outs[i].at[pl.ds(row, rows)]
        if not crosses:
            core_copy(r, zz, x).wait_recv()
            side_copy(r, zz).wait_recv()
            total = chip_sum(r, zz, x) + from_side[r][zz].astype(f32)
            if sign:
                pass_on(r, zz, total, sign)
            else:
                here[...] = total
                add_line(r, zz, here)
            return
        for xx in (1 - x, x):
            at = zz * NX + xx
            core_copy(r, zz, xx).wait_recv()
            total = chip_sum(r, zz, xx)
            if sign:
                pass_on(r, at, total, sign)
                continue
            here[...] = total
            add_line(r, at, here)
            if xx is x:
                side_copy(r, 0).wait_recv()
                here[...] += from_side[r][0].astype(f32)
            else:
                to_side[r][0] = here[...].astype(to_side[r].dtype)
                side_copy(r, 0).start()

    targets(along)
    hand_on()

    def settle(r, zz, sign):
        core_copy(r, zz, 1 - x).wait_send()
        core_copy(r, zz, x).wait_send()
        if not regions[r][3]:
            side_copy(r, zz).wait_send()
            if sign:
                z_copy(r, zz, sign > 0).wait_send()
        elif sign:
            z_copy(r, zz * NX, sign > 0).wait_send()
            z_copy(r, zz * NX + 1, sign > 0).wait_send()
        else:
            side_copy(r, 0).wait_send()

    targets(settle)
    finish()


def ctx_scatter_kernel(values, carry, number, x_first):
    plan, weights, results = carried(carry)
    regions = regions_of(values, x_first)
    count, made, many = len(values), len(results), len(regions)
    dma = pltpu.SemaphoreType.DMA
    scratch = []
    for straight, crossing in ((8, 8), (4, 1), (4, 1), (4, 8), (4, 8), (4, 8)):
        scratch += [
            pltpu.VMEM(
                (crossing if crosses else straight, rows, values[i].shape[2]), values[i].dtype
            )
            for i, _, rows, crosses in regions
        ]
    done = pl.pallas_call(
        functools.partial(scatter_kernel, count, regions, plan, made),
        out_shape=[jax.ShapeDtypeStruct(v.shape[1:], jnp.float32) for v in values] + results,
        in_specs=[VM] * (count + len(weights)),
        out_specs=[VM] * count + places(results, carry),
        scratch_shapes=scratch
        + [dma((many, NZ * NX)) for _ in range(7)]
        + carry_semaphores(len(plan)),
        compiler_params=settings(number, 3 * bytes_of(values) + bytes_of(weights)),
        name=f"scatter_{number}",
    )(*values, *weights)
    return done[:count], done[count:]


def planned():
    return lax.axis_size("ctx") == NZ * NX * NK and lax.axis_size("wa") == 2


def wa_gather(carry):
    joined = [jnp.concatenate(v, axis=1) if kind == "join" else v for kind, v in carry]
    return [
        pair_swap(v) if kind == "swap" else lax.all_gather(v, "wa", axis=0, tiled=True)
        for (kind, _), v in zip(carry, joined)
    ]


def ctx_gather(values, carry, number, x_first):
    if planned():
        return ctx_gather_kernel(values, carry, number, x_first)
    return [lax.all_gather(v, "ctx", axis=0) for v in values], wa_gather(carry)


def ctx_scatter_sum(values, carry, number, x_first):
    if planned():
        return ctx_scatter_kernel(values, carry, number, x_first)
    summed = [lax.psum_scatter(v, "ctx", scatter_dimension=0).astype(jnp.float32) for v in values]
    return summed, wa_gather(carry)


def per_device(
    tokens,
    doc_starts,
    routes,
    valid,
    teacher,
    out_grad,
    norm1_gain,
    w_query,
    w_key,
    w_value,
    w_out,
    norm2_gain,
    w_router,
    shared_gate,
    shared_up,
    shared_down,
    expert_gate,
    expert_up,
    expert_down,
):
    ctx_count = lax.axis_size("ctx")
    ctx_rank = lax.axis_index("ctx")
    wa_count = lax.axis_size("wa")
    side = lax.axis_index("wa")
    local_rows = tokens.shape[1]
    seq_len = local_rows * ctx_count
    groups = H // KVH
    kv_width = KVH * HD
    experts = w_router.shape[1]
    width = tokens.shape[2]
    lanes = 128
    shared_half = shared_down.shape[0]
    run = shared_half // ctx_count
    low = jnp.bfloat16

    gain_rows = width // wa_count // lanes
    valid_rows = valid[0].astype(jnp.float32)
    small = jnp.zeros((16, lanes), jnp.float32)
    small = small.at[:gain_rows].set(norm1_gain.astype(jnp.float32).reshape(gain_rows, lanes))
    small = small.at[8 : 8 + gain_rows].set(
        norm2_gain.astype(jnp.float32).reshape(gain_rows, lanes)
    )
    small = small.at[6].set(valid_rows)
    tokens_there = pair_swap(tokens[0])
    small_there = pair_swap(small)
    small_all = jnp.where(
        side == 0, jnp.stack([small, small_there]), jnp.stack([small_there, small])
    )
    gain_one = small_all[:, :gain_rows].reshape(width)
    gain_two = small_all[:, 8 : 8 + gain_rows].reshape(width)
    valid_here = jnp.sum(small_all[:, 6])

    doc_first = doc_starts[0]
    own_rows = ctx_rank * local_rows + jnp.arange(local_rows, dtype=jnp.int32)
    query_pos = stored_position(own_rows, local_rows, ctx_count)
    query_place = jnp.stack([query_pos, document_of(query_pos, doc_first)])
    key_pos = stored_position(jnp.arange(seq_len, dtype=jnp.int32), local_rows, ctx_count)
    key_place = jnp.stack([key_pos, document_of(key_pos, doc_first)], axis=1)

    residual = tokens[0].astype(jnp.float32)
    residual_there = tokens_there.astype(jnp.float32)
    inverse_one = rms_inverse(residual)
    scaled_half = jnp.concatenate(
        [
            my_half(residual * inverse_one, side, 1),
            my_half(residual_there * rms_inverse(residual_there), side, 1),
        ]
    )
    normed_half = (scaled_half * norm1_gain.astype(jnp.float32)).astype(low)
    key_value_part = jnp.concatenate(
        [matmul(normed_half, w_key), matmul(normed_half, w_value)], axis=1
    )
    key_value_there = pair_swap(key_value_part[local_rows:].astype(low))
    key_value_own = (key_value_part[:local_rows] + key_value_there.astype(jnp.float32)).astype(low)
    query_part = matmul(normed_half, w_query)

    def shared_columns(weight):
        return [
            lax.dynamic_slice_in_dim(weight, half * shared_half + ctx_rank * run, run, 1)
            for half in range(wa_count)
        ]

    units = wa_count * run
    blank = jnp.zeros((shared_gate.shape[0], lanes - units), low)
    down_rows = lax.dynamic_slice_in_dim(shared_down, ctx_rank * run, run, 0)
    (key_value_all, valid_all), (
        query_there,
        weight_out,
        router_t,
    ) = ctx_gather(
        [key_value_own, jnp.full((8, lanes), valid_here)],
        [
            ("swap", query_part[local_rows:].astype(low)),
            ("core", w_out),
            ("core", w_router.astype(jnp.float32).T),
        ],
        2,
        [16, 0],
    )
    wide_in = jnp.concatenate(
        [
            expert_gate[0],
            expert_up[0],
            *shared_columns(shared_gate),
            blank,
            *shared_columns(shared_up),
            blank,
        ],
        axis=1,
    )
    wide_in, down, down_rows, key_value_all = lax.optimization_barrier(
        (wide_in, expert_down[0], down_rows, key_value_all)
    )
    down_rows_there = pair_swap(down_rows)
    weight_sdown = jnp.where(
        side == 0,
        jnp.concatenate([down_rows, down_rows_there]),
        jnp.concatenate([down_rows_there, down_rows]),
    )
    weight_sdown = jnp.pad(weight_sdown, ((0, lanes - units), (0, 0)))
    down_there = pair_swap(down)
    expert_weights = [wide_in, pair_swap(wide_in), down, down_there, weight_sdown]
    which = jnp.full((1,), side, jnp.int32)
    queries = (query_part[:local_rows] + query_there.astype(jnp.float32)).astype(low)
    key_value_all = key_value_all.reshape(seq_len, 2 * kv_width)
    valid_total = jnp.sum(valid_all[:, 0, 0])
    router_t = router_t.reshape(wa_count, experts, width // wa_count)
    weight_router = jnp.transpose(router_t, (0, 2, 1)).reshape(width, experts).astype(low)
    attn, lse = attend_forward(queries, key_value_all, query_place, key_place)
    attn_low = attn.astype(low)
    attn_low, expert_weights[3] = lax.optimization_barrier((attn_low, expert_weights[3]))
    hidden_one = residual + matmul(attn_low, weight_out)
    inverse_two = rms_inverse(hidden_one)
    normed_two = (hidden_one * inverse_two * gain_two).astype(low)

    logits = matmul(normed_two, weight_router)
    choose = routes[0][:, :, None] == jnp.arange(experts, dtype=jnp.int32)[None, None, :]
    chosen = jnp.any(choose, axis=1)
    peak = jnp.max(jnp.where(chosen, logits, MASKED_SCORE), axis=1, keepdims=True)
    weights = jnp.where(chosen, jnp.exp(jnp.where(chosen, logits, peak) - peak), 0.0)
    gates = weights / jnp.sum(weights, axis=1, keepdims=True)

    (normed_all, gates_all), _ = ctx_gather([normed_two, gates.T], [], 3, [16, 0])
    normed_all = normed_all.reshape(seq_len, width)
    gate = lax.dynamic_slice_in_dim(gates_all, ctx_rank, 1, 1).reshape(seq_len, 1)
    acts, mixed = expert_forward(which, normed_all, gate, expert_weights)
    (routed,), _ = ctx_scatter_sum(
        [mixed.reshape(ctx_count, local_rows, width)], [], 4, [16]
    )
    produced = hidden_one + routed
    output = produced.astype(low)[None]

    errors = produced - teacher[0].astype(jnp.float32)
    local_error = jnp.sum(valid_rows[:, None] * errors * errors)
    tokens_all = wa_count * seq_len
    grad_out = (
        out_grad[0].astype(jnp.float32)
        + 2.0 * tokens_all / valid_total * valid_rows[:, None] * errors
    )
    (grad_all,), _ = ctx_gather([grad_out.astype(low)], [], 5, [16])
    grad_all = grad_all.reshape(seq_len, width)

    (
        grad_rows,
        gate_dot,
        gate_grad,
        up_grad,
        gate_grad_other,
        up_grad_other,
        down_grad,
        down_grad_other,
        shared_grad,
        sdown_grad,
    ) = expert_backward(which, normed_all, grad_all, acts, gate, expert_weights)
    shared_grad = jnp.concatenate([shared_grad[:units], shared_grad[lanes : lanes + units]])
    sdown_grad = sdown_grad[:units]
    small = jnp.full((ctx_count, experts + 8, local_rows), local_error)
    small = small.at[:, :experts].set(0.0)
    small = lax.dynamic_update_slice(
        small, gate_dot.reshape(ctx_count, 1, local_rows), (0, ctx_rank, 0)
    )
    (grad_back, small), (attn_there, normed_two_there) = ctx_scatter_sum(
        [grad_rows.reshape(ctx_count, local_rows, width), small],
        [
            ("swap", my_half(attn_low, 1 - side, 1)),
            ("swap", my_half(normed_two, 1 - side, 1)),
        ],
        6,
        [16, 0],
    )
    grad_gates = small[:experts].T
    error_total = small[experts, 0]
    grad_logits = (
        gates * (grad_gates - jnp.sum(gates * grad_gates, axis=1, keepdims=True))
    ).astype(low)
    grad_normed = grad_back + contract_cols(grad_logits, weight_router)

    def for_pair(full):
        return ("swap", my_half(full, 1 - side, 0).astype(low))

    def with_pair(full, other):
        return my_half(full, side, 0) + other.astype(jnp.float32)

    grad_hidden_norm, grad_gain_two = norm_backward(hidden_one, inverse_two, gain_two, grad_normed)
    grad_hidden_one = grad_out + grad_hidden_norm
    grad_attn_in = grad_hidden_one.astype(low)
    grad_heads = contract_cols(grad_attn_in, weight_out).astype(low)
    delta = jnp.einsum(
        "tagd,tagd->agt",
        grad_heads.astype(jnp.float32).reshape(local_rows, KVH, groups, HD),
        attn.reshape(local_rows, KVH, groups, HD),
    ).reshape(KVH, 1, groups * local_rows)
    grad_query, grad_keys, grad_values = attend_grads(
        queries, grad_heads, key_value_all, lse, delta, query_place, key_place
    )
    def for_all(vector):
        flat = jnp.zeros((16 * lanes,), jnp.float32).at[: vector.shape[0]].set(vector)
        return jnp.broadcast_to(flat.reshape(16, lanes), (ctx_count, 16, lanes))

    def from_all(summed, size):
        return summed.reshape(16 * lanes)[:size]

    def by_slot(value):
        return value.reshape(ctx_count, value.shape[0] // ctx_count, value.shape[1])

    half_width = width // wa_count
    (grad_key, grad_value, small), (
        da_there,
        logits_there,
        query_grad_there,
        error_there,
        shared_there,
        sdown_there,
    ) = ctx_scatter_sum(
        [
            grad_keys.reshape(ctx_count, local_rows, kv_width),
            grad_values.reshape(ctx_count, local_rows, kv_width),
            for_all(grad_gain_two),
        ],
        [
            ("swap", grad_attn_in),
            ("swap", grad_logits),
            ("swap", grad_query),
            ("swap", jnp.full((8, lanes), error_total)),
            ("swap", my_half(shared_grad, 1 - side, 1).astype(low)),
            for_pair(sdown_grad),
        ],
        7,
        [16, 16, 0],
    )
    error_total = error_total + error_there[0, 0]
    key_value_low = jnp.concatenate([grad_key, grad_value], axis=1).astype(low)
    gain_two_sum = from_all(small, width)

    def weight_grad(mine, right, theirs, right_there):
        mine = my_half(mine, side, 1)
        return (contract_rows(mine, right) + contract_rows(theirs, right_there)).astype(low)

    out_part = weight_grad(attn_low, grad_attn_in, attn_there, da_there)
    router_part = contract_rows(grad_logits, my_half(normed_two, side, 1)) + contract_rows(
        logits_there, normed_two_there
    )
    shared_part = my_half(shared_grad, side, 1) + shared_there.astype(jnp.float32)
    sdown_part = with_pair(sdown_grad, sdown_there).astype(low)
    rows_two = jnp.zeros((16, lanes), jnp.float32)
    rows_two = rows_two.at[: half_width // lanes].set(
        my_half(gain_two_sum, 1 - side, 0).reshape(-1, lanes)
    )
    router_rows = router_part.reshape(experts, half_width // lanes, lanes)
    router_rows = jnp.pad(router_rows, ((0, 0), (0, 8 - half_width // lanes), (0, 0)))
    (out_sum, router_sum), (kv_grad_there, rows_there, down_there) = ctx_scatter_sum(
        [by_slot(out_part), router_rows],
        [("swap", key_value_low), ("swap", rows_two), ("swap", down_grad_other)],
        8,
        [0, 0],
    )
    total_gain_two = my_half(gain_two_sum, side, 0) + rows_there.reshape(-1)[:half_width]

    query_both = jnp.concatenate([grad_query, query_grad_there])
    kv_both = jnp.concatenate([key_value_low, kv_grad_there])
    normed_grad = (
        contract_cols(query_both, w_query)
        + contract_cols(kv_both[:, :kv_width], w_key)
        + contract_cols(kv_both[:, kv_width:], w_value)
    )
    (query_sum, kv_sum, small), (normed_grad_there, gate_there) = ctx_scatter_sum(
        [
            by_slot(contract_rows(normed_half, query_both).astype(low)),
            by_slot(contract_rows(normed_half, kv_both).astype(low)),
            for_all(jnp.sum(normed_grad * scaled_half, axis=0)),
        ],
        [
            ("swap", normed_grad[local_rows:].astype(low)),
            ("swap", gate_grad_other),
        ],
        9,
        [0, 16, 0],
    )
    total_gain_one = from_all(small, half_width)
    low_half, high_half = normed_grad[:local_rows], normed_grad_there.astype(jnp.float32)
    grad_normed_one = jnp.where(
        side == 0,
        jnp.concatenate([low_half, high_half], axis=1),
        jnp.concatenate([high_half, low_half], axis=1),
    )
    grad_residual_norm, _ = norm_backward(residual, inverse_one, gain_one, grad_normed_one)
    grad_input = grad_hidden_one + grad_residual_norm
    (total_query, total_kv, total_out, router_sum, shared_parts, sdown_parts), (up_there,) = ctx_gather(
        [
            query_sum.astype(low),
            kv_sum.astype(low),
            out_sum.astype(low),
            router_sum,
            shared_part.astype(low),
            sdown_part,
        ],
        [("swap", up_grad_other)],
        10,
        [0, 0, 0, 0, 0, sdown_part.shape[0]],
    )
    total_query = total_query.reshape(half_width, width).astype(jnp.float32)
    total_kv = total_kv.reshape(half_width, 2 * kv_width).astype(jnp.float32)
    total_out = total_out.reshape(half_width, width).astype(jnp.float32)
    router_sum = router_sum[:, : half_width // lanes].reshape(experts, half_width)
    row = jnp.arange(ctx_count * units, dtype=jnp.int32)[:, None]
    half, unit = row % units // run, row % run
    column = half * shared_half + row // units * run + unit
    select = (column == jnp.arange(ctx_count * units, dtype=jnp.int32)[None, :]).astype(low)
    total_sgate, total_sup = [
        contract_rows(
            shared_parts[:, first : first + units].reshape(ctx_count * units, half_width), select
        )
        for first in (0, units)
    ]
    down_grad = down_grad + down_there.astype(jnp.float32)
    return (
        error_total / (valid_total * width),
        output,
        grad_input[None],
        total_gain_one,
        total_query,
        total_kv[:, :kv_width],
        total_kv[:, kv_width:],
        total_out,
        total_gain_two,
        router_sum.T,
        total_sgate,
        total_sup,
        sdown_parts.reshape(shared_half, width).astype(jnp.float32),
        (gate_grad + gate_there.astype(jnp.float32))[None],
        (up_grad + up_there.astype(jnp.float32))[None],
        down_grad[None],
    )


def solution(mesh):
    return jax.shard_map(
        per_device,
        mesh=mesh,
        in_specs=(
            P("wa", "ctx", None),
            P("wa", None),
            P("wa", "ctx", None),
            P("wa", "ctx"),
            P("wa", "ctx", None),
            P("wa", "ctx", None),
            P("wa"),
            P("wa", None),
            P("wa", None),
            P("wa", None),
            P("wa", None),
            P("wa"),
            P("wa", None),
            P("wa", None),
            P("wa", None),
            P("wa", None),
            P("ctx", "wa", None),
            P("ctx", "wa", None),
            P("ctx", "wa", None),
        ),
        out_specs=(
            P(),
            P("wa", "ctx", None),
            P("wa", "ctx", None),
            P("wa"),
            P("wa", None),
            P("wa", None),
            P("wa", None),
            P("wa", None),
            P("wa"),
            P("wa", None),
            P("wa", None),
            P("wa", None),
            P("wa", None),
            P("ctx", "wa", None),
            P("ctx", "wa", None),
            P("ctx", "wa", None),
        ),
        check_vma=False,
    )
```
